128 devices in a mesh: seq: 16 (over z_lo, x, core), head: 8 (over y, z_hi).
Axes of the slice: x: 4, y: 4, z: 4 (z_hi: 2, z_lo: 2; z = z_hi * 2 + z_lo), core: 2. Of those that a mesh axis runs over, the one named last changes fastest.
Arguments:
- queries: bfloat16 [10240, 5120], P('seq', 'head'), may hold values from -5 to 5
- key_states: bfloat16 [10240, 5120], P('seq', 'head'), may hold values from -5 to 5
- value_states: bfloat16 [10240, 5120], P('seq', 'head'), may hold values from -6 to 6
- tile_mask: int32 [80, 80], replicated, may hold values from 0 to 1, as said below
- out_weight: bfloat16 [5120, 5120], P('head'), may hold values from -0.078125 to 0.078125
- out_bias: float32 [5120], P('head'), may hold values from -1.5 to 1.5
- residual: bfloat16 [10240, 5120], P('seq', 'head'), may hold values from -3 to 3
- gate_scale: float32 [5120], P('head'), may hold values from 0.5 to 2
Outputs:
- block_out: bfloat16 [10240, 5120], P('seq', 'head')
The draws below stay inside these ranges and needn't reach their ends.
Inputs may be any that keep to these rules, and one draw needn't show every extreme that they name: tile_mask[i, j] is 1 wherever |i - j| <= 3; farther pairs are 1 less often the farther apart they are.
All inputs are finite; a program needn't handle non-finite values.
Results may differ from the reference program's by a relative error of at most 0.009.
Values may be sent and summed in bfloat16 or wider, within the bound.
A program may use at most 128 MiB of HBM per device.

```python
import math
import jax
import jax.numpy as jnp
from jax import lax

D = 5120
HEADS = 40
HEAD_DIM = 128
TILE = 128
TILE_COUNT = 80
TOKENS = 10240


def draw_queries(key, part):
    key = jax.random.fold_in(key, 11)
    drawn = jnp.clip(jax.random.normal(key, (TOKENS, HEADS * HEAD_DIM), jnp.float32), -5.0, 5.0)
    return drawn.astype(jnp.bfloat16)


def draw_key_states(key, part):
    key = jax.random.fold_in(key, 23)
    drawn = jnp.clip(jax.random.normal(key, (TOKENS, HEADS * HEAD_DIM), jnp.float32), -5.0, 5.0)
    return drawn.astype(jnp.bfloat16)


def draw_tile_mask(key, part):
    key = jax.random.fold_in(key, 5)
    positions = jnp.arange(TILE_COUNT, dtype=jnp.int32)
    spacing = jnp.abs(positions[:, None] - positions[None, :])
    lottery = jax.random.randint(key, (TILE_COUNT, TILE_COUNT), 0, 1 << 20)
    return (lottery % (spacing + 1) < 4).astype(jnp.int32)


def level_of(key, extent, shards, least, top_value):
    loudness = 1.0
    for axis_at, blocks in shards:
        steps = jax.random.uniform(jax.random.fold_in(jax.random.fold_in(key, 6), axis_at), (blocks,), jnp.float32, least / len(shards), top_value / len(shards))
        loudness = loudness * jnp.repeat(jnp.exp(steps), extent[axis_at] // blocks).reshape((-1,) + (1,) * (len(extent) - 1 - axis_at))
    return loudness


def normal_values(key, shape, width, bound, shards=(), kind=jnp.bfloat16):
    values = width * jax.random.normal(key, shape, jnp.float32)
    if shards:
        values = values * level_of(key, shape, shards, -0.22, 0.18)
    return jnp.clip(values, -bound, bound).astype(kind)


def setup_inputs(seed: int = 0) -> dict:
    key_list = jax.random.split(jax.random.key(seed), 9)
    return {
        "queries": draw_queries(jax.random.fold_in(key_list[8], 71), 0),
        "key_states": draw_key_states(jax.random.fold_in(key_list[8], 71), 0),
        "value_states": normal_values(key_list[2], (TOKENS, HEADS * HEAD_DIM), 1.0, 6.0, ((0, 16), (1, 8))),
        "tile_mask": draw_tile_mask(jax.random.fold_in(key_list[8], 71), 0),
        "out_weight": normal_values(key_list[4], (HEADS * HEAD_DIM, D), (HEADS * HEAD_DIM) ** -0.5, 0.078125, ((0, 8),)),
        "out_bias": normal_values(key_list[5], (D,), 0.3, 1.5, ((0, 8),), jnp.float32),
        "residual": normal_values(key_list[6], (TOKENS, D), 0.5, 3.0, ((0, 16), (1, 8))),
        "gate_scale": jnp.clip(jnp.exp(math.log(2.0) - 1.3862944 * jax.random.uniform(key_list[7], (D,), jnp.float32) ** level_of(key_list[7], (D,), ((0, 8),), -0.2, 0.2)), 0.5, 2.0),
    }


def reference(queries, key_states, value_states, tile_mask, out_weight, out_bias, residual, gate_scale):
    token_total = queries.shape[0]
    scaling = HEAD_DIM ** -0.5
    allowed = jnp.repeat(jnp.repeat(tile_mask > 0, TILE, axis=0), TILE, axis=1)

    def split_heads(tensor):
        return tensor.reshape(token_total, HEADS, HEAD_DIM).transpose(1, 0, 2)

    def one_head(triple):
        query_head, key_head, value_head = triple
        scores = jnp.dot(query_head, key_head.T, preferred_element_type=jnp.float32) * scaling
        row_max = jnp.max(jnp.where(allowed, scores, -jnp.inf), axis=1)
        weights = jnp.where(allowed, jnp.exp(scores - row_max[:, None]), 0.0)
        totals = jnp.sum(weights, axis=1)
        blended = jnp.dot(weights.astype(jnp.bfloat16), value_head, preferred_element_type=jnp.float32)
        return (blended / totals[:, None]).astype(jnp.bfloat16)

    attended = lax.map(one_head, (split_heads(queries), split_heads(key_states), split_heads(value_states)))
    attended = attended.transpose(1, 0, 2).reshape(token_total, HEADS * HEAD_DIM)
    projected = jnp.dot(attended, out_weight, preferred_element_type=jnp.float32)
    result = residual.astype(jnp.float32) + gate_scale.astype(jnp.float32)[None, :] * (projected + out_bias.astype(jnp.float32)[None, :])
    return result.astype(jnp.bfloat16)
```

```python
import jax
import jax.numpy as jnp
from jax import lax
from jax.experimental import pallas as pl
from jax.experimental.pallas import tpu as pltpu
from jax.sharding import PartitionSpec as P

HEAD_DIM = 128
TILE = 128
ROWS = 640
ROW_TILES = ROWS // TILE
SEQ = 16
RING = 4
TILE_COUNT = 80
MESH = pl.DeviceIdType.MESH
MASKED = -1e30


def place():
    s = lax.axis_index("seq")
    h = lax.axis_index("head")
    return lax.div(s, 8), lax.rem(lax.div(s, 2), 4), lax.rem(s, 2), lax.div(h, 2), lax.rem(h, 2)


def gather_kernel(
    q_ref, k_ref, v_ref, w_ref, kv_out, q_out, w_out,
    stage, stage_sem, local_sem, send_sem, z_sem, x_sem, far_sem, sib_sem, w_sem, w_sib_sem,
):
    zl, x, core, y, zh = place()
    other = 1 - zl
    right, left = lax.rem(x + 1, RING), lax.rem(x + 3, RING)
    opposite = lax.rem(x + 2, RING)

    def seq_of(zl_, x_, core_):
        return (zl_ * RING + x_) * 2 + core_

    head_me = y * 2 + zh
    me = seq_of(zl, x, core)
    to_pair = (seq_of(other, x, core), head_me)
    to_right = (seq_of(zl, right, core), head_me)
    to_left = (seq_of(zl, left, core), head_me)
    to_sib = (seq_of(zl, x, 1 - core), head_me)
    to_y = [(me, lax.rem(y + d, RING) * 2 + zh) for d in (1, 2, 3)]

    barrier = pltpu.get_barrier_semaphore()
    neighbours = [to_pair, to_right, to_left, to_sib] + to_y
    for n in neighbours:
        pl.semaphore_signal(barrier, inc=1, device_id=n, device_id_type=MESH)

    def head_columns(h):
        return pl.ds(pl.multiple_of(h * HEAD_DIM, HEAD_DIM), HEAD_DIM)

    staged = []
    for plane, base in ((zl, 0), (other, 6)):
        for j in range(2):
            staged.append((k_ref, plane * 2 + j, base + 2 * j))
            staged.append((v_ref, plane * 2 + j, base + 2 * j + 1))
    staged += [(k_ref, 4, 4), (v_ref, 4, 5), (q_ref, other * 2, 10), (q_ref, other * 2 + 1, 11)]
    stage_copies = [
        pltpu.make_async_copy(src.at[:, head_columns(h)], stage.at[at], stage_sem.at[at]) for src, h, at in staged
    ]
    for c in stage_copies:
        c.start()
    half = pl.ds(pl.multiple_of(core * (ROWS // 2), ROWS // 2), ROWS // 2)
    other_half = pl.ds(pl.multiple_of((1 - core) * (ROWS // 2), ROWS // 2), ROWS // 2)

    def panel(y_):
        return pl.ds(pl.multiple_of(y_ * (2 * ROWS), 2 * ROWS), 2 * ROWS)

    local = [
        pltpu.make_async_copy(q_ref.at[:, head_columns(zl * 2)], q_out.at[0], local_sem.at[0]),
        pltpu.make_async_copy(q_ref.at[:, head_columns(zl * 2 + 1)], q_out.at[1], local_sem.at[1]),
        pltpu.make_async_copy(q_ref.at[:, head_columns(4)], q_out.at[2], local_sem.at[2]),
        pltpu.make_async_copy(w_ref.at[half, panel(y)], w_out.at[y, half], local_sem.at[3]),
    ]
    for c in local:
        c.start()
    for c in stage_copies:
        c.wait()
    own = pltpu.make_async_copy(stage.at[pl.ds(0, 6)], kv_out.at[me], local_sem.at[4])
    own.start()
    pl.semaphore_wait(barrier, len(neighbours))

    sends = []

    def send(src, dst, recv, target):
        c = pltpu.make_async_remote_copy(
            src_ref=src, dst_ref=dst, send_sem=send_sem.at[len(sends)], recv_sem=recv, device_id=target, device_id_type=MESH
        )
        c.start()
        sends.append(c)

    def arrived(dst, recv, source):
        pltpu.make_async_remote_copy(
            src_ref=dst, dst_ref=dst, send_sem=send_sem.at[0], recv_sem=recv, device_id=source, device_id_type=MESH
        ).wait_recv()

    A, B, H = pl.ds(0, 2), pl.ds(2, 2), pl.ds(4, 2)
    H0, H1 = pl.ds(4, 1), pl.ds(5, 1)
    sib_waits = []

    def to_sibling(origin_zl, origin_x, part):
        n = len(sib_waits)
        block = kv_out.at[seq_of(origin_zl, origin_x, core), part]
        send(block, block, sib_sem.at[n], to_sib)
        sib_waits.append((origin_zl, origin_x, part))

    def pass_on(origin_zl, origin_x, part, recv, target):
        block = kv_out.at[seq_of(origin_zl, origin_x, core), part]
        send(block, block, recv, target)

    def block_of(origin_zl, origin_x, part):
        return kv_out.at[seq_of(origin_zl, origin_x, core), part]

    send(stage.at[pl.ds(6, 2)], kv_out.at[me, A], z_sem.at[0], to_pair)
    send(stage.at[pl.ds(8, 2)], kv_out.at[me, B], z_sem.at[1], to_pair)
    for item, part, at in ((0, H, 4), (1, A, 0), (2, B, 2)):
        send(stage.at[pl.ds(at, 2)], kv_out.at[me, part], x_sem.at[0, item], to_right)
        send(stage.at[pl.ds(at, 2)], kv_out.at[me, part], x_sem.at[1, item], to_left)
    for d in range(3):
        send(w_ref.at[half, panel(lax.rem(y + d + 1, RING))], w_out.at[y, half], w_sem.at[d], to_y[d])
    own.wait()
    to_sibling(zl, x, pl.ds(0, 6))

    for item, part, n in ((3, A, 0), (4, B, 1)):
        arrived(block_of(other, x, part), z_sem.at[n], to_pair)
        pass_on(other, x, part, x_sem.at[0, item], to_right)
        pass_on(other, x, part, x_sem.at[1, item], to_left)
        if n == 0:
            send(stage.at[pl.ds(4, 2)], kv_out.at[me, H], z_sem.at[2], to_pair)
        else:
            send(stage.at[pl.ds(10, 2)], q_out.at[pl.ds(3, 2)], z_sem.at[3], to_pair)
        to_sibling(other, x, part)

    def from_left(item, zl_, part):
        arrived(block_of(zl_, left, part), x_sem.at[0, item], to_left)

    def from_right(item, zl_, part):
        arrived(block_of(zl_, right, part), x_sem.at[1, item], to_right)

    from_left(0, zl, H)
    pass_on(zl, left, H0, far_sem.at[0, 0], to_right)
    pass_on(zl, left, H, z_sem.at[4], to_pair)
    to_sibling(zl, left, H)
    from_right(0, zl, H)
    pass_on(zl, right, H1, far_sem.at[1, 0], to_left)
    pass_on(zl, right, H, z_sem.at[5], to_pair)
    to_sibling(zl, right, H)

    for item, zl_, far in ((1, zl, 1), (3, other, 2)):
        from_left(item, zl_, A)
        pass_on(zl_, left, A, far_sem.at[0, far], to_right)
        to_sibling(zl_, left, A)
        from_right(item, zl_, A)
        to_sibling(zl_, right, A)
        from_right(item + 1, zl_, B)
        pass_on(zl_, right, B, far_sem.at[1, far], to_left)
        to_sibling(zl_, right, B)
        from_left(item + 1, zl_, B)
        to_sibling(zl_, left, B)
        if far == 1:
            arrived(block_of(zl, opposite, H0), far_sem.at[0, 0], to_left)
            arrived(block_of(zl, opposite, H1), far_sem.at[1, 0], to_right)
            pass_on(zl, opposite, H, z_sem.at[6], to_pair)
            to_sibling(zl, opposite, H)
            arrived(block_of(other, x, H), z_sem.at[2], to_pair)
            to_sibling(other, x, H)
    for d in range(3):
        y_ = lax.rem(y + 3 - d, RING)
        arrived(w_out.at[y_, half], w_sem.at[d], to_y[2 - d])
    for d in range(4):
        y_ = lax.rem(y + d, RING)
        if d == 0:
            local[3].wait()
        send(w_out.at[y_, half], w_out.at[y_, half], w_sib_sem.at[d], to_sib)
    for zl_, far in ((zl, 1), (other, 2)):
        arrived(block_of(zl_, opposite, A), far_sem.at[0, far], to_left)
        to_sibling(zl_, opposite, A)
        arrived(block_of(zl_, opposite, B), far_sem.at[1, far], to_right)
        to_sibling(zl_, opposite, B)
    for n, x_ in ((4, left), (5, right), (6, opposite)):
        arrived(block_of(other, x_, H), z_sem.at[n], to_pair)
        to_sibling(other, x_, H)
    arrived(q_out.at[pl.ds(3, 2)], z_sem.at[3], to_pair)
    for d in range(4):
        y_ = lax.rem(y + d, RING)
        arrived(w_out.at[y_, other_half], w_sib_sem.at[d], to_sib)
    for n, (zl_, x_, part) in enumerate(sib_waits):
        arrived(kv_out.at[seq_of(zl_, x_, 1 - core), part], sib_sem.at[n], to_sib)
    for c in sends:
        c.wait_send()
    for c in local[:3]:
        c.wait()


def gather(q, k, v, w):
    bf16 = jnp.bfloat16
    return pl.pallas_call(
        gather_kernel,
        out_shape=[
            jax.ShapeDtypeStruct((SEQ, 6, ROWS, HEAD_DIM), bf16),
            jax.ShapeDtypeStruct((5, ROWS, HEAD_DIM), bf16),
            jax.ShapeDtypeStruct((RING, ROWS, 2 * ROWS), bf16),
        ],
        in_specs=[pl.BlockSpec(memory_space=pl.ANY)] * 4,
        out_specs=[pl.BlockSpec(memory_space=pl.ANY)] * 3,
        scratch_shapes=[
            pltpu.VMEM((12, ROWS, HEAD_DIM), bf16),
            pltpu.SemaphoreType.DMA((12,)),
            pltpu.SemaphoreType.DMA((5,)),
            pltpu.SemaphoreType.DMA((64,)),
            pltpu.SemaphoreType.DMA((7,)),
            pltpu.SemaphoreType.DMA((2, 5)),
            pltpu.SemaphoreType.DMA((2, 3)),
            pltpu.SemaphoreType.DMA((24,)),
            pltpu.SemaphoreType.DMA((3,)),
            pltpu.SemaphoreType.DMA((4,)),
        ],
        compiler_params=pltpu.CompilerParams(collective_id=0, has_side_effects=True),
        name="gather_heads",
    )(q, k, v, w)


GROUP = 4


def attend_kernel(tiles_ref, counts_ref, q_ref, k_ref, v_ref, o_ref, scores):
    j = pl.program_id(0)
    scaling = HEAD_DIM ** -0.5

    def one_row(i, _):
        mine = i < ROW_TILES
        slot = jnp.where(mine, j, 3 + j)
        rows = pl.ds(pl.multiple_of(jnp.where(mine, i, i - ROW_TILES) * TILE, TILE), TILE)
        q = q_ref[slot, rows, :]
        count = counts_ref[i]
        groups = lax.div(count + (GROUP - 1), GROUP)

        def tile_of(ref, n):
            t = tiles_ref[i, n]
            owner = lax.div(t, ROW_TILES)
            return ref[owner, 0, pl.ds(pl.multiple_of((t - owner * ROW_TILES) * TILE, TILE), TILE), :]

        def score(g, peak):
            keys = jnp.concatenate([tile_of(k_ref, g * GROUP + t) for t in range(GROUP)], axis=0)
            s = lax.dot_general(q, keys, (((1,), (1,)), ((), ())), preferred_element_type=jnp.float32)
            for t in range(GROUP):
                part = jnp.where(g * GROUP + t < count, s[:, t * TILE : (t + 1) * TILE], MASKED)
                scores[g * GROUP + t] = part
                peak = jnp.maximum(peak, part)
            return peak

        peak = lax.fori_loop(0, groups, score, jnp.full((TILE, TILE), MASKED, jnp.float32))
        row_max = jnp.max(peak, axis=1, keepdims=True)

        def blend(g, carry):
            total, acc = carry
            values = jnp.concatenate([tile_of(v_ref, g * GROUP + t) for t in range(GROUP)], axis=0)
            weights = [jnp.exp((scores[g * GROUP + t] - row_max) * scaling) for t in range(GROUP)]
            for part in weights:
                total = total + part
            w = jnp.concatenate(weights, axis=1).astype(jnp.bfloat16)
            return total, acc + jnp.dot(w, values, preferred_element_type=jnp.float32)

        zero = jnp.zeros((TILE, HEAD_DIM), jnp.float32)
        total, acc = lax.fori_loop(0, groups, blend, (zero, zero))
        o_ref[slot, rows, :] = (acc / jnp.sum(total, axis=1, keepdims=True)).astype(o_ref.dtype)
        return 0

    lax.fori_loop(0, jnp.where(j < 2, 2 * ROW_TILES, ROW_TILES), one_row, 0)


def attend(tiles, counts, q, kv):
    return pl.pallas_call(
        attend_kernel,
        out_shape=jax.ShapeDtypeStruct((5, ROWS, HEAD_DIM), jnp.bfloat16),
        grid_spec=pltpu.PrefetchScalarGridSpec(
            num_scalar_prefetch=2,
            grid=(3,),
            in_specs=[
                pl.BlockSpec((5, ROWS, HEAD_DIM), lambda j, *_: (0, 0, 0)),
                pl.BlockSpec((SEQ, 1, ROWS, HEAD_DIM), lambda j, *_: (0, 2 * j, 0, 0)),
                pl.BlockSpec((SEQ, 1, ROWS, HEAD_DIM), lambda j, *_: (0, 2 * j + 1, 0, 0)),
            ],
            out_specs=pl.BlockSpec((5, ROWS, HEAD_DIM), lambda j, *_: (0, 0, 0)),
            scratch_shapes=[pltpu.VMEM((TILE_COUNT, TILE, TILE), jnp.float32)],
        ),
        compiler_params=pltpu.CompilerParams(vmem_limit_bytes=48 << 20),
        name="attend",
    )(tiles, counts, q, kv, kv)


def tile_lists(tile_mask):
    zl, x, core, _, _ = place()
    own = (zl * RING + x) * 2 + core
    pair = ((1 - zl) * RING + x) * 2 + core
    rows = jnp.concatenate(
        [lax.dynamic_slice_in_dim(tile_mask, first * ROW_TILES, ROW_TILES, 0) for first in (own, pair)], axis=0
    )
    allowed = rows > 0
    at = jnp.arange(TILE_COUNT, dtype=jnp.int32)
    before = jnp.sum(jnp.where(allowed[:, None, :] & (at[None, None, :] < at[None, :, None]), 1, 0), axis=2)
    hit = allowed[:, None, :] & (before[:, None, :] == at[None, :, None])
    tiles = jnp.sum(jnp.where(hit, at[None, None, :], 0), axis=2)
    return tiles.astype(jnp.int32), jnp.sum(allowed, axis=1).astype(jnp.int32)


def local(queries, key_states, value_states, tile_mask, out_weight, out_bias, residual, gate_scale):
    zl, x, core, y, zh = place()
    tiles, counts = tile_lists(tile_mask)
    kv, q, panel = gather(queries, key_states, value_states, out_weight)
    o = attend(tiles, counts, q, kv)
    pairs = [(s, (s + 8) % 16) for s in range(SEQ)]
    back = lax.ppermute(o[3:5], "seq", pairs)
    low = jnp.where(zl == 0, o[0:2], back)
    high = jnp.where(zl == 0, back, o[0:2])
    attended = jnp.concatenate([low, high, o[2:3]], axis=0).transpose(1, 0, 2).reshape(ROWS, ROWS)
    gathered = lax.all_gather(
        attended, "head", axis=1, tiled=True, axis_index_groups=[[0, 2, 4, 6], [1, 3, 5, 7]]
    )
    partial = jnp.dot(gathered, panel.reshape(RING * ROWS, 2 * ROWS), preferred_element_type=jnp.float32)
    mine = lax.dynamic_slice_in_dim(partial, zh * ROWS, ROWS, 1)
    theirs = lax.dynamic_slice_in_dim(partial, (1 - zh) * ROWS, ROWS, 1).astype(jnp.bfloat16)
    projected = mine + lax.ppermute(theirs, "head", [(h, h ^ 1) for h in range(8)]).astype(jnp.float32)
    result = residual.astype(jnp.float32) + gate_scale[None, :] * (projected + out_bias[None, :])
    return result.astype(jnp.bfloat16)


def solution(mesh):
    return jax.shard_map(
        local,
        mesh=mesh,
        in_specs=(
            P("seq", "head"),
            P("seq", "head"),
            P("seq", "head"),
            P(),
            P("head", None),
            P("head"),
            P("seq", "head"),
            P("head"),
        ),
        out_specs=P("seq", "head"),
        check_vma=False,
    )
```

```python
import jax
import jax.numpy as jnp
from jax import lax
from jax.experimental import pallas as pl
from jax.experimental.pallas import tpu as pltpu
from jax.sharding import PartitionSpec as P

HEAD_DIM = 128
TILE = 128
ROWS = 640
ROW_TILES = ROWS // TILE
SEQ = 16
RING = 4
TILE_COUNT = 80
MESH = pl.DeviceIdType.MESH
MASKED = -1e30


def place():
    s = lax.axis_index("seq")
    h = lax.axis_index("head")
    return lax.div(s, 8), lax.rem(lax.div(s, 2), 4), lax.rem(s, 2), lax.div(h, 2), lax.rem(h, 2)


def gather_kernel(
    q_ref, k_ref, v_ref, w_ref, kv_out, q_out, w_out,
    stage, raw_values, stage_sem, local_sem, send_sem, z_sem, x_sem, far_sem, sib_sem, w_sem, w_sib_sem,
):
    zl, x, core, y, zh = place()
    other = 1 - zl
    right, left = lax.rem(x + 1, RING), lax.rem(x + 3, RING)
    opposite = lax.rem(x + 2, RING)

    def seq_of(zl_, x_, core_):
        return (zl_ * RING + x_) * 2 + core_

    head_me = y * 2 + zh
    me = seq_of(zl, x, core)
    to_pair = (seq_of(other, x, core), head_me)
    to_right = (seq_of(zl, right, core), head_me)
    to_left = (seq_of(zl, left, core), head_me)
    to_sib = (seq_of(zl, x, 1 - core), head_me)
    to_y = [(me, lax.rem(y + d, RING) * 2 + zh) for d in (1, 2, 3)]

    barrier = pltpu.get_barrier_semaphore()
    neighbours = [to_pair, to_right, to_left, to_sib] + to_y
    for n in neighbours:
        pl.semaphore_signal(barrier, inc=1, device_id=n, device_id_type=MESH)

    def head_columns(h):
        return pl.ds(pl.multiple_of(h * HEAD_DIM, HEAD_DIM), HEAD_DIM)

    own_a, pair_a = zl * 2, other * 2
    staged = [
        (k_ref, own_a, stage.at[0]),
        (k_ref, own_a + 1, stage.at[2]),
        (k_ref, 4, stage.at[4]),
        (k_ref, pair_a, stage.at[6]),
        (k_ref, pair_a + 1, stage.at[8]),
        (q_ref, pair_a, stage.at[10]),
        (q_ref, pair_a + 1, stage.at[11]),
        (v_ref, own_a, raw_values.at[0]),
        (v_ref, own_a + 1, raw_values.at[1]),
        (v_ref, 4, raw_values.at[2]),
        (v_ref, pair_a, raw_values.at[3]),
        (v_ref, pair_a + 1, raw_values.at[4]),
    ]
    stage_copies = [
        pltpu.make_async_copy(src.at[:, head_columns(h)], dst, stage_sem.at[n])
        for n, (src, h, dst) in enumerate(staged)
    ]
    for c in stage_copies:
        c.start()
    half = pl.ds(pl.multiple_of(core * (ROWS // 2), ROWS // 2), ROWS // 2)
    other_half = pl.ds(pl.multiple_of((1 - core) * (ROWS // 2), ROWS // 2), ROWS // 2)

    def panel(y_):
        return pl.ds(pl.multiple_of(y_ * (2 * ROWS), 2 * ROWS), 2 * ROWS)

    local = [
        pltpu.make_async_copy(q_ref.at[:, head_columns(zl * 2)], q_out.at[0], local_sem.at[0]),
        pltpu.make_async_copy(q_ref.at[:, head_columns(zl * 2 + 1)], q_out.at[1], local_sem.at[1]),
        pltpu.make_async_copy(q_ref.at[:, head_columns(4)], q_out.at[2], local_sem.at[2]),
        pltpu.make_async_copy(w_ref.at[half, panel(y)], w_out.at[y, half], local_sem.at[3]),
    ]
    for c in local:
        c.start()
    for c in stage_copies:
        c.wait()

    def turn(n, _):
        piece = lax.div(n, ROW_TILES)
        rows = pl.ds(pl.multiple_of((n - piece * ROW_TILES) * TILE, TILE), TILE)
        stage[2 * piece + 1, rows, :] = raw_values[piece, rows, :].T
        return 0

    lax.fori_loop(0, 5 * ROW_TILES, turn, 0)
    own = pltpu.make_async_copy(stage.at[pl.ds(0, 6)], kv_out.at[me], local_sem.at[4])
    own.start()
    pl.semaphore_wait(barrier, len(neighbours))

    sends = []

    def send(src, dst, recv, target):
        c = pltpu.make_async_remote_copy(
            src_ref=src, dst_ref=dst, send_sem=send_sem.at[len(sends)], recv_sem=recv, device_id=target, device_id_type=MESH
        )
        c.start()
        sends.append(c)

    def arrived(dst, recv, source):
        pltpu.make_async_remote_copy(
            src_ref=dst, dst_ref=dst, send_sem=send_sem.at[0], recv_sem=recv, device_id=source, device_id_type=MESH
        ).wait_recv()

    A, B, H = pl.ds(0, 2), pl.ds(2, 2), pl.ds(4, 2)
    H0, H1 = pl.ds(4, 1), pl.ds(5, 1)
    sib_waits = []

    def to_sibling(origin_zl, origin_x, part):
        n = len(sib_waits)
        block = kv_out.at[seq_of(origin_zl, origin_x, core), part]
        send(block, block, sib_sem.at[n], to_sib)
        sib_waits.append((origin_zl, origin_x, part))

    def pass_on(origin_zl, origin_x, part, recv, target):
        block = kv_out.at[seq_of(origin_zl, origin_x, core), part]
        send(block, block, recv, target)

    def block_of(origin_zl, origin_x, part):
        return kv_out.at[seq_of(origin_zl, origin_x, core), part]

    send(stage.at[pl.ds(6, 2)], kv_out.at[me, A], z_sem.at[0], to_pair)
    send(stage.at[pl.ds(8, 2)], kv_out.at[me, B], z_sem.at[1], to_pair)
    for item, part, at in ((0, H, 4), (1, A, 0), (2, B, 2)):
        send(stage.at[pl.ds(at, 2)], kv_out.at[me, part], x_sem.at[0, item], to_right)
        send(stage.at[pl.ds(at, 2)], kv_out.at[me, part], x_sem.at[1, item], to_left)
    for d in range(3):
        send(w_ref.at[half, panel(lax.rem(y + d + 1, RING))], w_out.at[y, half], w_sem.at[d], to_y[d])
    own.wait()
    to_sibling(zl, x, pl.ds(0, 6))

    for item, part, n in ((3, A, 0), (4, B, 1)):
        arrived(block_of(other, x, part), z_sem.at[n], to_pair)
        pass_on(other, x, part, x_sem.at[0, item], to_right)
        pass_on(other, x, part, x_sem.at[1, item], to_left)
        if n == 0:
            send(stage.at[pl.ds(4, 2)], kv_out.at[me, H], z_sem.at[2], to_pair)
        else:
            send(stage.at[pl.ds(10, 2)], q_out.at[pl.ds(3, 2)], z_sem.at[3], to_pair)
        to_sibling(other, x, part)

    def from_left(item, zl_, part):
        arrived(block_of(zl_, left, part), x_sem.at[0, item], to_left)

    def from_right(item, zl_, part):
        arrived(block_of(zl_, right, part), x_sem.at[1, item], to_right)

    from_left(0, zl, H)
    pass_on(zl, left, H0, far_sem.at[0, 0], to_right)
    pass_on(zl, left, H, z_sem.at[4], to_pair)
    to_sibling(zl, left, H)
    from_right(0, zl, H)
    pass_on(zl, right, H1, far_sem.at[1, 0], to_left)
    pass_on(zl, right, H, z_sem.at[5], to_pair)
    to_sibling(zl, right, H)

    for item, zl_, far in ((1, zl, 1), (3, other, 2)):
        from_left(item, zl_, A)
        pass_on(zl_, left, A, far_sem.at[0, far], to_right)
        to_sibling(zl_, left, A)
        from_right(item, zl_, A)
        to_sibling(zl_, right, A)
        from_right(item + 1, zl_, B)
        pass_on(zl_, right, B, far_sem.at[1, far], to_left)
        to_sibling(zl_, right, B)
        from_left(item + 1, zl_, B)
        to_sibling(zl_, left, B)
        if far == 1:
            arrived(block_of(zl, opposite, H0), far_sem.at[0, 0], to_left)
            arrived(block_of(zl, opposite, H1), far_sem.at[1, 0], to_right)
            pass_on(zl, opposite, H, z_sem.at[6], to_pair)
            to_sibling(zl, opposite, H)
            arrived(block_of(other, x, H), z_sem.at[2], to_pair)
            to_sibling(other, x, H)
    for d in range(3):
        y_ = lax.rem(y + 3 - d, RING)
        arrived(w_out.at[y_, half], w_sem.at[d], to_y[2 - d])
    for d in range(4):
        y_ = lax.rem(y + d, RING)
        if d == 0:
            local[3].wait()
        send(w_out.at[y_, half], w_out.at[y_, half], w_sib_sem.at[d], to_sib)
    for zl_, far in ((zl, 1), (other, 2)):
        arrived(block_of(zl_, opposite, A), far_sem.at[0, far], to_left)
        to_sibling(zl_, opposite, A)
        arrived(block_of(zl_, opposite, B), far_sem.at[1, far], to_right)
        to_sibling(zl_, opposite, B)
    for n, x_ in ((4, left), (5, right), (6, opposite)):
        arrived(block_of(other, x_, H), z_sem.at[n], to_pair)
        to_sibling(other, x_, H)
    arrived(q_out.at[pl.ds(3, 2)], z_sem.at[3], to_pair)
    for d in range(4):
        y_ = lax.rem(y + d, RING)
        arrived(w_out.at[y_, other_half], w_sib_sem.at[d], to_sib)
    for n, (zl_, x_, part) in enumerate(sib_waits):
        arrived(kv_out.at[seq_of(zl_, x_, 1 - core), part], sib_sem.at[n], to_sib)
    for c in sends:
        c.wait_send()
    for c in local[:3]:
        c.wait()


def gather(q, k, v, w):
    bf16 = jnp.bfloat16
    return pl.pallas_call(
        gather_kernel,
        out_shape=[
            jax.ShapeDtypeStruct((SEQ, 6, ROWS, HEAD_DIM), bf16),
            jax.ShapeDtypeStruct((5, ROWS, HEAD_DIM), bf16),
            jax.ShapeDtypeStruct((RING, ROWS, 2 * ROWS), bf16),
        ],
        in_specs=[pl.BlockSpec(memory_space=pl.ANY)] * 4,
        out_specs=[pl.BlockSpec(memory_space=pl.ANY)] * 3,
        scratch_shapes=[
            pltpu.VMEM((12, ROWS, HEAD_DIM), bf16),
            pltpu.VMEM((5, ROWS, HEAD_DIM), bf16),
            pltpu.SemaphoreType.DMA((12,)),
            pltpu.SemaphoreType.DMA((5,)),
            pltpu.SemaphoreType.DMA((64,)),
            pltpu.SemaphoreType.DMA((7,)),
            pltpu.SemaphoreType.DMA((2, 5)),
            pltpu.SemaphoreType.DMA((2, 3)),
            pltpu.SemaphoreType.DMA((24,)),
            pltpu.SemaphoreType.DMA((3,)),
            pltpu.SemaphoreType.DMA((4,)),
        ],
        compiler_params=pltpu.CompilerParams(collective_id=0, has_side_effects=True),
        name="gather_heads",
    )(q, k, v, w)


GROUP = 10
LOG2E = 1.4426950408889634


def attend_kernel(tiles_ref, counts_ref, q_ref, kv_hbm, o_ref, kv_ref, s00, s01, s02, s10, s11, s12, acc0, acc1, acc2, sem):
    scores = ((s00, s01, s02), (s10, s11, s12))
    accs = (acc0, acc1, acc2)
    factor = HEAD_DIM ** -0.5 * LOG2E
    loads = [pltpu.make_async_copy(kv_hbm.at[:, p], kv_ref.at[:, p], sem.at[p]) for p in (0, 2, 4, 1, 3, 5)]
    for c in loads:
        c.start()
    for c in loads[:3]:
        c.wait()

    def place_of(row, n):
        t = tiles_ref[row, n]
        owner = lax.shift_right_logical(t * 205, 10)
        return owner, pl.ds(pl.multiple_of((t - owner * ROW_TILES) * TILE, TILE), TILE)

    def run(slots, base, between):
        heads = len(slots)

        def rows_of(i):
            return pl.ds(pl.multiple_of(i * TILE, TILE), TILE)

        def groups_of(i):
            return lax.div(counts_ref[base + i] + (GROUP - 1), GROUP)

        def load_queries(i):
            qs = [q_ref[slot, rows_of(i), :].T for slot in slots]
            zero = jnp.zeros((HEAD_DIM, TILE), jnp.bfloat16)
            both = jnp.concatenate(
                [jnp.concatenate([qs[0], zero], axis=1), jnp.concatenate([zero, qs[1]], axis=1)], axis=0
            )
            return [both] + qs[2:]

        def score(i, side, g, peak, qt):
            count = counts_ref[base + i]
            at = [place_of(base + i, g * GROUP + t) for t in range(GROUP)]
            keys = [jnp.concatenate([kv_ref[o, 2 * h, r, :] for o, r in at], axis=0) for h in range(heads)]
            pair = jnp.dot(jnp.concatenate(keys[:2], axis=1), qt[0], preferred_element_type=jnp.float32)
            s = [pair[:, :TILE], pair[:, TILE:]]
            if heads == 3:
                s.append(jnp.dot(keys[2], qt[1], preferred_element_type=jnp.float32))
            out = []
            for h in range(heads):
                top = peak[h]
                for t in range(GROUP):
                    part = jnp.where(g * GROUP + t < count, s[h][t * TILE : (t + 1) * TILE], MASKED)
                    scores[side][h][g * GROUP + t] = part
                    top = jnp.maximum(top, jnp.max(part.reshape(TILE // 8, 8, TILE), axis=0))
                out.append(top)
            return tuple(out)

        def blend(i, side, g, totals, peak):
            at = [place_of(base + i, g * GROUP + t) for t in range(GROUP)]
            out = []
            for h in range(heads):
                total = totals[h]
                weights = []
                for t in range(GROUP):
                    w = jnp.exp2((scores[side][h][g * GROUP + t] - peak[h]) * factor)
                    total = total + jnp.sum(w.reshape(TILE // 8, 8, TILE), axis=0)
                    weights.append(w.astype(jnp.bfloat16))
                values = jnp.concatenate([kv_ref[o, 2 * h + 1, r, :] for o, r in at], axis=1)
                accs[h][...] += jnp.dot(values, jnp.concatenate(weights, axis=0), preferred_element_type=jnp.float32)
                out.append(total)
            return tuple(out)

        lowest = tuple(jnp.full((8, TILE), MASKED, jnp.float32) for _ in slots)
        zeros = tuple(jnp.zeros((8, TILE), jnp.float32) for _ in slots)

        def row_max(peak):
            return tuple(jnp.max(p, axis=0, keepdims=True) for p in peak)

        def clear():
            for h in range(heads):
                accs[h][...] = jnp.zeros((HEAD_DIM, TILE), jnp.float32)

        def finish(i, totals):
            for h in range(heads):
                o = accs[h][...] * (1.0 / jnp.sum(totals[h], axis=0, keepdims=True))
                o_ref[slots[h], rows_of(i), :] = o.T.astype(o_ref.dtype)

        def step(i, side, peak):
            qt = load_queries(i + 1)
            peak = row_max(peak)
            clear()
            here, there = groups_of(i), groups_of(i + 1)
            both = jnp.minimum(here, there)

            def together(g, carry):
                return score(i + 1, 1 - side, g, carry[0], qt), blend(i, side, g, carry[1], peak)

            above, totals = lax.fori_loop(0, both, together, (lowest, zeros))
            above = lax.fori_loop(both, there, lambda g, c: score(i + 1, 1 - side, g, c, qt), above)
            totals = lax.fori_loop(both, here, lambda g, c: blend(i, side, g, c, peak), totals)
            finish(i, totals)
            return above

        qt = load_queries(0)
        peak = lax.fori_loop(0, groups_of(0), lambda g, c: score(0, 0, g, c, qt), lowest)
        between()
        peak = lax.fori_loop(0, 2, lambda n, c: step(2 * n + 1, 1, step(2 * n, 0, c)), peak)
        peak = row_max(peak)
        clear()
        finish(4, lax.fori_loop(0, groups_of(4), lambda g, c: blend(4, 0, g, c, peak), zeros))

    def values_here():
        for c in loads[3:]:
            c.wait()

    run((0, 1, 2), 0, values_here)
    run((3, 4), ROW_TILES, lambda: None)


def attend(tiles, counts, q, kv):
    room = -(-TILE_COUNT // GROUP) * GROUP
    return pl.pallas_call(
        attend_kernel,
        out_shape=jax.ShapeDtypeStruct((5, ROWS, HEAD_DIM), jnp.bfloat16),
        in_specs=[pl.BlockSpec(memory_space=pltpu.SMEM)] * 2
        + [pl.BlockSpec(memory_space=pltpu.VMEM), pl.BlockSpec(memory_space=pl.ANY)],
        out_specs=pl.BlockSpec(memory_space=pltpu.VMEM),
        scratch_shapes=[pltpu.VMEM((SEQ, 6, ROWS, HEAD_DIM), jnp.bfloat16)]
        + [pltpu.VMEM((room, TILE, TILE), jnp.float32)] * 6
        + [pltpu.VMEM((HEAD_DIM, TILE), jnp.float32)] * 3
        + [pltpu.SemaphoreType.DMA((6,))],
        compiler_params=pltpu.CompilerParams(vmem_limit_bytes=60 << 20),
        name="attend",
    )(tiles, counts, q, kv)


def project_kernel(
    o_ref, w_hbm, bias_ref, gate_ref, res_ref, out_ref,
    w, att, mine, sent, got, w_sem, put_sem, send_sem, z_sem, y_sem, far_sem, sum_sem,
):
    zl, x, core, y, zh = place()
    other = 1 - zl
    me = (zl * RING + x) * 2 + core
    head_me = y * 2 + zh
    to_pair = ((other * RING + x) * 2 + core, head_me)
    right, left, opposite = lax.rem(y + 1, RING), lax.rem(y + 3, RING), lax.rem(y + 2, RING)
    to_right, to_left = (me, right * 2 + zh), (me, left * 2 + zh)
    to_sum = (me, y * 2 + 1 - zh)

    barrier = pltpu.get_barrier_semaphore()
    neighbours = [to_pair, to_right, to_left, to_sum]
    for n in neighbours:
        pl.semaphore_signal(barrier, inc=1, device_id=n, device_id_type=MESH)
    fetch = pltpu.make_async_copy(w_hbm, w, w_sem)
    fetch.start()
    puts = []
    for c in range(ROW_TILES):
        rows = pl.ds(c * TILE, TILE)
        puts.append(
            pltpu.make_async_copy(o_ref.at[pl.ds(0, 2), rows], att.at[c, y, pl.ds(2 * zl, 2)], put_sem.at[2 * c])
        )
        puts.append(pltpu.make_async_copy(o_ref.at[2, rows], att.at[c, y, 4], put_sem.at[2 * c + 1]))
    for c in puts:
        c.start()
    pl.semaphore_wait(barrier, len(neighbours))

    sends = []

    def send(src, dst, recv, target):
        c = pltpu.make_async_remote_copy(
            src_ref=src, dst_ref=dst, send_sem=send_sem.at[len(sends)], recv_sem=recv, device_id=target, device_id_type=MESH
        )
        c.start()
        sends.append(c)

    def arrived(dst, recv, source):
        pltpu.make_async_remote_copy(
            src_ref=dst, dst_ref=dst, send_sem=send_sem.at[0], recv_sem=recv, device_id=source, device_id_type=MESH
        ).wait_recv()

    for c in range(ROW_TILES):
        send(
            o_ref.at[pl.ds(3, 2), pl.ds(c * TILE, TILE)], att.at[c, y, pl.ds(2 * zl, 2)], z_sem.at[c], to_pair
        )
    for c in range(ROW_TILES):
        puts[2 * c].wait()
        puts[2 * c + 1].wait()
        arrived(att.at[c, y, pl.ds(2 * other, 2)], z_sem.at[c], to_pair)
        send(att.at[c, y], att.at[c, y], y_sem.at[0, c], to_right)
        send(att.at[c, y], att.at[c, y], y_sem.at[1, c], to_left)

    def halves(c):
        cut = 3 if c % 2 == 0 else 2
        return pl.ds(0, cut), pl.ds(cut, 5 - cut)

    def contract(c):
        first, second = halves(c)
        arrived(att.at[c, opposite, first], far_sem.at[0, c], to_left)
        arrived(att.at[c, opposite, second], far_sem.at[1, c], to_right)
        if c == 0:
            fetch.wait()
        rows = jnp.concatenate([att[c, n, h] for n in range(RING) for h in range(5)], axis=1)
        theirs = w[:, pl.ds(pl.multiple_of((1 - zh) * ROWS, TILE), ROWS)]
        sent[c] = jnp.dot(rows, theirs, preferred_element_type=jnp.float32).astype(jnp.bfloat16)
        send(sent.at[c], got.at[c], sum_sem.at[c], to_sum)
        ours = w[:, pl.ds(pl.multiple_of(zh * ROWS, TILE), ROWS)]
        mine[c] = jnp.dot(rows, ours, preferred_element_type=jnp.float32)

    for c in range(ROW_TILES):
        first, second = halves(c)
        arrived(att.at[c, left], y_sem.at[0, c], to_left)
        send(att.at[c, left, first], att.at[c, left, first], far_sem.at[0, c], to_right)
        arrived(att.at[c, right], y_sem.at[1, c], to_right)
        send(att.at[c, right, second], att.at[c, right, second], far_sem.at[1, c], to_left)
        if c > 0:
            contract(c - 1)
    contract(ROW_TILES - 1)
    for c in range(ROW_TILES):
        arrived(got.at[c], sum_sem.at[c], to_sum)
        rows = pl.ds(c * TILE, TILE)
        projected = mine[c] + got[c].astype(jnp.float32)
        out = res_ref[rows, :].astype(jnp.float32) + gate_ref[...] * (projected + bias_ref[...])
        out_ref[rows, :] = out.astype(out_ref.dtype)
    for c in sends:
        c.wait_send()


def project(o, panel, bias, gate, residual):
    bf16 = jnp.bfloat16
    return pl.pallas_call(
        project_kernel,
        out_shape=jax.ShapeDtypeStruct((ROWS, ROWS), bf16),
        in_specs=[
            pl.BlockSpec(memory_space=pltpu.VMEM),
            pl.BlockSpec(memory_space=pl.ANY),
            pl.BlockSpec(memory_space=pltpu.VMEM),
            pl.BlockSpec(memory_space=pltpu.VMEM),
            pl.BlockSpec(memory_space=pltpu.VMEM),
        ],
        out_specs=pl.BlockSpec(memory_space=pltpu.VMEM),
        scratch_shapes=[
            pltpu.VMEM((RING * ROWS, 2 * ROWS), bf16),
            pltpu.VMEM((ROW_TILES, RING, 5, TILE, HEAD_DIM), bf16),
            pltpu.VMEM((ROW_TILES, TILE, ROWS), jnp.float32),
            pltpu.VMEM((ROW_TILES, TILE, ROWS), bf16),
            pltpu.VMEM((ROW_TILES, TILE, ROWS), bf16),
            pltpu.SemaphoreType.DMA,
            pltpu.SemaphoreType.DMA((10,)),
            pltpu.SemaphoreType.DMA((32,)),
            pltpu.SemaphoreType.DMA((5,)),
            pltpu.SemaphoreType.DMA((2, 5)),
            pltpu.SemaphoreType.DMA((2, 5)),
            pltpu.SemaphoreType.DMA((5,)),
        ],
        compiler_params=pltpu.CompilerParams(collective_id=1, has_side_effects=True, vmem_limit_bytes=40 << 20),
        name="project",
    )(o, panel, bias, gate, residual)


def tile_lists(tile_mask):
    zl, x, core, _, _ = place()
    own = (zl * RING + x) * 2 + core
    pair = ((1 - zl) * RING + x) * 2 + core
    rows = jnp.concatenate(
        [lax.dynamic_slice_in_dim(tile_mask, first * ROW_TILES, ROW_TILES, 0) for first in (own, pair)], axis=0
    )
    allowed = rows > 0
    at = jnp.arange(TILE_COUNT, dtype=jnp.int32)
    before = jnp.sum(jnp.where(allowed[:, None, :] & (at[None, None, :] < at[None, :, None]), 1, 0), axis=2)
    hit = allowed[:, None, :] & (before[:, None, :] == at[None, :, None])
    tiles = jnp.sum(jnp.where(hit, at[None, None, :], 0), axis=2)
    return tiles.astype(jnp.int32), jnp.sum(allowed, axis=1).astype(jnp.int32)


def local(queries, key_states, value_states, tile_mask, out_weight, out_bias, residual, gate_scale):
    tiles, counts = tile_lists(tile_mask)
    kv, q, panel = gather(queries, key_states, value_states, out_weight)
    o = attend(tiles, counts, q, kv)
    return project(o, panel.reshape(RING * ROWS, 2 * ROWS), out_bias[None, :], gate_scale[None, :], residual)


def solution(mesh):
    return jax.shard_map(
        local,
        mesh=mesh,
        in_specs=(
            P("seq", "head"),
            P("seq", "head"),
            P("seq", "head"),
            P(),
            P("head", None),
            P("head"),
            P("seq", "head"),
            P("head"),
        ),
        out_specs=P("seq", "head"),
        check_vma=False,
    )
```

```python
import jax
import jax.numpy as jnp
from jax import lax
from jax.experimental import pallas as pl
from jax.experimental.pallas import tpu as pltpu
from jax.sharding import PartitionSpec as P

HEAD_DIM = 128
TILE = 128
ROWS = 640
ROW_TILES = ROWS // TILE
SEQ = 16
RING = 4
TILE_COUNT = 80
MESH = pl.DeviceIdType.MESH
MASKED = -1e30


def place():
    s = lax.axis_index("seq")
    h = lax.axis_index("head")
    return lax.div(s, 8), lax.rem(lax.div(s, 2), 4), lax.rem(s, 2), lax.div(h, 2), lax.rem(h, 2)


def gather_kernel(
    q_ref, k_ref, v_ref, w_ref, kv_out, q_out, w_out,
    stage, raw_values, stage_sem, local_sem, send_sem, z_sem, x_sem, far_sem, sib_sem, w_sem, w_sib_sem,
):
    zl, x, core, y, zh = place()
    other = 1 - zl
    right, left = lax.rem(x + 1, RING), lax.rem(x + 3, RING)
    opposite = lax.rem(x + 2, RING)

    def seq_of(zl_, x_, core_):
        return (zl_ * RING + x_) * 2 + core_

    head_me = y * 2 + zh
    me = seq_of(zl, x, core)
    to_pair = (seq_of(other, x, core), head_me)
    to_right = (seq_of(zl, right, core), head_me)
    to_left = (seq_of(zl, left, core), head_me)
    to_sib = (seq_of(zl, x, 1 - core), head_me)
    to_y = [(me, lax.rem(y + d, RING) * 2 + zh) for d in (1, 2, 3)]

    barrier = pltpu.get_barrier_semaphore()
    neighbours = [to_pair, to_right, to_left, to_sib] + to_y
    for n in neighbours:
        pl.semaphore_signal(barrier, inc=1, device_id=n, device_id_type=MESH)

    def head_columns(h):
        return pl.ds(pl.multiple_of(h * HEAD_DIM, HEAD_DIM), HEAD_DIM)

    own_a, pair_a = zl * 2, other * 2
    staged = [
        (k_ref, own_a, stage.at[0]),
        (k_ref, own_a + 1, stage.at[2]),
        (k_ref, 4, stage.at[4]),
        (k_ref, pair_a, stage.at[6]),
        (k_ref, pair_a + 1, stage.at[8]),
        (q_ref, pair_a, stage.at[10]),
        (q_ref, pair_a + 1, stage.at[11]),
        (v_ref, own_a, raw_values.at[0]),
        (v_ref, own_a + 1, raw_values.at[1]),
        (v_ref, 4, raw_values.at[2]),
        (v_ref, pair_a, raw_values.at[3]),
        (v_ref, pair_a + 1, raw_values.at[4]),
    ]
    stage_copies = [
        pltpu.make_async_copy(src.at[:, head_columns(h)], dst, stage_sem.at[n])
        for n, (src, h, dst) in enumerate(staged)
    ]
    for c in stage_copies:
        c.start()
    half = pl.ds(pl.multiple_of(core * (ROWS // 2), ROWS // 2), ROWS // 2)
    other_half = pl.ds(pl.multiple_of((1 - core) * (ROWS // 2), ROWS // 2), ROWS // 2)

    def panel(y_):
        return pl.ds(pl.multiple_of(y_ * (2 * ROWS), 2 * ROWS), 2 * ROWS)

    local = [
        pltpu.make_async_copy(q_ref.at[:, head_columns(zl * 2)], q_out.at[0], local_sem.at[0]),
        pltpu.make_async_copy(q_ref.at[:, head_columns(zl * 2 + 1)], q_out.at[1], local_sem.at[1]),
        pltpu.make_async_copy(q_ref.at[:, head_columns(4)], q_out.at[2], local_sem.at[2]),
        pltpu.make_async_copy(w_ref.at[half, panel(y)], w_out.at[y, half], local_sem.at[3]),
    ]
    for c in local:
        c.start()
    for c in stage_copies:
        c.wait()

    def turn(n, _):
        piece = lax.div(n, ROW_TILES)
        rows = pl.ds(pl.multiple_of((n - piece * ROW_TILES) * TILE, TILE), TILE)
        stage[2 * piece + 1, rows, :] = raw_values[piece, rows, :].T
        return 0

    lax.fori_loop(0, 5 * ROW_TILES, turn, 0)
    own = pltpu.make_async_copy(stage.at[pl.ds(0, 6)], kv_out.at[me], local_sem.at[4])
    own.start()
    pl.semaphore_wait(barrier, len(neighbours))

    sends = []

    def send(src, dst, recv, target):
        c = pltpu.make_async_remote_copy(
            src_ref=src, dst_ref=dst, send_sem=send_sem.at[len(sends)], recv_sem=recv, device_id=target, device_id_type=MESH
        )
        c.start()
        sends.append(c)

    def arrived(dst, recv, source):
        pltpu.make_async_remote_copy(
            src_ref=dst, dst_ref=dst, send_sem=send_sem.at[0], recv_sem=recv, device_id=source, device_id_type=MESH
        ).wait_recv()

    A, B, H = pl.ds(0, 2), pl.ds(2, 2), pl.ds(4, 2)
    H0, H1 = pl.ds(4, 1), pl.ds(5, 1)
    sib_waits = []

    def to_sibling(origin_zl, origin_x, part):
        n = len(sib_waits)
        block = kv_out.at[seq_of(origin_zl, origin_x, core), part]
        send(block, block, sib_sem.at[n], to_sib)
        sib_waits.append((origin_zl, origin_x, part))

    def pass_on(origin_zl, origin_x, part, recv, target):
        block = kv_out.at[seq_of(origin_zl, origin_x, core), part]
        send(block, block, recv, target)

    def block_of(origin_zl, origin_x, part):
        return kv_out.at[seq_of(origin_zl, origin_x, core), part]

    send(stage.at[pl.ds(6, 2)], kv_out.at[me, A], z_sem.at[0], to_pair)
    send(stage.at[pl.ds(8, 2)], kv_out.at[me, B], z_sem.at[1], to_pair)
    for item, part, at in ((0, H, 4), (1, A, 0), (2, B, 2)):
        send(stage.at[pl.ds(at, 2)], kv_out.at[me, part], x_sem.at[0, item], to_right)
        send(stage.at[pl.ds(at, 2)], kv_out.at[me, part], x_sem.at[1, item], to_left)
    for d in range(3):
        send(w_ref.at[half, panel(lax.rem(y + d + 1, RING))], w_out.at[y, half], w_sem.at[d], to_y[d])
    own.wait()
    to_sibling(zl, x, pl.ds(0, 6))

    for item, part, n in ((3, A, 0), (4, B, 1)):
        arrived(block_of(other, x, part), z_sem.at[n], to_pair)
        pass_on(other, x, part, x_sem.at[0, item], to_right)
        pass_on(other, x, part, x_sem.at[1, item], to_left)
        if n == 0:
            send(stage.at[pl.ds(4, 2)], kv_out.at[me, H], z_sem.at[2], to_pair)
        else:
            send(stage.at[pl.ds(10, 2)], q_out.at[pl.ds(3, 2)], z_sem.at[3], to_pair)
        to_sibling(other, x, part)

    def from_left(item, zl_, part):
        arrived(block_of(zl_, left, part), x_sem.at[0, item], to_left)

    def from_right(item, zl_, part):
        arrived(block_of(zl_, right, part), x_sem.at[1, item], to_right)

    from_left(0, zl, H)
    pass_on(zl, left, H0, far_sem.at[0, 0], to_right)
    pass_on(zl, left, H, z_sem.at[4], to_pair)
    to_sibling(zl, left, H)
    from_right(0, zl, H)
    pass_on(zl, right, H1, far_sem.at[1, 0], to_left)
    pass_on(zl, right, H, z_sem.at[5], to_pair)
    to_sibling(zl, right, H)

    for item, zl_, far in ((1, zl, 1), (3, other, 2)):
        from_left(item, zl_, A)
        pass_on(zl_, left, A, far_sem.at[0, far], to_right)
        to_sibling(zl_, left, A)
        from_right(item, zl_, A)
        to_sibling(zl_, right, A)
        from_right(item + 1, zl_, B)
        pass_on(zl_, right, B, far_sem.at[1, far], to_left)
        to_sibling(zl_, right, B)
        from_left(item + 1, zl_, B)
        to_sibling(zl_, left, B)
        if far == 1:
            arrived(block_of(zl, opposite, H0), far_sem.at[0, 0], to_left)
            arrived(block_of(zl, opposite, H1), far_sem.at[1, 0], to_right)
            pass_on(zl, opposite, H, z_sem.at[6], to_pair)
            to_sibling(zl, opposite, H)
            arrived(block_of(other, x, H), z_sem.at[2], to_pair)
            to_sibling(other, x, H)
    for d in range(3):
        y_ = lax.rem(y + 3 - d, RING)
        arrived(w_out.at[y_, half], w_sem.at[d], to_y[2 - d])
    for d in range(4):
        y_ = lax.rem(y + d, RING)
        if d == 0:
            local[3].wait()
        send(w_out.at[y_, half], w_out.at[y_, half], w_sib_sem.at[d], to_sib)
    for zl_, far in ((zl, 1), (other, 2)):
        arrived(block_of(zl_, opposite, A), far_sem.at[0, far], to_left)
        to_sibling(zl_, opposite, A)
        arrived(block_of(zl_, opposite, B), far_sem.at[1, far], to_right)
        to_sibling(zl_, opposite, B)
    for n, x_ in ((4, left), (5, right), (6, opposite)):
        arrived(block_of(other, x_, H), z_sem.at[n], to_pair)
        to_sibling(other, x_, H)
    arrived(q_out.at[pl.ds(3, 2)], z_sem.at[3], to_pair)
    for d in range(4):
        y_ = lax.rem(y + d, RING)
        arrived(w_out.at[y_, other_half], w_sib_sem.at[d], to_sib)
    for n, (zl_, x_, part) in enumerate(sib_waits):
        arrived(kv_out.at[seq_of(zl_, x_, 1 - core), part], sib_sem.at[n], to_sib)
    for c in sends:
        c.wait_send()
    for c in local[:3]:
        c.wait()


def gather(q, k, v, w):
    bf16 = jnp.bfloat16
    return pl.pallas_call(
        gather_kernel,
        out_shape=[
            jax.ShapeDtypeStruct((SEQ, 6, ROWS, HEAD_DIM), bf16),
            jax.ShapeDtypeStruct((5, ROWS, HEAD_DIM), bf16),
            jax.ShapeDtypeStruct((RING, ROWS, 2 * ROWS), bf16),
        ],
        in_specs=[pl.BlockSpec(memory_space=pl.ANY)] * 4,
        out_specs=[pl.BlockSpec(memory_space=pl.ANY)] * 3,
        scratch_shapes=[
            pltpu.VMEM((12, ROWS, HEAD_DIM), bf16),
            pltpu.VMEM((5, ROWS, HEAD_DIM), bf16),
            pltpu.SemaphoreType.DMA((12,)),
            pltpu.SemaphoreType.DMA((5,)),
            pltpu.SemaphoreType.DMA((64,)),
            pltpu.SemaphoreType.DMA((7,)),
            pltpu.SemaphoreType.DMA((2, 5)),
            pltpu.SemaphoreType.DMA((2, 3)),
            pltpu.SemaphoreType.DMA((24,)),
            pltpu.SemaphoreType.DMA((3,)),
            pltpu.SemaphoreType.DMA((4,)),
        ],
        compiler_params=pltpu.CompilerParams(collective_id=0, has_side_effects=True),
        name="gather_heads",
    )(q, k, v, w)


GROUP = 10
LOG2E = 1.4426950408889634


def attend_kernel(
    mask_ref, q_ref, kv_hbm, o_ref, tiles_ref, counts_ref, kv_ref, s00, s01, s02, s10, s11, s12, acc0, acc1, acc2, sem
):
    scores = ((s00, s01, s02), (s10, s11, s12))
    accs = (acc0, acc1, acc2)
    factor = HEAD_DIM ** -0.5 * LOG2E
    loads = [pltpu.make_async_copy(kv_hbm.at[:, p], kv_ref.at[:, p], sem.at[p]) for p in (0, 2, 4, 1, 3, 5)]
    for c in loads:
        c.start()
    zl, x, core, _, _ = place()
    first = ((zl * RING + x) * 2 + core) * ROW_TILES
    first_pair = (((1 - zl) * RING + x) * 2 + core) * ROW_TILES

    def compact(i, _):
        row = jnp.where(i < ROW_TILES, first + i, first_pair + i - ROW_TILES)
        count = jnp.int32(0)
        for t in range(TILE_COUNT):
            tiles_ref[i, count] = jnp.int32(t)
            count = count + jnp.where(mask_ref[row, t] > 0, 1, 0)
        for t in range(GROUP):
            tiles_ref[i, count + t] = jnp.int32(0)
        counts_ref[i] = count
        return 0

    lax.fori_loop(0, 2 * ROW_TILES, compact, 0)
    for c in loads[:3]:
        c.wait()

    def place_of(row, n):
        t = tiles_ref[row, n]
        owner = lax.shift_right_logical(t * 205, 10)
        return owner, pl.ds(pl.multiple_of((t - owner * ROW_TILES) * TILE, TILE), TILE)

    def run(slots, base, between):
        heads = len(slots)

        def rows_of(i):
            return pl.ds(pl.multiple_of(i * TILE, TILE), TILE)

        def groups_of(i):
            return lax.div(counts_ref[base + i] + (GROUP - 1), GROUP)

        def load_queries(i):
            qs = [q_ref[slot, rows_of(i), :].T for slot in slots]
            zero = jnp.zeros((HEAD_DIM, TILE), jnp.bfloat16)
            both = jnp.concatenate(
                [jnp.concatenate([qs[0], zero], axis=1), jnp.concatenate([zero, qs[1]], axis=1)], axis=0
            )
            return [both] + qs[2:]

        def score(i, side, g, peak, qt):
            count = counts_ref[base + i]
            at = [place_of(base + i, g * GROUP + t) for t in range(GROUP)]
            keys = [jnp.concatenate([kv_ref[o, 2 * h, r, :] for o, r in at], axis=0) for h in range(heads)]
            pair = jnp.dot(jnp.concatenate(keys[:2], axis=1), qt[0], preferred_element_type=jnp.float32)
            s = [pair[:, :TILE], pair[:, TILE:]]
            if heads == 3:
                s.append(jnp.dot(keys[2], qt[1], preferred_element_type=jnp.float32))
            out = []
            for h in range(heads):
                top = peak[h]
                for t in range(GROUP):
                    part = jnp.where(g * GROUP + t < count, s[h][t * TILE : (t + 1) * TILE], MASKED)
                    scores[side][h][g * GROUP + t] = part
                    top = jnp.maximum(top, jnp.max(part.reshape(TILE // 8, 8, TILE), axis=0))
                out.append(top)
            return tuple(out)

        def blend(i, side, g, totals, peak):
            at = [place_of(base + i, g * GROUP + t) for t in range(GROUP)]
            out = []
            for h in range(heads):
                total = totals[h]
                weights = []
                for t in range(GROUP):
                    w = jnp.exp2((scores[side][h][g * GROUP + t] - peak[h]) * factor)
                    total = total + jnp.sum(w.reshape(TILE // 8, 8, TILE), axis=0)
                    weights.append(w.astype(jnp.bfloat16))
                values = jnp.concatenate([kv_ref[o, 2 * h + 1, r, :] for o, r in at], axis=1)
                accs[h][...] += jnp.dot(values, jnp.concatenate(weights, axis=0), preferred_element_type=jnp.float32)
                out.append(total)
            return tuple(out)

        lowest = tuple(jnp.full((8, TILE), MASKED, jnp.float32) for _ in slots)
        zeros = tuple(jnp.zeros((8, TILE), jnp.float32) for _ in slots)

        def row_max(peak):
            return tuple(jnp.max(p, axis=0, keepdims=True) for p in peak)

        def clear():
            for h in range(heads):
                accs[h][...] = jnp.zeros((HEAD_DIM, TILE), jnp.float32)

        def finish(i, totals):
            for h in range(heads):
                o = accs[h][...] * (1.0 / jnp.sum(totals[h], axis=0, keepdims=True))
                o_ref[slots[h], rows_of(i), :] = o.T.astype(o_ref.dtype)

        def step(i, side, peak):
            qt = load_queries(i + 1)
            peak = row_max(peak)
            clear()
            here, there = groups_of(i), groups_of(i + 1)
            both = jnp.minimum(here, there)

            def together(g, carry):
                return score(i + 1, 1 - side, g, carry[0], qt), blend(i, side, g, carry[1], peak)

            above, totals = lax.fori_loop(0, both, together, (lowest, zeros))
            above = lax.fori_loop(both, there, lambda g, c: score(i + 1, 1 - side, g, c, qt), above)
            totals = lax.fori_loop(both, here, lambda g, c: blend(i, side, g, c, peak), totals)
            finish(i, totals)
            return above

        qt = load_queries(0)
        peak = lax.fori_loop(0, groups_of(0), lambda g, c: score(0, 0, g, c, qt), lowest)
        between()
        peak = lax.fori_loop(0, 2, lambda n, c: step(2 * n + 1, 1, step(2 * n, 0, c)), peak)
        peak = row_max(peak)
        clear()
        finish(4, lax.fori_loop(0, groups_of(4), lambda g, c: blend(4, 0, g, c, peak), zeros))

    def values_here():
        for c in loads[3:]:
            c.wait()

    run((0, 1, 2), 0, values_here)
    run((3, 4), ROW_TILES, lambda: None)


def attend(tile_mask, q, kv):
    room = -(-TILE_COUNT // GROUP) * GROUP
    return pl.pallas_call(
        attend_kernel,
        out_shape=jax.ShapeDtypeStruct((5, ROWS, HEAD_DIM), jnp.bfloat16),
        in_specs=[
            pl.BlockSpec(memory_space=pltpu.SMEM),
            pl.BlockSpec(memory_space=pltpu.VMEM),
            pl.BlockSpec(memory_space=pl.ANY),
        ],
        out_specs=pl.BlockSpec(memory_space=pltpu.VMEM),
        scratch_shapes=[
            pltpu.SMEM((2 * ROW_TILES, TILE_COUNT + 16), jnp.int32),
            pltpu.SMEM((2 * ROW_TILES,), jnp.int32),
            pltpu.VMEM((SEQ, 6, ROWS, HEAD_DIM), jnp.bfloat16),
        ]
        + [pltpu.VMEM((room, TILE, TILE), jnp.float32)] * 6
        + [pltpu.VMEM((HEAD_DIM, TILE), jnp.float32)] * 3
        + [pltpu.SemaphoreType.DMA((6,))],
        compiler_params=pltpu.CompilerParams(vmem_limit_bytes=60 << 20),
        name="attend",
    )(tile_mask, q, kv)


def project_kernel(
    o_ref, w_hbm, bias_ref, gate_ref, res_hbm, out_ref,
    w, res_ref, att, mine, sent, got, w_sem, res_sem, put_sem, send_sem, z_sem, y_sem, far_sem, sum_sem,
):
    zl, x, core, y, zh = place()
    other = 1 - zl
    me = (zl * RING + x) * 2 + core
    head_me = y * 2 + zh
    to_pair = ((other * RING + x) * 2 + core, head_me)
    right, left, opposite = lax.rem(y + 1, RING), lax.rem(y + 3, RING), lax.rem(y + 2, RING)
    to_right, to_left = (me, right * 2 + zh), (me, left * 2 + zh)
    to_sum = (me, y * 2 + 1 - zh)

    barrier = pltpu.get_barrier_semaphore()
    neighbours = [to_pair, to_right, to_left, to_sum]
    for n in neighbours:
        pl.semaphore_signal(barrier, inc=1, device_id=n, device_id_type=MESH)
    fetch = pltpu.make_async_copy(w_hbm, w, w_sem)
    fetch.start()
    fetch_res = pltpu.make_async_copy(res_hbm, res_ref, res_sem)
    fetch_res.start()
    puts = []
    for c in range(ROW_TILES):
        rows = pl.ds(c * TILE, TILE)
        puts.append(
            pltpu.make_async_copy(o_ref.at[pl.ds(0, 2), rows], att.at[c, y, pl.ds(2 * zl, 2)], put_sem.at[2 * c])
        )
        puts.append(pltpu.make_async_copy(o_ref.at[2, rows], att.at[c, y, 4], put_sem.at[2 * c + 1]))
    for c in puts:
        c.start()
    pl.semaphore_wait(barrier, len(neighbours))

    sends = []

    def send(src, dst, recv, target):
        c = pltpu.make_async_remote_copy(
            src_ref=src, dst_ref=dst, send_sem=send_sem.at[len(sends)], recv_sem=recv, device_id=target, device_id_type=MESH
        )
        c.start()
        sends.append(c)

    def arrived(dst, recv, source):
        pltpu.make_async_remote_copy(
            src_ref=dst, dst_ref=dst, send_sem=send_sem.at[0], recv_sem=recv, device_id=source, device_id_type=MESH
        ).wait_recv()

    for c in range(ROW_TILES):
        send(
            o_ref.at[pl.ds(3, 2), pl.ds(c * TILE, TILE)], att.at[c, y, pl.ds(2 * zl, 2)], z_sem.at[c], to_pair
        )
    for c in range(ROW_TILES):
        puts[2 * c].wait()
        puts[2 * c + 1].wait()
        arrived(att.at[c, y, pl.ds(2 * other, 2)], z_sem.at[c], to_pair)
        send(att.at[c, y], att.at[c, y], y_sem.at[0, c], to_right)
        send(att.at[c, y], att.at[c, y], y_sem.at[1, c], to_left)

    def halves(c):
        cut = 3 if c % 2 == 0 else 2
        return pl.ds(0, cut), pl.ds(cut, 5 - cut)

    def contract(c):
        first, second = halves(c)
        arrived(att.at[c, opposite, first], far_sem.at[0, c], to_left)
        arrived(att.at[c, opposite, second], far_sem.at[1, c], to_right)
        if c == 0:
            fetch.wait()
        rows = jnp.concatenate([att[c, n, h] for n in range(RING) for h in range(5)], axis=1)
        theirs = w[:, pl.ds(pl.multiple_of((1 - zh) * ROWS, TILE), ROWS)]
        sent[c] = jnp.dot(rows, theirs, preferred_element_type=jnp.float32).astype(jnp.bfloat16)
        send(sent.at[c], got.at[c], sum_sem.at[c], to_sum)
        ours = w[:, pl.ds(pl.multiple_of(zh * ROWS, TILE), ROWS)]
        mine[c] = jnp.dot(rows, ours, preferred_element_type=jnp.float32)

    for c in range(ROW_TILES):
        first, second = halves(c)
        arrived(att.at[c, left], y_sem.at[0, c], to_left)
        send(att.at[c, left, first], att.at[c, left, first], far_sem.at[0, c], to_right)
        arrived(att.at[c, right], y_sem.at[1, c], to_right)
        send(att.at[c, right, second], att.at[c, right, second], far_sem.at[1, c], to_left)
        if c > 0:
            contract(c - 1)
    contract(ROW_TILES - 1)
    fetch_res.wait()
    for c in range(ROW_TILES):
        arrived(got.at[c], sum_sem.at[c], to_sum)
        rows = pl.ds(c * TILE, TILE)
        projected = mine[c] + got[c].astype(jnp.float32)
        out = res_ref[rows, :].astype(jnp.float32) + gate_ref[...] * (projected + bias_ref[...])
        out_ref[rows, :] = out.astype(out_ref.dtype)
    for c in sends:
        c.wait_send()


def project(o, panel, bias, gate, residual):
    bf16 = jnp.bfloat16
    return pl.pallas_call(
        project_kernel,
        out_shape=jax.ShapeDtypeStruct((ROWS, ROWS), bf16),
        in_specs=[
            pl.BlockSpec(memory_space=pltpu.VMEM),
            pl.BlockSpec(memory_space=pl.ANY),
            pl.BlockSpec(memory_space=pltpu.VMEM),
            pl.BlockSpec(memory_space=pltpu.VMEM),
            pl.BlockSpec(memory_space=pl.ANY),
        ],
        out_specs=pl.BlockSpec(memory_space=pltpu.VMEM),
        scratch_shapes=[
            pltpu.VMEM((RING * ROWS, 2 * ROWS), bf16),
            pltpu.VMEM((ROWS, ROWS), bf16),
            pltpu.VMEM((ROW_TILES, RING, 5, TILE, HEAD_DIM), bf16),
            pltpu.VMEM((ROW_TILES, TILE, ROWS), jnp.float32),
            pltpu.VMEM((ROW_TILES, TILE, ROWS), bf16),
            pltpu.VMEM((ROW_TILES, TILE, ROWS), bf16),
            pltpu.SemaphoreType.DMA,
            pltpu.SemaphoreType.DMA,
            pltpu.SemaphoreType.DMA((10,)),
            pltpu.SemaphoreType.DMA((32,)),
            pltpu.SemaphoreType.DMA((5,)),
            pltpu.SemaphoreType.DMA((2, 5)),
            pltpu.SemaphoreType.DMA((2, 5)),
            pltpu.SemaphoreType.DMA((5,)),
        ],
        compiler_params=pltpu.CompilerParams(collective_id=1, has_side_effects=True, vmem_limit_bytes=62 << 20),
        name="project",
    )(o, panel, bias, gate, residual)


LIMIT = 40
STEPS = LIMIT // GROUP
KEYS_OF = pl.ds(0, 1)
VALUES_OF = pl.ds(1, 1)


def whole_kernel(
    owners_ref, starts_ref, bars_ref, q_ref, k_ref, v_ref, w_ref, bias_ref, gate_ref, res_hbm, out_ref,
    stage, raw_values, kva, kvb, kvh, q_own, q_pair, att, back, panel, mine, theirs, sent, got, res_ref,
    s00, s01, s10, s11, acc0, acc1,
    stage_sem, local_sem, send_sem, z_sem, x_sem, far_sem, sib_sem, w_sem, w_sib_sem, ret_sem, y_sem, y_far_sem, sum_sem,
):
    zl, x, core, y, zh = place()
    other = 1 - zl
    right, left, opposite = lax.rem(x + 1, RING), lax.rem(x + 3, RING), lax.rem(x + 2, RING)
    y_right, y_left, y_opposite = lax.rem(y + 1, RING), lax.rem(y + 3, RING), lax.rem(y + 2, RING)

    def seq_of(zl_, x_, core_):
        return (zl_ * RING + x_) * 2 + core_

    head_me = y * 2 + zh
    me = seq_of(zl, x, core)
    to_pair = (seq_of(other, x, core), head_me)
    to_right = (seq_of(zl, right, core), head_me)
    to_left = (seq_of(zl, left, core), head_me)
    to_sib = (seq_of(zl, x, 1 - core), head_me)
    to_y = [(me, lax.rem(y + d, RING) * 2 + zh) for d in (1, 2, 3)]
    to_sum = (me, y * 2 + 1 - zh)

    barrier = pltpu.get_barrier_semaphore()
    neighbours = [to_pair, to_right, to_left, to_sib, to_sum] + to_y
    for n in neighbours:
        pl.semaphore_signal(barrier, inc=1, device_id=n, device_id_type=MESH)

    def head_columns(h):
        return pl.ds(pl.multiple_of(h * HEAD_DIM, HEAD_DIM), HEAD_DIM)

    own_a, pair_a = zl * 2, other * 2
    staged = [
        (k_ref, pair_a, stage.at[6]),
        (v_ref, pair_a, raw_values.at[3]),
        (k_ref, own_a, stage.at[0]),
        (v_ref, own_a, raw_values.at[0]),
        (k_ref, own_a + 1, stage.at[2]),
        (v_ref, own_a + 1, raw_values.at[1]),
        (k_ref, pair_a + 1, stage.at[8]),
        (v_ref, pair_a + 1, raw_values.at[4]),
        (k_ref, 4, stage.at[4]),
        (v_ref, 4, raw_values.at[2]),
        (q_ref, pair_a, stage.at[10]),
        (q_ref, pair_a + 1, stage.at[11]),
    ]
    stage_copies = [
        pltpu.make_async_copy(src.at[:, :, head_columns(h)], dst, stage_sem.at[n])
        for n, (src, h, dst) in enumerate(staged)
    ]
    for c in stage_copies:
        c.start()
    half = pl.ds(pl.multiple_of(core * (ROWS // 2), ROWS // 2), ROWS // 2)
    other_half = pl.ds(pl.multiple_of((1 - core) * (ROWS // 2), ROWS // 2), ROWS // 2)

    def columns_of(y_):
        return pl.ds(pl.multiple_of(y_ * (2 * ROWS), 2 * ROWS), 2 * ROWS)

    local = [
        pltpu.make_async_copy(q_ref.at[:, :, head_columns(own_a)], q_own.at[0], local_sem.at[0]),
        pltpu.make_async_copy(q_ref.at[:, :, head_columns(own_a + 1)], q_own.at[1], local_sem.at[1]),
        pltpu.make_async_copy(q_ref.at[:, :, head_columns(4)], q_own.at[2], local_sem.at[2]),
        pltpu.make_async_copy(w_ref.at[half, columns_of(y)], panel.at[y, half], local_sem.at[3]),
        pltpu.make_async_copy(res_hbm, res_ref, local_sem.at[4]),
    ]
    for c in local:
        c.start()
    for c in stage_copies:
        c.wait()

    def turn(n, _):
        piece = lax.div(n, ROW_TILES)
        r = n - piece * ROW_TILES
        stage[2 * piece + 1, r] = raw_values[piece, r].T
        return 0

    lax.fori_loop(0, 5 * ROW_TILES, turn, 0)
    own = [
        pltpu.make_async_copy(stage.at[pl.ds(2 * n, 2)], kv.at[me], local_sem.at[5 + n])
        for n, kv in enumerate((kva, kvb, kvh))
    ]
    for c in own:
        c.start()
    pl.semaphore_wait(barrier, len(neighbours))

    sends = []

    def send(src, dst, recv, target):
        c = pltpu.make_async_remote_copy(
            src_ref=src, dst_ref=dst, send_sem=send_sem.at[len(sends)], recv_sem=recv, device_id=target, device_id_type=MESH
        )
        c.start()
        sends.append(c)

    def arrived(dst, recv, source):
        pltpu.make_async_remote_copy(
            src_ref=dst, dst_ref=dst, send_sem=send_sem.at[0], recv_sem=recv, device_id=source, device_id_type=MESH
        ).wait_recv()

    both_parts = pl.ds(0, 2)
    k_part, v_part = KEYS_OF, VALUES_OF
    sib_waits = {"a": [], "b": [], "h": []}
    sib_count = [0]

    def block(kv, zl_, x_, part=both_parts):
        return kv.at[seq_of(zl_, x_, core), part]

    def to_sibling(name, kv, zl_, x_, part=both_parts):
        n = sib_count[0]
        sib_count[0] += 1
        send(block(kv, zl_, x_, part), block(kv, zl_, x_, part), sib_sem.at[n], to_sib)
        sib_waits[name].append((n, kv, zl_, x_, part))

    def from_sibling(name):
        for n, kv, zl_, x_, part in sib_waits[name]:
            arrived(kv.at[seq_of(zl_, x_, 1 - core), part], sib_sem.at[n], to_sib)

    def ring_send(item, kv, zl_, x_, part=both_parts):
        send(block(kv, zl_, x_, part), block(kv, zl_, x_, part), x_sem.at[0, item], to_right)
        send(block(kv, zl_, x_, part), block(kv, zl_, x_, part), x_sem.at[1, item], to_left)

    def ring_pass(item, name, kv, zl_):
        arrived(block(kv, zl_, left), x_sem.at[0, item], to_left)
        send(block(kv, zl_, left, k_part), block(kv, zl_, left, k_part), far_sem.at[0, item], to_right)
        arrived(block(kv, zl_, right), x_sem.at[1, item], to_right)
        send(block(kv, zl_, right, v_part), block(kv, zl_, right, v_part), far_sem.at[1, item], to_left)
        to_sibling(name, kv, zl_, left)
        to_sibling(name, kv, zl_, right)

    def ring_far(item, name, kv, zl_):
        arrived(block(kv, zl_, opposite, k_part), far_sem.at[0, item], to_left)
        arrived(block(kv, zl_, opposite, v_part), far_sem.at[1, item], to_right)
        to_sibling(name, kv, zl_, opposite)

    A0, A1, B0, B1, H0, V1 = range(6)
    send(stage.at[pl.ds(6, 2)], kva.at[me], z_sem.at[0], to_pair)
    own[0].wait()
    ring_send(A0, kva, zl, x)
    to_sibling("a", kva, zl, x)
    for d in range(3):
        send(w_ref.at[half, columns_of(lax.rem(y + d + 1, RING))], panel.at[y, half], w_sem.at[d], to_y[d])
    own[1].wait()
    own[2].wait()
    arrived(block(kva, other, x), z_sem.at[0], to_pair)
    ring_send(A1, kva, other, x)
    send(stage.at[pl.ds(8, 2)], kvb.at[me], z_sem.at[1], to_pair)
    send(stage.at[pl.ds(10, 2)], q_pair, z_sem.at[2], to_pair)
    to_sibling("a", kva, other, x)
    ring_pass(A0, "a", kva, zl)
    ring_pass(A1, "a", kva, other)
    ring_send(B0, kvb, zl, x)
    to_sibling("b", kvb, zl, x)
    arrived(block(kvb, other, x), z_sem.at[1], to_pair)
    ring_send(B1, kvb, other, x)
    to_sibling("b", kvb, other, x)
    send(stage.at[pl.ds(4, 2)], kvh.at[me], z_sem.at[3], to_pair)
    ring_far(A0, "a", kva, zl)
    ring_far(A1, "a", kva, other)
    for c in local[:3]:
        c.wait()
    arrived(q_pair, z_sem.at[2], to_pair)
    from_sibling("a")

    scores = ((s00, s01), (s10, s11))
    accs = (acc0, acc1)
    factor = HEAD_DIM ** -0.5 * LOG2E
    lowest = jnp.full((8, TILE), MASKED, jnp.float32)
    nothing = jnp.zeros((8, TILE), jnp.float32)

    def place_of(row, n):
        return owners_ref[row, n], starts_ref[row, n]

    def score(kv, rows, side, g, peaks, queries):
        out = []
        for u, row in enumerate(rows):
            at = [place_of(row, g * GROUP + t) for t in range(GROUP)]
            keys = jnp.concatenate([kv[o, 0, r] for o, r in at], axis=0)
            s = jnp.dot(keys, queries[u], preferred_element_type=jnp.float32)
            top = peaks[u]
            for t in range(GROUP):
                part = s[t * TILE : (t + 1) * TILE] + bars_ref[row, g * GROUP + t]
                scores[side][u][g * GROUP + t] = part
                top = jnp.maximum(top, jnp.max(part.reshape(TILE // 8, 8, TILE), axis=0))
            out.append(top)
        return tuple(out)

    def blend(kv, rows, side, g, totals, peaks):
        out = []
        for u, row in enumerate(rows):
            total = totals[u]
            weights = []
            for t in range(GROUP):
                w = jnp.exp2((scores[side][u][g * GROUP + t] - peaks[u]) * factor)
                total = total + jnp.sum(w.reshape(TILE // 8, 8, TILE), axis=0)
                weights.append(w.astype(jnp.bfloat16))
            at = [place_of(row, g * GROUP + t) for t in range(GROUP)]
            values = jnp.concatenate([kv[o, 1, r] for o, r in at], axis=1)
            accs[u][...] += jnp.dot(values, jnp.concatenate(weights, axis=0), preferred_element_type=jnp.float32)
            out.append(total)
        return tuple(out)

    def attention(kv, plan, tasks):
        peaks = None
        for i in range(-1, len(plan)):
            here = plan[i] if i >= 0 else []
            there = plan[i + 1] if i + 1 < len(plan) else []
            side = i % 2
            rows, rows_next = [u[0] for u in here], [u[0] for u in there]
            queries = [q_of[j, r].T for _, (q_of, j, r), _ in there]
            tops = [jnp.max(p, axis=0, keepdims=True) for p in peaks] if here else []
            for u in range(len(here)):
                accs[u][...] = jnp.zeros((HEAD_DIM, TILE), jnp.float32)

            def body(g, carry):
                new_peaks = score(kv, rows_next, 1 - side, g, carry[0], queries)
                return new_peaks, blend(kv, rows, side, g, carry[1], tops)

            peaks, totals = lax.fori_loop(0, STEPS, body, ((lowest,) * len(there), (nothing,) * len(here)))
            for u, (_, _, (dst, r)) in enumerate(here):
                o = accs[u][...] * (1.0 / jnp.sum(totals[u], axis=0, keepdims=True))
                dst[r, :] = o.T.astype(jnp.bfloat16)
            if i in tasks:
                tasks[i]()

    def tile_rows(i):
        return pl.ds(i * TILE, TILE)

    def plan_of(j):
        return [
            [
                (i, (q_own, j, i), (att.at[y, own_a + j], tile_rows(i))),
                (ROW_TILES + i, (q_pair, j, i), (back.at[j], tile_rows(i))),
            ]
            for i in range(ROW_TILES)
        ]

    positions = [own_a, own_a + 1, pair_a, pair_a + 1, 4]

    def y_send(n):
        send(att.at[y, positions[n]], att.at[y, positions[n]], y_sem.at[0, n], to_y[0])
        send(att.at[y, positions[n]], att.at[y, positions[n]], y_sem.at[1, n], to_y[2])

    def y_parts(n):
        cut = (3 if n % 2 == 0 else 2) * TILE
        return pl.ds(0, cut), pl.ds(cut, ROWS - cut)

    def y_pass(n):
        first, second = y_parts(n)
        arrived(att.at[y_left, positions[n]], y_sem.at[0, n], to_y[2])
        part = att.at[y_left, positions[n], first]
        send(part, part, y_far_sem.at[0, n], to_y[0])
        arrived(att.at[y_right, positions[n]], y_sem.at[1, n], to_y[0])
        part = att.at[y_right, positions[n], second]
        send(part, part, y_far_sem.at[1, n], to_y[2])

    def y_far(n):
        first, second = y_parts(n)
        arrived(att.at[y_opposite, positions[n], first], y_far_sem.at[0, n], to_y[2])
        arrived(att.at[y_opposite, positions[n], second], y_far_sem.at[1, n], to_y[0])

    def give_back(j):
        send(back.at[j], att.at[y, own_a + j], ret_sem.at[j], to_pair)

    def given_back(j):
        arrived(att.at[y, pair_a + j], ret_sem.at[j], to_pair)
        y_send(2 + j)

    ours_columns = pl.ds(pl.multiple_of(zh * ROWS, TILE), ROWS)
    theirs_columns = pl.ds(pl.multiple_of((1 - zh) * ROWS, TILE), ROWS)

    def product(units, rows, columns):
        lhs = jnp.concatenate([att[n, positions[u], rows, :] for u in units for n in range(RING)], axis=1)
        rhs = jnp.concatenate([panel[n, head_columns(positions[u]), columns] for u in units for n in range(RING)], axis=0)
        return jnp.dot(lhs, rhs, preferred_element_type=jnp.float32)

    def contract(units, first):
        def one(c, _):
            rows = pl.ds(pl.multiple_of(c * TILE, TILE), TILE)
            for total, columns in ((theirs, theirs_columns), (mine, ours_columns)):
                p = product(units, rows, columns)
                total[rows, :] = p if first else total[rows, :] + p
            return 0

        lax.fori_loop(0, ROW_TILES, one, 0)

    def panel_here():
        for d in range(3):
            arrived(panel.at[lax.rem(y + 3 - d, RING), half], w_sem.at[d], to_y[2 - d])
        local[3].wait()
        for d in range(RING):
            y_ = lax.rem(y + d, RING)
            send(panel.at[y_, half], panel.at[y_, half], w_sib_sem.at[d], to_sib)

    def after_a1():
        ring_pass(B0, "b", kvb, zl)

    def after_a3():
        ring_pass(B1, "b", kvb, other)
        ring_send(H0, kvh, zl, x)
        to_sibling("h", kvh, zl, x)

    attention(kva, plan_of(0), {1: after_a1, 3: after_a3})
    give_back(0)
    y_send(0)
    arrived(block(kvh, other, x), z_sem.at[3], to_pair)
    ring_send(V1, kvh, other, x, v_part)
    to_sibling("h", kvh, other, x)
    ring_far(B0, "b", kvb, zl)
    ring_far(B1, "b", kvb, other)
    panel_here()
    from_sibling("b")

    v_first, v_second = pl.ds(0, 3), pl.ds(3, 2)

    def v_block(x_, rows=None):
        at = kvh.at[seq_of(other, x_, core), 1]
        return at if rows is None else at.at[rows]

    def after_b1():
        given_back(0)
        ring_pass(H0, "h", kvh, zl)
        for n, x_ in ((4, left), (5, right)):
            send(block(kvh, zl, x_, k_part), block(kvh, zl, x_, k_part), z_sem.at[n], to_pair)
        y_pass(0)

    def after_b3():
        arrived(block(kvh, other, left, v_part), x_sem.at[0, V1], to_left)
        send(v_block(left, v_first), v_block(left, v_first), far_sem.at[0, V1], to_right)
        arrived(block(kvh, other, right, v_part), x_sem.at[1, V1], to_right)
        send(v_block(right, v_second), v_block(right, v_second), far_sem.at[1, V1], to_left)
        to_sibling("h", kvh, other, left, v_part)
        to_sibling("h", kvh, other, right, v_part)
        y_pass(2)

    attention(kvb, plan_of(1), {1: after_b1, 3: after_b3})
    give_back(1)
    y_send(1)
    ring_far(H0, "h", kvh, zl)
    send(block(kvh, zl, opposite, k_part), block(kvh, zl, opposite, k_part), z_sem.at[6], to_pair)
    arrived(v_block(opposite, v_first), far_sem.at[0, V1], to_left)
    arrived(v_block(opposite, v_second), far_sem.at[1, V1], to_right)
    to_sibling("h", kvh, other, opposite, v_part)
    for n, x_ in ((4, left), (5, right)):
        arrived(block(kvh, other, x_, k_part), z_sem.at[n], to_pair)
        to_sibling("h", kvh, other, x_, k_part)
    given_back(1)
    y_far(0)
    y_far(2)
    for d in range(RING):
        arrived(panel.at[lax.rem(y + d, RING), other_half], w_sib_sem.at[d], to_sib)
    contract((0, 2), True)
    arrived(block(kvh, other, opposite, k_part), z_sem.at[6], to_pair)
    to_sibling("h", kvh, other, opposite, k_part)
    y_pass(1)
    from_sibling("h")

    units = [
        (i, (q_own, 2, i), (att.at[y, 4], tile_rows(i))) for i in range(ROW_TILES)
    ]
    attention(kvh, [units[0:2], units[2:4], units[4:5]], {0: lambda: y_pass(3)})
    y_send(4)
    y_far(1)
    y_far(3)
    contract((1, 3), False)
    y_pass(4)
    y_far(4)
    for c in range(ROW_TILES):
        rows = tile_rows(c)
        sent[rows, :] = (theirs[rows, :] + product((4,), rows, theirs_columns)).astype(sent.dtype)
        send(sent.at[rows], got.at[rows], sum_sem.at[c], to_sum)
    local[4].wait()
    for c in range(ROW_TILES):
        rows = tile_rows(c)
        mine[rows, :] = mine[rows, :] + product((4,), rows, ours_columns)
    for c in range(ROW_TILES):
        rows = tile_rows(c)
        arrived(got.at[rows], sum_sem.at[c], to_sum)
        projected = mine[rows, :] + got[rows, :].astype(jnp.float32)
        out = res_ref[rows, :].astype(jnp.float32) + gate_ref[...] * (projected + bias_ref[...])
        out_ref[rows, :] = out.astype(out_ref.dtype)
    for c in sends:
        c.wait_send()


def whole(owners, starts, bars, q, k, v, w, bias, gate, residual):
    bf16, f32 = jnp.bfloat16, jnp.float32

    def by_tile(array):
        return array.reshape(ROW_TILES, TILE, ROWS)

    smem, vmem, anywhere = (
        pl.BlockSpec(memory_space=pltpu.SMEM),
        pl.BlockSpec(memory_space=pltpu.VMEM),
        pl.BlockSpec(memory_space=pl.ANY),
    )
    dma = pltpu.SemaphoreType.DMA
    return pl.pallas_call(
        whole_kernel,
        out_shape=jax.ShapeDtypeStruct((ROWS, ROWS), bf16),
        in_specs=[smem, smem, smem, anywhere, anywhere, anywhere, anywhere, vmem, vmem, anywhere],
        out_specs=vmem,
        scratch_shapes=[
            pltpu.VMEM((12, ROW_TILES, TILE, HEAD_DIM), bf16),
            pltpu.VMEM((5, ROW_TILES, TILE, HEAD_DIM), bf16),
            pltpu.VMEM((SEQ, 2, ROW_TILES, TILE, HEAD_DIM), bf16),
            pltpu.VMEM((SEQ, 2, ROW_TILES, TILE, HEAD_DIM), bf16),
            pltpu.VMEM((SEQ, 2, ROW_TILES, TILE, HEAD_DIM), bf16),
            pltpu.VMEM((3, ROW_TILES, TILE, HEAD_DIM), bf16),
            pltpu.VMEM((2, ROW_TILES, TILE, HEAD_DIM), bf16),
            pltpu.VMEM((RING, 5, ROWS, HEAD_DIM), bf16),
            pltpu.VMEM((2, ROWS, HEAD_DIM), bf16),
            pltpu.VMEM((RING, ROWS, 2 * ROWS), bf16),
            pltpu.VMEM((ROWS, ROWS), f32),
            pltpu.VMEM((ROWS, ROWS), f32),
            pltpu.VMEM((ROWS, ROWS), bf16),
            pltpu.VMEM((ROWS, ROWS), bf16),
            pltpu.VMEM((ROWS, ROWS), bf16),
        ]
        + [pltpu.VMEM((LIMIT, TILE, TILE), f32)] * 4
        + [pltpu.VMEM((HEAD_DIM, TILE), f32)] * 2
        + [
            dma((12,)), dma((8,)), dma((96,)), dma((7,)), dma((2, 6)), dma((2, 6)), dma((28,)), dma((3,)), dma((4,)),
            dma((2,)), dma((2, 5)), dma((2, 5)), dma((5,)),
        ],
        compiler_params=pltpu.CompilerParams(collective_id=2, has_side_effects=True, vmem_limit_bytes=62 << 20),
        name="whole",
    )(owners, starts, bars, by_tile(q), by_tile(k), by_tile(v), w, bias, gate, residual)


def tile_lists(tile_mask):
    zl, x, core, _, _ = place()
    own = (zl * RING + x) * 2 + core
    pair = ((1 - zl) * RING + x) * 2 + core
    rows = jnp.concatenate(
        [lax.dynamic_slice_in_dim(tile_mask, first * ROW_TILES, ROW_TILES, 0) for first in (own, pair)], axis=0
    )
    allowed = rows > 0
    at = jnp.arange(TILE_COUNT, dtype=jnp.int32)
    before = jnp.sum(jnp.where(allowed[:, None, :] & (at[None, None, :] < at[None, :, None]), 1, 0), axis=2)
    hit = allowed[:, None, :] & (before[:, None, :] == at[None, :LIMIT, None])
    tiles = jnp.sum(jnp.where(hit, at[None, None, :], 0), axis=2)
    tiles = tiles.astype(jnp.int32)
    bars = jnp.where(at[None, :LIMIT] < jnp.sum(allowed, axis=1)[:, None], 0.0, MASKED).astype(jnp.float32)
    return tiles // ROW_TILES, tiles % ROW_TILES, bars


def local(queries, key_states, value_states, tile_mask, out_weight, out_bias, residual, gate_scale):
    bias, gate = out_bias[None, :], gate_scale[None, :]

    def by_lists(_):
        owners, starts, bars = tile_lists(tile_mask)
        return whole(owners, starts, bars, queries, key_states, value_states, out_weight, bias, gate, residual)

    def in_parts(_):
        kv, q, panel = gather(queries, key_states, value_states, out_weight)
        o = attend(tile_mask, q, kv)
        return project(o, panel.reshape(RING * ROWS, 2 * ROWS), bias, gate, residual)

    longest = jnp.max(jnp.sum((tile_mask > 0).astype(jnp.int32), axis=1))
    return lax.cond(longest <= LIMIT, by_lists, in_parts, 0)


def solution(mesh):
    return jax.shard_map(
        local,
        mesh=mesh,
        in_specs=(
            P("seq", "head"),
            P("seq", "head"),
            P("seq", "head"),
            P(),
            P("head", None),
            P("head"),
            P("seq", "head"),
            P("head"),
        ),
        out_specs=P("seq", "head"),
        check_vma=False,
    )
```

```python
import jax
import jax.numpy as jnp
from jax import lax
from jax.experimental import pallas as pl
from jax.experimental.pallas import tpu as pltpu
from jax.sharding import PartitionSpec as P

HEAD_DIM = 128
TILE = 128
ROWS = 640
ROW_TILES = ROWS // TILE
SEQ = 16
RING = 4
TILE_COUNT = 80
MESH = pl.DeviceIdType.MESH
MASKED = -1e30


def place():
    s = lax.axis_index("seq")
    h = lax.axis_index("head")
    return lax.div(s, 8), lax.rem(lax.div(s, 2), 4), lax.rem(s, 2), lax.div(h, 2), lax.rem(h, 2)


def gather_kernel(
    q_ref, k_ref, v_ref, w_ref, kv_out, q_out, w_out,
    stage, raw_values, stage_sem, local_sem, send_sem, z_sem, x_sem, far_sem, sib_sem, w_sem, w_sib_sem,
):
    zl, x, core, y, zh = place()
    other = 1 - zl
    right, left = lax.rem(x + 1, RING), lax.rem(x + 3, RING)
    opposite = lax.rem(x + 2, RING)

    def seq_of(zl_, x_, core_):
        return (zl_ * RING + x_) * 2 + core_

    head_me = y * 2 + zh
    me = seq_of(zl, x, core)
    to_pair = (seq_of(other, x, core), head_me)
    to_right = (seq_of(zl, right, core), head_me)
    to_left = (seq_of(zl, left, core), head_me)
    to_sib = (seq_of(zl, x, 1 - core), head_me)
    to_y = [(me, lax.rem(y + d, RING) * 2 + zh) for d in (1, 2, 3)]

    barrier = pltpu.get_barrier_semaphore()
    neighbours = [to_pair, to_right, to_left, to_sib] + to_y
    for n in neighbours:
        pl.semaphore_signal(barrier, inc=1, device_id=n, device_id_type=MESH)

    def head_columns(h):
        return pl.ds(pl.multiple_of(h * HEAD_DIM, HEAD_DIM), HEAD_DIM)

    own_a, pair_a = zl * 2, other * 2
    staged = [
        (k_ref, own_a, stage.at[0]),
        (k_ref, own_a + 1, stage.at[2]),
        (k_ref, 4, stage.at[4]),
        (k_ref, pair_a, stage.at[6]),
        (k_ref, pair_a + 1, stage.at[8]),
        (q_ref, pair_a, stage.at[10]),
        (q_ref, pair_a + 1, stage.at[11]),
        (v_ref, own_a, raw_values.at[0]),
        (v_ref, own_a + 1, raw_values.at[1]),
        (v_ref, 4, raw_values.at[2]),
        (v_ref, pair_a, raw_values.at[3]),
        (v_ref, pair_a + 1, raw_values.at[4]),
    ]
    stage_copies = [
        pltpu.make_async_copy(src.at[:, head_columns(h)], dst, stage_sem.at[n])
        for n, (src, h, dst) in enumerate(staged)
    ]
    for c in stage_copies:
        c.start()
    half = pl.ds(pl.multiple_of(core * (ROWS // 2), ROWS // 2), ROWS // 2)
    other_half = pl.ds(pl.multiple_of((1 - core) * (ROWS // 2), ROWS // 2), ROWS // 2)

    def panel(y_):
        return pl.ds(pl.multiple_of(y_ * (2 * ROWS), 2 * ROWS), 2 * ROWS)

    local = [
        pltpu.make_async_copy(q_ref.at[:, head_columns(zl * 2)], q_out.at[0], local_sem.at[0]),
        pltpu.make_async_copy(q_ref.at[:, head_columns(zl * 2 + 1)], q_out.at[1], local_sem.at[1]),
        pltpu.make_async_copy(q_ref.at[:, head_columns(4)], q_out.at[2], local_sem.at[2]),
        pltpu.make_async_copy(w_ref.at[half, panel(y)], w_out.at[y, half], local_sem.at[3]),
    ]
    for c in local:
        c.start()
    for c in stage_copies:
        c.wait()

    def turn(n, _):
        piece = lax.div(n, ROW_TILES)
        rows = pl.ds(pl.multiple_of((n - piece * ROW_TILES) * TILE, TILE), TILE)
        stage[2 * piece + 1, rows, :] = raw_values[piece, rows, :].T
        return 0

    lax.fori_loop(0, 5 * ROW_TILES, turn, 0)
    own = pltpu.make_async_copy(stage.at[pl.ds(0, 6)], kv_out.at[me], local_sem.at[4])
    own.start()
    pl.semaphore_wait(barrier, len(neighbours))

    sends = []

    def send(src, dst, recv, target):
        c = pltpu.make_async_remote_copy(
            src_ref=src, dst_ref=dst, send_sem=send_sem.at[len(sends)], recv_sem=recv, device_id=target, device_id_type=MESH
        )
        c.start()
        sends.append(c)

    def arrived(dst, recv, source):
        pltpu.make_async_remote_copy(
            src_ref=dst, dst_ref=dst, send_sem=send_sem.at[0], recv_sem=recv, device_id=source, device_id_type=MESH
        ).wait_recv()

    A, B, H = pl.ds(0, 2), pl.ds(2, 2), pl.ds(4, 2)
    H0, H1 = pl.ds(4, 1), pl.ds(5, 1)
    sib_waits = []

    def to_sibling(origin_zl, origin_x, part):
        n = len(sib_waits)
        block = kv_out.at[seq_of(origin_zl, origin_x, core), part]
        send(block, block, sib_sem.at[n], to_sib)
        sib_waits.append((origin_zl, origin_x, part))

    def pass_on(origin_zl, origin_x, part, recv, target):
        block = kv_out.at[seq_of(origin_zl, origin_x, core), part]
        send(block, block, recv, target)

    def block_of(origin_zl, origin_x, part):
        return kv_out.at[seq_of(origin_zl, origin_x, core), part]

    send(stage.at[pl.ds(6, 2)], kv_out.at[me, A], z_sem.at[0], to_pair)
    send(stage.at[pl.ds(8, 2)], kv_out.at[me, B], z_sem.at[1], to_pair)
    for item, part, at in ((0, H, 4), (1, A, 0), (2, B, 2)):
        send(stage.at[pl.ds(at, 2)], kv_out.at[me, part], x_sem.at[0, item], to_right)
        send(stage.at[pl.ds(at, 2)], kv_out.at[me, part], x_sem.at[1, item], to_left)
    for d in range(3):
        send(w_ref.at[half, panel(lax.rem(y + d + 1, RING))], w_out.at[y, half], w_sem.at[d], to_y[d])
    own.wait()
    to_sibling(zl, x, pl.ds(0, 6))

    for item, part, n in ((3, A, 0), (4, B, 1)):
        arrived(block_of(other, x, part), z_sem.at[n], to_pair)
        pass_on(other, x, part, x_sem.at[0, item], to_right)
        pass_on(other, x, part, x_sem.at[1, item], to_left)
        if n == 0:
            send(stage.at[pl.ds(4, 2)], kv_out.at[me, H], z_sem.at[2], to_pair)
        else:
            send(stage.at[pl.ds(10, 2)], q_out.at[pl.ds(3, 2)], z_sem.at[3], to_pair)
        to_sibling(other, x, part)

    def from_left(item, zl_, part):
        arrived(block_of(zl_, left, part), x_sem.at[0, item], to_left)

    def from_right(item, zl_, part):
        arrived(block_of(zl_, right, part), x_sem.at[1, item], to_right)

    from_left(0, zl, H)
    pass_on(zl, left, H0, far_sem.at[0, 0], to_right)
    pass_on(zl, left, H, z_sem.at[4], to_pair)
    to_sibling(zl, left, H)
    from_right(0, zl, H)
    pass_on(zl, right, H1, far_sem.at[1, 0], to_left)
    pass_on(zl, right, H, z_sem.at[5], to_pair)
    to_sibling(zl, right, H)

    for item, zl_, far in ((1, zl, 1), (3, other, 2)):
        from_left(item, zl_, A)
        pass_on(zl_, left, A, far_sem.at[0, far], to_right)
        to_sibling(zl_, left, A)
        from_right(item, zl_, A)
        to_sibling(zl_, right, A)
        from_right(item + 1, zl_, B)
        pass_on(zl_, right, B, far_sem.at[1, far], to_left)
        to_sibling(zl_, right, B)
        from_left(item + 1, zl_, B)
        to_sibling(zl_, left, B)
        if far == 1:
            arrived(block_of(zl, opposite, H0), far_sem.at[0, 0], to_left)
            arrived(block_of(zl, opposite, H1), far_sem.at[1, 0], to_right)
            pass_on(zl, opposite, H, z_sem.at[6], to_pair)
            to_sibling(zl, opposite, H)
            arrived(block_of(other, x, H), z_sem.at[2], to_pair)
            to_sibling(other, x, H)
    for d in range(3):
        y_ = lax.rem(y + 3 - d, RING)
        arrived(w_out.at[y_, half], w_sem.at[d], to_y[2 - d])
    for d in range(4):
        y_ = lax.rem(y + d, RING)
        if d == 0:
            local[3].wait()
        send(w_out.at[y_, half], w_out.at[y_, half], w_sib_sem.at[d], to_sib)
    for zl_, far in ((zl, 1), (other, 2)):
        arrived(block_of(zl_, opposite, A), far_sem.at[0, far], to_left)
        to_sibling(zl_, opposite, A)
        arrived(block_of(zl_, opposite, B), far_sem.at[1, far], to_right)
        to_sibling(zl_, opposite, B)
    for n, x_ in ((4, left), (5, right), (6, opposite)):
        arrived(block_of(other, x_, H), z_sem.at[n], to_pair)
        to_sibling(other, x_, H)
    arrived(q_out.at[pl.ds(3, 2)], z_sem.at[3], to_pair)
    for d in range(4):
        y_ = lax.rem(y + d, RING)
        arrived(w_out.at[y_, other_half], w_sib_sem.at[d], to_sib)
    for n, (zl_, x_, part) in enumerate(sib_waits):
        arrived(kv_out.at[seq_of(zl_, x_, 1 - core), part], sib_sem.at[n], to_sib)
    for c in sends:
        c.wait_send()
    for c in local[:3]:
        c.wait()


def gather(q, k, v, w):
    bf16 = jnp.bfloat16
    return pl.pallas_call(
        gather_kernel,
        out_shape=[
            jax.ShapeDtypeStruct((SEQ, 6, ROWS, HEAD_DIM), bf16),
            jax.ShapeDtypeStruct((5, ROWS, HEAD_DIM), bf16),
            jax.ShapeDtypeStruct((RING, ROWS, 2 * ROWS), bf16),
        ],
        in_specs=[pl.BlockSpec(memory_space=pl.ANY)] * 4,
        out_specs=[pl.BlockSpec(memory_space=pl.ANY)] * 3,
        scratch_shapes=[
            pltpu.VMEM((12, ROWS, HEAD_DIM), bf16),
            pltpu.VMEM((5, ROWS, HEAD_DIM), bf16),
            pltpu.SemaphoreType.DMA((12,)),
            pltpu.SemaphoreType.DMA((5,)),
            pltpu.SemaphoreType.DMA((64,)),
            pltpu.SemaphoreType.DMA((7,)),
            pltpu.SemaphoreType.DMA((2, 5)),
            pltpu.SemaphoreType.DMA((2, 3)),
            pltpu.SemaphoreType.DMA((24,)),
            pltpu.SemaphoreType.DMA((3,)),
            pltpu.SemaphoreType.DMA((4,)),
        ],
        compiler_params=pltpu.CompilerParams(collective_id=0, has_side_effects=True),
        name="gather_heads",
    )(q, k, v, w)


GROUP = 10
LOG2E = 1.4426950408889634


def attend_kernel(
    mask_ref, q_ref, kv_hbm, o_ref, tiles_ref, counts_ref, kv_ref, s00, s01, s02, s10, s11, s12, acc0, acc1, acc2, sem
):
    scores = ((s00, s01, s02), (s10, s11, s12))
    accs = (acc0, acc1, acc2)
    factor = HEAD_DIM ** -0.5 * LOG2E
    loads = [pltpu.make_async_copy(kv_hbm.at[:, p], kv_ref.at[:, p], sem.at[p]) for p in (0, 2, 4, 1, 3, 5)]
    for c in loads:
        c.start()
    zl, x, core, _, _ = place()
    first = ((zl * RING + x) * 2 + core) * ROW_TILES
    first_pair = (((1 - zl) * RING + x) * 2 + core) * ROW_TILES

    def compact(i, _):
        row = jnp.where(i < ROW_TILES, first + i, first_pair + i - ROW_TILES)
        count = jnp.int32(0)
        for t in range(TILE_COUNT):
            tiles_ref[i, count] = jnp.int32(t)
            count = count + jnp.where(mask_ref[row, t] > 0, 1, 0)
        for t in range(GROUP):
            tiles_ref[i, count + t] = jnp.int32(0)
        counts_ref[i] = count
        return 0

    lax.fori_loop(0, 2 * ROW_TILES, compact, 0)
    for c in loads[:3]:
        c.wait()

    def place_of(row, n):
        t = tiles_ref[row, n]
        owner = lax.shift_right_logical(t * 205, 10)
        return owner, pl.ds(pl.multiple_of((t - owner * ROW_TILES) * TILE, TILE), TILE)

    def run(slots, base, between):
        heads = len(slots)

        def rows_of(i):
            return pl.ds(pl.multiple_of(i * TILE, TILE), TILE)

        def groups_of(i):
            return lax.div(counts_ref[base + i] + (GROUP - 1), GROUP)

        def load_queries(i):
            qs = [q_ref[slot, rows_of(i), :].T for slot in slots]
            zero = jnp.zeros((HEAD_DIM, TILE), jnp.bfloat16)
            both = jnp.concatenate(
                [jnp.concatenate([qs[0], zero], axis=1), jnp.concatenate([zero, qs[1]], axis=1)], axis=0
            )
            return [both] + qs[2:]

        def score(i, side, g, peak, qt):
            count = counts_ref[base + i]
            at = [place_of(base + i, g * GROUP + t) for t in range(GROUP)]
            keys = [jnp.concatenate([kv_ref[o, 2 * h, r, :] for o, r in at], axis=0) for h in range(heads)]
            pair = jnp.dot(jnp.concatenate(keys[:2], axis=1), qt[0], preferred_element_type=jnp.float32)
            s = [pair[:, :TILE], pair[:, TILE:]]
            if heads == 3:
                s.append(jnp.dot(keys[2], qt[1], preferred_element_type=jnp.float32))
            out = []
            for h in range(heads):
                top = peak[h]
                for t in range(GROUP):
                    part = jnp.where(g * GROUP + t < count, s[h][t * TILE : (t + 1) * TILE], MASKED)
                    scores[side][h][g * GROUP + t] = part
                    top = jnp.maximum(top, jnp.max(part.reshape(TILE // 8, 8, TILE), axis=0))
                out.append(top)
            return tuple(out)

        def blend(i, side, g, totals, peak):
            at = [place_of(base + i, g * GROUP + t) for t in range(GROUP)]
            out = []
            for h in range(heads):
                total = totals[h]
                weights = []
                for t in range(GROUP):
                    w = jnp.exp2((scores[side][h][g * GROUP + t] - peak[h]) * factor)
                    total = total + jnp.sum(w.reshape(TILE // 8, 8, TILE), axis=0)
                    weights.append(w.astype(jnp.bfloat16))
                values = jnp.concatenate([kv_ref[o, 2 * h + 1, r, :] for o, r in at], axis=1)
                accs[h][...] += jnp.dot(values, jnp.concatenate(weights, axis=0), preferred_element_type=jnp.float32)
                out.append(total)
            return tuple(out)

        lowest = tuple(jnp.full((8, TILE), MASKED, jnp.float32) for _ in slots)
        zeros = tuple(jnp.zeros((8, TILE), jnp.float32) for _ in slots)

        def row_max(peak):
            return tuple(jnp.max(p, axis=0, keepdims=True) for p in peak)

        def clear():
            for h in range(heads):
                accs[h][...] = jnp.zeros((HEAD_DIM, TILE), jnp.float32)

        def finish(i, totals):
            for h in range(heads):
                o = accs[h][...] * (1.0 / jnp.sum(totals[h], axis=0, keepdims=True))
                o_ref[slots[h], rows_of(i), :] = o.T.astype(o_ref.dtype)

        def step(i, side, peak):
            qt = load_queries(i + 1)
            peak = row_max(peak)
            clear()
            here, there = groups_of(i), groups_of(i + 1)
            both = jnp.minimum(here, there)

            def together(g, carry):
                return score(i + 1, 1 - side, g, carry[0], qt), blend(i, side, g, carry[1], peak)

            above, totals = lax.fori_loop(0, both, together, (lowest, zeros))
            above = lax.fori_loop(both, there, lambda g, c: score(i + 1, 1 - side, g, c, qt), above)
            totals = lax.fori_loop(both, here, lambda g, c: blend(i, side, g, c, peak), totals)
            finish(i, totals)
            return above

        qt = load_queries(0)
        peak = lax.fori_loop(0, groups_of(0), lambda g, c: score(0, 0, g, c, qt), lowest)
        between()
        peak = lax.fori_loop(0, 2, lambda n, c: step(2 * n + 1, 1, step(2 * n, 0, c)), peak)
        peak = row_max(peak)
        clear()
        finish(4, lax.fori_loop(0, groups_of(4), lambda g, c: blend(4, 0, g, c, peak), zeros))

    def values_here():
        for c in loads[3:]:
            c.wait()

    run((0, 1, 2), 0, values_here)
    run((3, 4), ROW_TILES, lambda: None)


def attend(tile_mask, q, kv):
    room = -(-TILE_COUNT // GROUP) * GROUP
    return pl.pallas_call(
        attend_kernel,
        out_shape=jax.ShapeDtypeStruct((5, ROWS, HEAD_DIM), jnp.bfloat16),
        in_specs=[
            pl.BlockSpec(memory_space=pltpu.SMEM),
            pl.BlockSpec(memory_space=pltpu.VMEM),
            pl.BlockSpec(memory_space=pl.ANY),
        ],
        out_specs=pl.BlockSpec(memory_space=pltpu.VMEM),
        scratch_shapes=[
            pltpu.SMEM((2 * ROW_TILES, TILE_COUNT + 16), jnp.int32),
            pltpu.SMEM((2 * ROW_TILES,), jnp.int32),
            pltpu.VMEM((SEQ, 6, ROWS, HEAD_DIM), jnp.bfloat16),
        ]
        + [pltpu.VMEM((room, TILE, TILE), jnp.float32)] * 6
        + [pltpu.VMEM((HEAD_DIM, TILE), jnp.float32)] * 3
        + [pltpu.SemaphoreType.DMA((6,))],
        compiler_params=pltpu.CompilerParams(vmem_limit_bytes=60 << 20),
        name="attend",
    )(tile_mask, q, kv)


def project_kernel(
    o_ref, w_hbm, bias_ref, gate_ref, res_hbm, out_ref,
    w, res_ref, att, mine, sent, got, w_sem, res_sem, put_sem, send_sem, z_sem, y_sem, far_sem, sum_sem,
):
    zl, x, core, y, zh = place()
    other = 1 - zl
    me = (zl * RING + x) * 2 + core
    head_me = y * 2 + zh
    to_pair = ((other * RING + x) * 2 + core, head_me)
    right, left, opposite = lax.rem(y + 1, RING), lax.rem(y + 3, RING), lax.rem(y + 2, RING)
    to_right, to_left = (me, right * 2 + zh), (me, left * 2 + zh)
    to_sum = (me, y * 2 + 1 - zh)

    barrier = pltpu.get_barrier_semaphore()
    neighbours = [to_pair, to_right, to_left, to_sum]
    for n in neighbours:
        pl.semaphore_signal(barrier, inc=1, device_id=n, device_id_type=MESH)
    fetch = pltpu.make_async_copy(w_hbm, w, w_sem)
    fetch.start()
    fetch_res = pltpu.make_async_copy(res_hbm, res_ref, res_sem)
    fetch_res.start()
    puts = []
    for c in range(ROW_TILES):
        rows = pl.ds(c * TILE, TILE)
        puts.append(
            pltpu.make_async_copy(o_ref.at[pl.ds(0, 2), rows], att.at[c, y, pl.ds(2 * zl, 2)], put_sem.at[2 * c])
        )
        puts.append(pltpu.make_async_copy(o_ref.at[2, rows], att.at[c, y, 4], put_sem.at[2 * c + 1]))
    for c in puts:
        c.start()
    pl.semaphore_wait(barrier, len(neighbours))

    sends = []

    def send(src, dst, recv, target):
        c = pltpu.make_async_remote_copy(
            src_ref=src, dst_ref=dst, send_sem=send_sem.at[len(sends)], recv_sem=recv, device_id=target, device_id_type=MESH
        )
        c.start()
        sends.append(c)

    def arrived(dst, recv, source):
        pltpu.make_async_remote_copy(
            src_ref=dst, dst_ref=dst, send_sem=send_sem.at[0], recv_sem=recv, device_id=source, device_id_type=MESH
        ).wait_recv()

    for c in range(ROW_TILES):
        send(
            o_ref.at[pl.ds(3, 2), pl.ds(c * TILE, TILE)], att.at[c, y, pl.ds(2 * zl, 2)], z_sem.at[c], to_pair
        )
    for c in range(ROW_TILES):
        puts[2 * c].wait()
        puts[2 * c + 1].wait()
        arrived(att.at[c, y, pl.ds(2 * other, 2)], z_sem.at[c], to_pair)
        send(att.at[c, y], att.at[c, y], y_sem.at[0, c], to_right)
        send(att.at[c, y], att.at[c, y], y_sem.at[1, c], to_left)

    def halves(c):
        cut = 3 if c % 2 == 0 else 2
        return pl.ds(0, cut), pl.ds(cut, 5 - cut)

    def contract(c):
        first, second = halves(c)
        arrived(att.at[c, opposite, first], far_sem.at[0, c], to_left)
        arrived(att.at[c, opposite, second], far_sem.at[1, c], to_right)
        if c == 0:
            fetch.wait()
        rows = jnp.concatenate([att[c, n, h] for n in range(RING) for h in range(5)], axis=1)
        theirs = w[:, pl.ds(pl.multiple_of((1 - zh) * ROWS, TILE), ROWS)]
        sent[c] = jnp.dot(rows, theirs, preferred_element_type=jnp.float32).astype(jnp.bfloat16)
        send(sent.at[c], got.at[c], sum_sem.at[c], to_sum)
        ours = w[:, pl.ds(pl.multiple_of(zh * ROWS, TILE), ROWS)]
        mine[c] = jnp.dot(rows, ours, preferred_element_type=jnp.float32)

    for c in range(ROW_TILES):
        first, second = halves(c)
        arrived(att.at[c, left], y_sem.at[0, c], to_left)
        send(att.at[c, left, first], att.at[c, left, first], far_sem.at[0, c], to_right)
        arrived(att.at[c, right], y_sem.at[1, c], to_right)
        send(att.at[c, right, second], att.at[c, right, second], far_sem.at[1, c], to_left)
        if c > 0:
            contract(c - 1)
    contract(ROW_TILES - 1)
    fetch_res.wait()
    for c in range(ROW_TILES):
        arrived(got.at[c], sum_sem.at[c], to_sum)
        rows = pl.ds(c * TILE, TILE)
        projected = mine[c] + got[c].astype(jnp.float32)
        out = res_ref[rows, :].astype(jnp.float32) + gate_ref[...] * (projected + bias_ref[...])
        out_ref[rows, :] = out.astype(out_ref.dtype)
    for c in sends:
        c.wait_send()


def project(o, panel, bias, gate, residual):
    bf16 = jnp.bfloat16
    return pl.pallas_call(
        project_kernel,
        out_shape=jax.ShapeDtypeStruct((ROWS, ROWS), bf16),
        in_specs=[
            pl.BlockSpec(memory_space=pltpu.VMEM),
            pl.BlockSpec(memory_space=pl.ANY),
            pl.BlockSpec(memory_space=pltpu.VMEM),
            pl.BlockSpec(memory_space=pltpu.VMEM),
            pl.BlockSpec(memory_space=pl.ANY),
        ],
        out_specs=pl.BlockSpec(memory_space=pltpu.VMEM),
        scratch_shapes=[
            pltpu.VMEM((RING * ROWS, 2 * ROWS), bf16),
            pltpu.VMEM((ROWS, ROWS), bf16),
            pltpu.VMEM((ROW_TILES, RING, 5, TILE, HEAD_DIM), bf16),
            pltpu.VMEM((ROW_TILES, TILE, ROWS), jnp.float32),
            pltpu.VMEM((ROW_TILES, TILE, ROWS), bf16),
            pltpu.VMEM((ROW_TILES, TILE, ROWS), bf16),
            pltpu.SemaphoreType.DMA,
            pltpu.SemaphoreType.DMA,
            pltpu.SemaphoreType.DMA((10,)),
            pltpu.SemaphoreType.DMA((32,)),
            pltpu.SemaphoreType.DMA((5,)),
            pltpu.SemaphoreType.DMA((2, 5)),
            pltpu.SemaphoreType.DMA((2, 5)),
            pltpu.SemaphoreType.DMA((5,)),
        ],
        compiler_params=pltpu.CompilerParams(collective_id=1, has_side_effects=True, vmem_limit_bytes=62 << 20),
        name="project",
    )(o, panel, bias, gate, residual)


LIMIT = 40
STEPS = LIMIT // GROUP
KEYS_OF = pl.ds(0, 1)
VALUES_OF = pl.ds(1, 1)


def whole_kernel(
    owners_ref, starts_ref, bars_ref, q_ref, k_ref, v_ref, w_ref, bias_ref, gate_ref, res_hbm, out_ref,
    stage, raw_values, kva, kvb, kvh, q_own, q_pair, att, back, panel, mine, theirs, sent, got, res_ref,
    s00, s01, s10, s11, acc0, acc1,
    stage_sem, local_sem, send_sem, z_sem, x_sem, far_sem, sib_sem, w_sem, w_sib_sem, ret_sem, y_sem, y_far_sem, sum_sem,
):
    zl, x, core, y, zh = place()
    other = 1 - zl
    right, left, opposite = lax.rem(x + 1, RING), lax.rem(x + 3, RING), lax.rem(x + 2, RING)
    y_right, y_left, y_opposite = lax.rem(y + 1, RING), lax.rem(y + 3, RING), lax.rem(y + 2, RING)

    def seq_of(zl_, x_, core_):
        return (zl_ * RING + x_) * 2 + core_

    head_me = y * 2 + zh
    me = seq_of(zl, x, core)
    to_pair = (seq_of(other, x, core), head_me)
    to_right = (seq_of(zl, right, core), head_me)
    to_left = (seq_of(zl, left, core), head_me)
    to_sib = (seq_of(zl, x, 1 - core), head_me)
    to_y = [(me, lax.rem(y + d, RING) * 2 + zh) for d in (1, 2, 3)]
    to_sum = (me, y * 2 + 1 - zh)

    barrier = pltpu.get_barrier_semaphore()
    neighbours = [to_pair, to_right, to_left, to_sib, to_sum] + to_y
    for n in neighbours:
        pl.semaphore_signal(barrier, inc=1, device_id=n, device_id_type=MESH)

    def head_columns(h):
        return pl.ds(pl.multiple_of(h * HEAD_DIM, HEAD_DIM), HEAD_DIM)

    own_a, pair_a = zl * 2, other * 2
    staged = [
        (k_ref, pair_a, stage.at[6]),
        (v_ref, pair_a, raw_values.at[3]),
        (k_ref, own_a, stage.at[0]),
        (v_ref, own_a, raw_values.at[0]),
        (k_ref, own_a + 1, stage.at[2]),
        (v_ref, own_a + 1, raw_values.at[1]),
        (k_ref, pair_a + 1, stage.at[8]),
        (v_ref, pair_a + 1, raw_values.at[4]),
        (k_ref, 4, stage.at[4]),
        (v_ref, 4, raw_values.at[2]),
        (q_ref, pair_a, stage.at[10]),
        (q_ref, pair_a + 1, stage.at[11]),
    ]
    stage_copies = [
        pltpu.make_async_copy(src.at[:, :, head_columns(h)], dst, stage_sem.at[n])
        for n, (src, h, dst) in enumerate(staged)
    ]
    for c in stage_copies:
        c.start()
    half = pl.ds(pl.multiple_of(core * (ROWS // 2), ROWS // 2), ROWS // 2)
    other_half = pl.ds(pl.multiple_of((1 - core) * (ROWS // 2), ROWS // 2), ROWS // 2)

    def columns_of(y_):
        return pl.ds(pl.multiple_of(y_ * (2 * ROWS), 2 * ROWS), 2 * ROWS)

    local = [
        pltpu.make_async_copy(q_ref.at[:, :, head_columns(own_a)], q_own.at[0], local_sem.at[0]),
        pltpu.make_async_copy(q_ref.at[:, :, head_columns(own_a + 1)], q_own.at[1], local_sem.at[1]),
        pltpu.make_async_copy(q_ref.at[:, :, head_columns(4)], q_own.at[2], local_sem.at[2]),
        pltpu.make_async_copy(w_ref.at[half, columns_of(y)], panel.at[y, half], local_sem.at[3]),
        pltpu.make_async_copy(res_hbm, res_ref, local_sem.at[4]),
    ]
    for c in local:
        c.start()

    def turn(piece):
        def one(r, _):
            stage[2 * piece + 1, r] = raw_values[piece, r].T
            return 0

        lax.fori_loop(0, ROW_TILES, one, 0)

    for c in stage_copies[:4]:
        c.wait()
    turn(0)
    turn(3)
    own = [
        pltpu.make_async_copy(stage.at[pl.ds(2 * n, 2)], kv.at[me], local_sem.at[5 + n])
        for n, kv in enumerate((kva, kvb, kvh))
    ]
    own[0].start()
    pl.semaphore_wait(barrier, len(neighbours))

    sends = []

    def send(src, dst, recv, target):
        c = pltpu.make_async_remote_copy(
            src_ref=src, dst_ref=dst, send_sem=send_sem.at[len(sends)], recv_sem=recv, device_id=target, device_id_type=MESH
        )
        c.start()
        sends.append(c)

    def arrived(dst, recv, source):
        pltpu.make_async_remote_copy(
            src_ref=dst, dst_ref=dst, send_sem=send_sem.at[0], recv_sem=recv, device_id=source, device_id_type=MESH
        ).wait_recv()

    both_parts = pl.ds(0, 2)
    k_part, v_part = KEYS_OF, VALUES_OF
    sib_waits = {"a": [], "b": [], "h": []}
    sib_count = [0]

    def block(kv, zl_, x_, part=both_parts):
        return kv.at[seq_of(zl_, x_, core), part]

    def to_sibling(name, kv, zl_, x_, part=both_parts):
        n = sib_count[0]
        sib_count[0] += 1
        send(block(kv, zl_, x_, part), block(kv, zl_, x_, part), sib_sem.at[n], to_sib)
        sib_waits[name].append((n, kv, zl_, x_, part))

    def from_sibling(name):
        for n, kv, zl_, x_, part in sib_waits[name]:
            arrived(kv.at[seq_of(zl_, x_, 1 - core), part], sib_sem.at[n], to_sib)

    def ring_send(item, kv, zl_, x_, part=both_parts):
        send(block(kv, zl_, x_, part), block(kv, zl_, x_, part), x_sem.at[0, item], to_right)
        send(block(kv, zl_, x_, part), block(kv, zl_, x_, part), x_sem.at[1, item], to_left)

    def ring_pass(item, name, kv, zl_):
        arrived(block(kv, zl_, left), x_sem.at[0, item], to_left)
        send(block(kv, zl_, left, k_part), block(kv, zl_, left, k_part), far_sem.at[0, item], to_right)
        arrived(block(kv, zl_, right), x_sem.at[1, item], to_right)
        send(block(kv, zl_, right, v_part), block(kv, zl_, right, v_part), far_sem.at[1, item], to_left)
        to_sibling(name, kv, zl_, left)
        to_sibling(name, kv, zl_, right)

    def ring_far(item, name, kv, zl_):
        arrived(block(kv, zl_, opposite, k_part), far_sem.at[0, item], to_left)
        arrived(block(kv, zl_, opposite, v_part), far_sem.at[1, item], to_right)
        to_sibling(name, kv, zl_, opposite)

    A0, A1, B0, B1, H0, V1 = range(6)
    send(stage.at[pl.ds(6, 2)], kva.at[me], z_sem.at[0], to_pair)
    send(stage.at[pl.ds(0, 2)], kva.at[me], x_sem.at[0, A0], to_right)
    send(stage.at[pl.ds(0, 2)], kva.at[me], x_sem.at[1, A0], to_left)
    send(stage.at[pl.ds(0, 2)], kva.at[me], sib_sem.at[0], to_sib)
    sib_count[0] = 1
    sib_waits["a"].append((0, kva, zl, x, both_parts))
    for d in range(3):
        send(w_ref.at[half, columns_of(lax.rem(y + d + 1, RING))], panel.at[y, half], w_sem.at[d], to_y[d])
    for c in stage_copies[4:]:
        c.wait()
    turn(1)
    turn(4)
    turn(2)
    for c in own[1:]:
        c.start()
    for c in own:
        c.wait()
    arrived(block(kva, other, x), z_sem.at[0], to_pair)
    ring_send(A1, kva, other, x)
    send(stage.at[pl.ds(8, 2)], kvb.at[me], z_sem.at[1], to_pair)
    send(stage.at[pl.ds(10, 2)], q_pair, z_sem.at[2], to_pair)
    to_sibling("a", kva, other, x)
    ring_pass(A0, "a", kva, zl)
    ring_pass(A1, "a", kva, other)
    ring_send(B0, kvb, zl, x)
    to_sibling("b", kvb, zl, x)
    arrived(block(kvb, other, x), z_sem.at[1], to_pair)
    ring_send(B1, kvb, other, x)
    to_sibling("b", kvb, other, x)
    send(stage.at[pl.ds(4, 2)], kvh.at[me], z_sem.at[3], to_pair)
    ring_far(A0, "a", kva, zl)
    ring_far(A1, "a", kva, other)
    for c in local[:3]:
        c.wait()
    arrived(q_pair, z_sem.at[2], to_pair)
    from_sibling("a")

    scores = ((s00, s01), (s10, s11))
    accs = (acc0, acc1)
    factor = HEAD_DIM ** -0.5 * LOG2E
    lowest = jnp.full((8, TILE), MASKED, jnp.float32)
    nothing = jnp.zeros((8, TILE), jnp.float32)

    def place_of(row, n):
        return owners_ref[row, n], starts_ref[row, n]

    def score(kv, rows, side, g, peaks, queries):
        out = []
        for u, row in enumerate(rows):
            at = [place_of(row, g * GROUP + t) for t in range(GROUP)]
            keys = jnp.concatenate([kv[o, 0, r] for o, r in at], axis=0)
            s = jnp.dot(keys, queries[u], preferred_element_type=jnp.float32)
            top = peaks[u]
            for t in range(GROUP):
                part = s[t * TILE : (t + 1) * TILE] + bars_ref[row, g * GROUP + t]
                scores[side][u][g * GROUP + t] = part
                top = jnp.maximum(top, jnp.max(part.reshape(TILE // 8, 8, TILE), axis=0))
            out.append(top)
        return tuple(out)

    def blend(kv, rows, side, g, totals, peaks):
        out = []
        for u, row in enumerate(rows):
            total = totals[u]
            weights = []
            for t in range(GROUP):
                w = jnp.exp2((scores[side][u][g * GROUP + t] - peaks[u]) * factor)
                total = total + jnp.sum(w.reshape(TILE // 8, 8, TILE), axis=0)
                weights.append(w.astype(jnp.bfloat16))
            at = [place_of(row, g * GROUP + t) for t in range(GROUP)]
            values = jnp.concatenate([kv[o, 1, r] for o, r in at], axis=1)
            accs[u][...] += jnp.dot(values, jnp.concatenate(weights, axis=0), preferred_element_type=jnp.float32)
            out.append(total)
        return tuple(out)

    def attention(kv, plan, tasks):
        peaks = None
        for i in range(-1, len(plan)):
            here = plan[i] if i >= 0 else []
            there = plan[i + 1] if i + 1 < len(plan) else []
            side = i % 2
            rows, rows_next = [u[0] for u in here], [u[0] for u in there]
            queries = [q_of[j, r].T for _, (q_of, j, r), _ in there]
            tops = [jnp.max(p, axis=0, keepdims=True) for p in peaks] if here else []
            for u in range(len(here)):
                accs[u][...] = jnp.zeros((HEAD_DIM, TILE), jnp.float32)

            def body(g, carry):
                new_peaks = score(kv, rows_next, 1 - side, g, carry[0], queries)
                return new_peaks, blend(kv, rows, side, g, carry[1], tops)

            peaks, totals = lax.fori_loop(0, STEPS, body, ((lowest,) * len(there), (nothing,) * len(here)))
            for u, (_, _, (dst, r)) in enumerate(here):
                o = accs[u][...] * (1.0 / jnp.sum(totals[u], axis=0, keepdims=True))
                dst[r, :] = o.T.astype(jnp.bfloat16)
            if i in tasks:
                tasks[i]()

    def tile_rows(i):
        return pl.ds(i * TILE, TILE)

    def plan_of(j):
        return [
            [
                (i, (q_own, j, i), (att.at[y, own_a + j], tile_rows(i))),
                (ROW_TILES + i, (q_pair, j, i), (back.at[j], tile_rows(i))),
            ]
            for i in range(ROW_TILES)
        ]

    positions = [own_a, own_a + 1, pair_a, pair_a + 1, 4]

    row_groups = {0: [(0, 640)], 1: [(0, 384), (384, 256)], 2: [(0, 640)], 3: [(0, 384), (384, 256)]}
    row_groups[4] = [(0, 256), (256, 256), (512, 128)]
    first_sem = {0: 0, 1: 1, 2: 3, 3: 4, 4: 6}

    def y_block(n, y_, start, count):
        return att.at[y_, positions[n], pl.ds(start, count)]

    def y_send(n, g=0):
        part = y_block(n, y, *row_groups[n][g])
        send(part, part, y_sem.at[0, first_sem[n] + g], to_y[0])
        send(part, part, y_sem.at[1, first_sem[n] + g], to_y[2])

    def y_pass(n, g=0):
        start, count = row_groups[n][g]
        arrived(y_block(n, y_left, start, count), y_sem.at[0, first_sem[n] + g], to_y[2])
        part = y_block(n, y_left, start, count // 2)
        send(part, part, y_far_sem.at[0, first_sem[n] + g], to_y[0])
        arrived(y_block(n, y_right, start, count), y_sem.at[1, first_sem[n] + g], to_y[0])
        part = y_block(n, y_right, start + count // 2, count // 2)
        send(part, part, y_far_sem.at[1, first_sem[n] + g], to_y[2])

    def y_far(n, g=0):
        start, count = row_groups[n][g]
        arrived(y_block(n, y_opposite, start, count // 2), y_far_sem.at[0, first_sem[n] + g], to_y[2])
        arrived(y_block(n, y_opposite, start + count // 2, count // 2), y_far_sem.at[1, first_sem[n] + g], to_y[0])

    def give_back(j, g=0):
        rows = pl.ds(*row_groups[2 + j][g])
        send(back.at[j, rows], att.at[y, own_a + j, rows], ret_sem.at[j + g], to_pair)

    def given_back(j, g=0):
        rows = pl.ds(*row_groups[2 + j][g])
        arrived(att.at[y, pair_a + j, rows], ret_sem.at[j + g], to_pair)
        y_send(2 + j, g)

    ours_columns = pl.ds(pl.multiple_of(zh * ROWS, TILE), ROWS)
    theirs_columns = pl.ds(pl.multiple_of((1 - zh) * ROWS, TILE), ROWS)

    def product(units, rows, columns):
        lhs = jnp.concatenate([att[n, positions[u], rows, :] for u in units for n in range(RING)], axis=1)
        rhs = jnp.concatenate([panel[n, head_columns(positions[u]), columns] for u in units for n in range(RING)], axis=0)
        return jnp.dot(lhs, rhs, preferred_element_type=jnp.float32)

    def contract(units, first, parts):
        def one(c, _):
            rows = pl.ds(pl.multiple_of(c * TILE, TILE), TILE)
            for total, columns in parts:
                p = product(units, rows, columns)
                total[rows, :] = p if first else total[rows, :] + p
            return 0

        lax.fori_loop(0, ROW_TILES, one, 0)

    def panel_here():
        for d in range(3):
            arrived(panel.at[lax.rem(y + 3 - d, RING), half], w_sem.at[d], to_y[2 - d])
        local[3].wait()
        for d in range(RING):
            y_ = lax.rem(y + d, RING)
            send(panel.at[y_, half], panel.at[y_, half], w_sib_sem.at[d], to_sib)

    def after_a1():
        ring_pass(B0, "b", kvb, zl)

    def after_a3():
        ring_pass(B1, "b", kvb, other)
        ring_send(H0, kvh, zl, x)
        to_sibling("h", kvh, zl, x)

    attention(kva, plan_of(0), {1: after_a1, 3: after_a3})
    give_back(0)
    y_send(0)
    arrived(block(kvh, other, x), z_sem.at[3], to_pair)
    ring_send(V1, kvh, other, x, v_part)
    to_sibling("h", kvh, other, x)
    ring_far(B0, "b", kvb, zl)
    ring_far(B1, "b", kvb, other)
    panel_here()
    from_sibling("b")

    v_first, v_second = pl.ds(0, 3), pl.ds(3, 2)

    def v_block(x_, rows=None):
        at = kvh.at[seq_of(other, x_, core), 1]
        return at if rows is None else at.at[rows]

    def after_b1():
        given_back(0)
        ring_pass(H0, "h", kvh, zl)
        for n, x_ in ((4, left), (5, right)):
            send(block(kvh, zl, x_, k_part), block(kvh, zl, x_, k_part), z_sem.at[n], to_pair)
        y_pass(0)

    def after_b3():
        arrived(block(kvh, other, left, v_part), x_sem.at[0, V1], to_left)
        send(v_block(left, v_first), v_block(left, v_first), far_sem.at[0, V1], to_right)
        arrived(block(kvh, other, right, v_part), x_sem.at[1, V1], to_right)
        send(v_block(right, v_second), v_block(right, v_second), far_sem.at[1, V1], to_left)
        to_sibling("h", kvh, other, left, v_part)
        to_sibling("h", kvh, other, right, v_part)
        y_pass(2)

    def after_b2():
        give_back(1, 0)
        y_send(1, 0)

    attention(kvb, plan_of(1), {1: after_b1, 2: after_b2, 3: after_b3})
    give_back(1, 1)
    y_send(1, 1)
    ring_far(H0, "h", kvh, zl)
    send(block(kvh, zl, opposite, k_part), block(kvh, zl, opposite, k_part), z_sem.at[6], to_pair)
    arrived(v_block(opposite, v_first), far_sem.at[0, V1], to_left)
    arrived(v_block(opposite, v_second), far_sem.at[1, V1], to_right)
    to_sibling("h", kvh, other, opposite, v_part)
    for n, x_ in ((4, left), (5, right)):
        arrived(block(kvh, other, x_, k_part), z_sem.at[n], to_pair)
        to_sibling("h", kvh, other, x_, k_part)
    given_back(1, 0)
    y_pass(1, 0)
    y_far(0)
    y_far(2)
    for d in range(RING):
        arrived(panel.at[lax.rem(y + d, RING), other_half], w_sib_sem.at[d], to_sib)
    contract((0, 2), True, ((theirs, theirs_columns), (mine, ours_columns)))
    given_back(1, 1)
    arrived(block(kvh, other, opposite, k_part), z_sem.at[6], to_pair)
    to_sibling("h", kvh, other, opposite, k_part)
    y_pass(1, 1)
    y_pass(3, 0)
    from_sibling("h")

    units = [
        (i, (q_own, 2, i), (att.at[y, 4], tile_rows(i))) for i in range(ROW_TILES)
    ]

    def after_h0():
        y_send(4, 0)
        y_pass(3, 1)

    def after_h1():
        y_send(4, 1)
        y_pass(4, 0)

    attention(kvh, [units[0:2], units[2:4], units[4:5]], {0: after_h0, 1: after_h1, 2: lambda: y_send(4, 2)})
    y_pass(4, 1)
    for n in (1, 3):
        for g in range(2):
            y_far(n, g)
    for g, tiles in enumerate(((0, 1), (2, 3), (4,))):
        y_far(4, g)
        for c in tiles:
            rows = tile_rows(c)
            sent[rows, :] = (theirs[rows, :] + product((1, 3, 4), rows, theirs_columns)).astype(sent.dtype)
            send(sent.at[rows], got.at[rows], sum_sem.at[c], to_sum)
        if g == 0:
            y_pass(4, 2)
    local[4].wait()
    contract((1, 3, 4), False, ((mine, ours_columns),))
    for c in range(ROW_TILES):
        rows = tile_rows(c)
        arrived(got.at[rows], sum_sem.at[c], to_sum)
        projected = mine[rows, :] + got[rows, :].astype(jnp.float32)
        out = res_ref[rows, :].astype(jnp.float32) + gate_ref[...][None, :] * (projected + bias_ref[...][None, :])
        out_ref[rows, :] = out.astype(out_ref.dtype)
    for c in sends:
        c.wait_send()


def whole(owners, starts, bars, q, k, v, w, bias, gate, residual):
    bf16, f32 = jnp.bfloat16, jnp.float32

    def by_tile(array):
        return array.reshape(ROW_TILES, TILE, ROWS)

    smem, vmem, anywhere = (
        pl.BlockSpec(memory_space=pltpu.SMEM),
        pl.BlockSpec(memory_space=pltpu.VMEM),
        pl.BlockSpec(memory_space=pl.ANY),
    )
    dma = pltpu.SemaphoreType.DMA
    return pl.pallas_call(
        whole_kernel,
        out_shape=jax.ShapeDtypeStruct((ROWS, ROWS), bf16),
        in_specs=[smem, smem, smem, anywhere, anywhere, anywhere, anywhere, vmem, vmem, anywhere],
        out_specs=vmem,
        scratch_shapes=[
            pltpu.VMEM((12, ROW_TILES, TILE, HEAD_DIM), bf16),
            pltpu.VMEM((5, ROW_TILES, TILE, HEAD_DIM), bf16),
            pltpu.VMEM((SEQ, 2, ROW_TILES, TILE, HEAD_DIM), bf16),
            pltpu.VMEM((SEQ, 2, ROW_TILES, TILE, HEAD_DIM), bf16),
            pltpu.VMEM((SEQ, 2, ROW_TILES, TILE, HEAD_DIM), bf16),
            pltpu.VMEM((3, ROW_TILES, TILE, HEAD_DIM), bf16),
            pltpu.VMEM((2, ROW_TILES, TILE, HEAD_DIM), bf16),
            pltpu.VMEM((RING, 5, ROWS, HEAD_DIM), bf16),
            pltpu.VMEM((2, ROWS, HEAD_DIM), bf16),
            pltpu.VMEM((RING, ROWS, 2 * ROWS), bf16),
            pltpu.VMEM((ROWS, ROWS), f32),
            pltpu.VMEM((ROWS, ROWS), f32),
            pltpu.VMEM((ROWS, ROWS), bf16),
            pltpu.VMEM((ROWS, ROWS), bf16),
            pltpu.VMEM((ROWS, ROWS), bf16),
        ]
        + [pltpu.VMEM((LIMIT, TILE, TILE), f32)] * 4
        + [pltpu.VMEM((HEAD_DIM, TILE), f32)] * 2
        + [
            dma((12,)), dma((8,)), dma((128,)), dma((7,)), dma((2, 6)), dma((2, 6)), dma((28,)), dma((3,)), dma((4,)),
            dma((3,)), dma((2, 9)), dma((2, 9)), dma((5,)),
        ],
        compiler_params=pltpu.CompilerParams(collective_id=2, has_side_effects=True, vmem_limit_bytes=62 << 20),
        name="whole",
    )(owners, starts, bars, by_tile(q), by_tile(k), by_tile(v), w, bias, gate, residual)


def tile_lists(tile_mask):
    zl, x, core, _, _ = place()
    own = (zl * RING + x) * 2 + core
    pair = ((1 - zl) * RING + x) * 2 + core
    rows = jnp.concatenate(
        [lax.dynamic_slice_in_dim(tile_mask, first * ROW_TILES, ROW_TILES, 0) for first in (own, pair)], axis=0
    )
    allowed = rows > 0
    at = jnp.arange(TILE_COUNT, dtype=jnp.int32)
    before = jnp.sum(jnp.where(allowed[:, None, :] & (at[None, None, :] < at[None, :, None]), 1, 0), axis=2)
    hit = allowed[:, None, :] & (before[:, None, :] == at[None, :LIMIT, None])
    tiles = jnp.sum(jnp.where(hit, at[None, None, :], 0), axis=2)
    tiles = tiles.astype(jnp.int32)
    bars = jnp.where(at[None, :LIMIT] < jnp.sum(allowed, axis=1)[:, None], 0.0, MASKED).astype(jnp.float32)
    return tiles // ROW_TILES, tiles % ROW_TILES, bars


def local(queries, key_states, value_states, tile_mask, out_weight, out_bias, residual, gate_scale):
    bias, gate = out_bias, gate_scale

    def by_lists(_):
        owners, starts, bars = tile_lists(tile_mask)
        return whole(owners, starts, bars, queries, key_states, value_states, out_weight, bias, gate, residual)

    def in_parts(_):
        kv, q, panel = gather(queries, key_states, value_states, out_weight)
        o = attend(tile_mask, q, kv)
        return project(o, panel.reshape(RING * ROWS, 2 * ROWS), bias[None, :], gate[None, :], residual)

    longest = jnp.max(jnp.sum((tile_mask > 0).astype(jnp.int32), axis=1))
    return lax.cond(longest <= LIMIT, by_lists, in_parts, 0)


def solution(mesh):
    return jax.shard_map(
        local,
        mesh=mesh,
        in_specs=(
            P("seq", "head"),
            P("seq", "head"),
            P("seq", "head"),
            P(),
            P("head", None),
            P("head"),
            P("seq", "head"),
            P("head"),
        ),
        out_specs=P("seq", "head"),
        check_vma=False,
    )
```

```python
import functools

import jax
import jax.numpy as jnp
from jax import lax
from jax.experimental import pallas as pl
from jax.experimental.pallas import tpu as pltpu
from jax.sharding import PartitionSpec as P

HEAD_DIM = 128
TILE = 128
ROWS = 640
ROW_TILES = ROWS // TILE
SEQ = 16
RING = 4
TILE_COUNT = 80
MESH = pl.DeviceIdType.MESH
MASKED = -1e30


def place():
    s = lax.axis_index("seq")
    h = lax.axis_index("head")
    return lax.div(s, 8), lax.rem(lax.div(s, 2), 4), lax.rem(s, 2), lax.div(h, 2), lax.rem(h, 2)


def gather_kernel(
    q_ref, k_ref, v_ref, w_ref, kv_out, q_out, w_out,
    stage, raw_values, stage_sem, local_sem, send_sem, z_sem, x_sem, far_sem, sib_sem, w_sem, w_sib_sem,
):
    zl, x, core, y, zh = place()
    other = 1 - zl
    right, left = lax.rem(x + 1, RING), lax.rem(x + 3, RING)
    opposite = lax.rem(x + 2, RING)

    def seq_of(zl_, x_, core_):
        return (zl_ * RING + x_) * 2 + core_

    head_me = y * 2 + zh
    me = seq_of(zl, x, core)
    to_pair = (seq_of(other, x, core), head_me)
    to_right = (seq_of(zl, right, core), head_me)
    to_left = (seq_of(zl, left, core), head_me)
    to_sib = (seq_of(zl, x, 1 - core), head_me)
    to_y = [(me, lax.rem(y + d, RING) * 2 + zh) for d in (1, 2, 3)]

    barrier = pltpu.get_barrier_semaphore()
    neighbours = [to_pair, to_right, to_left, to_sib] + to_y
    for n in neighbours:
        pl.semaphore_signal(barrier, inc=1, device_id=n, device_id_type=MESH)

    def head_columns(h):
        return pl.ds(pl.multiple_of(h * HEAD_DIM, HEAD_DIM), HEAD_DIM)

    own_a, pair_a = zl * 2, other * 2
    staged = [
        (k_ref, own_a, stage.at[0]),
        (k_ref, own_a + 1, stage.at[2]),
        (k_ref, 4, stage.at[4]),
        (k_ref, pair_a, stage.at[6]),
        (k_ref, pair_a + 1, stage.at[8]),
        (q_ref, pair_a, stage.at[10]),
        (q_ref, pair_a + 1, stage.at[11]),
        (v_ref, own_a, raw_values.at[0]),
        (v_ref, own_a + 1, raw_values.at[1]),
        (v_ref, 4, raw_values.at[2]),
        (v_ref, pair_a, raw_values.at[3]),
        (v_ref, pair_a + 1, raw_values.at[4]),
    ]
    stage_copies = [
        pltpu.make_async_copy(src.at[:, head_columns(h)], dst, stage_sem.at[n])
        for n, (src, h, dst) in enumerate(staged)
    ]
    for c in stage_copies:
        c.start()
    half = pl.ds(pl.multiple_of(core * (ROWS // 2), ROWS // 2), ROWS // 2)
    other_half = pl.ds(pl.multiple_of((1 - core) * (ROWS // 2), ROWS // 2), ROWS // 2)

    def panel(y_):
        return pl.ds(pl.multiple_of(y_ * (2 * ROWS), 2 * ROWS), 2 * ROWS)

    local = [
        pltpu.make_async_copy(q_ref.at[:, head_columns(zl * 2)], q_out.at[0], local_sem.at[0]),
        pltpu.make_async_copy(q_ref.at[:, head_columns(zl * 2 + 1)], q_out.at[1], local_sem.at[1]),
        pltpu.make_async_copy(q_ref.at[:, head_columns(4)], q_out.at[2], local_sem.at[2]),
        pltpu.make_async_copy(w_ref.at[half, panel(y)], w_out.at[y, half], local_sem.at[3]),
    ]
    for c in local:
        c.start()
    for c in stage_copies:
        c.wait()

    def turn(n, _):
        piece = lax.div(n, ROW_TILES)
        rows = pl.ds(pl.multiple_of((n - piece * ROW_TILES) * TILE, TILE), TILE)
        stage[2 * piece + 1, rows, :] = raw_values[piece, rows, :].T
        return 0

    lax.fori_loop(0, 5 * ROW_TILES, turn, 0)
    own = pltpu.make_async_copy(stage.at[pl.ds(0, 6)], kv_out.at[me], local_sem.at[4])
    own.start()
    pl.semaphore_wait(barrier, len(neighbours))

    sends = []

    def send(src, dst, recv, target):
        c = pltpu.make_async_remote_copy(
            src_ref=src, dst_ref=dst, send_sem=send_sem.at[len(sends)], recv_sem=recv, device_id=target, device_id_type=MESH
        )
        c.start()
        sends.append(c)

    def arrived(dst, recv, source):
        pltpu.make_async_remote_copy(
            src_ref=dst, dst_ref=dst, send_sem=send_sem.at[0], recv_sem=recv, device_id=source, device_id_type=MESH
        ).wait_recv()

    A, B, H = pl.ds(0, 2), pl.ds(2, 2), pl.ds(4, 2)
    H0, H1 = pl.ds(4, 1), pl.ds(5, 1)
    sib_waits = []

    def to_sibling(origin_zl, origin_x, part):
        n = len(sib_waits)
        block = kv_out.at[seq_of(origin_zl, origin_x, core), part]
        send(block, block, sib_sem.at[n], to_sib)
        sib_waits.append((origin_zl, origin_x, part))

    def pass_on(origin_zl, origin_x, part, recv, target):
        block = kv_out.at[seq_of(origin_zl, origin_x, core), part]
        send(block, block, recv, target)

    def block_of(origin_zl, origin_x, part):
        return kv_out.at[seq_of(origin_zl, origin_x, core), part]

    send(stage.at[pl.ds(6, 2)], kv_out.at[me, A], z_sem.at[0], to_pair)
    send(stage.at[pl.ds(8, 2)], kv_out.at[me, B], z_sem.at[1], to_pair)
    for item, part, at in ((0, H, 4), (1, A, 0), (2, B, 2)):
        send(stage.at[pl.ds(at, 2)], kv_out.at[me, part], x_sem.at[0, item], to_right)
        send(stage.at[pl.ds(at, 2)], kv_out.at[me, part], x_sem.at[1, item], to_left)
    for d in range(3):
        send(w_ref.at[half, panel(lax.rem(y + d + 1, RING))], w_out.at[y, half], w_sem.at[d], to_y[d])
    own.wait()
    to_sibling(zl, x, pl.ds(0, 6))

    for item, part, n in ((3, A, 0), (4, B, 1)):
        arrived(block_of(other, x, part), z_sem.at[n], to_pair)
        pass_on(other, x, part, x_sem.at[0, item], to_right)
        pass_on(other, x, part, x_sem.at[1, item], to_left)
        if n == 0:
            send(stage.at[pl.ds(4, 2)], kv_out.at[me, H], z_sem.at[2], to_pair)
        else:
            send(stage.at[pl.ds(10, 2)], q_out.at[pl.ds(3, 2)], z_sem.at[3], to_pair)
        to_sibling(other, x, part)

    def from_left(item, zl_, part):
        arrived(block_of(zl_, left, part), x_sem.at[0, item], to_left)

    def from_right(item, zl_, part):
        arrived(block_of(zl_, right, part), x_sem.at[1, item], to_right)

    from_left(0, zl, H)
    pass_on(zl, left, H0, far_sem.at[0, 0], to_right)
    pass_on(zl, left, H, z_sem.at[4], to_pair)
    to_sibling(zl, left, H)
    from_right(0, zl, H)
    pass_on(zl, right, H1, far_sem.at[1, 0], to_left)
    pass_on(zl, right, H, z_sem.at[5], to_pair)
    to_sibling(zl, right, H)

    for item, zl_, far in ((1, zl, 1), (3, other, 2)):
        from_left(item, zl_, A)
        pass_on(zl_, left, A, far_sem.at[0, far], to_right)
        to_sibling(zl_, left, A)
        from_right(item, zl_, A)
        to_sibling(zl_, right, A)
        from_right(item + 1, zl_, B)
        pass_on(zl_, right, B, far_sem.at[1, far], to_left)
        to_sibling(zl_, right, B)
        from_left(item + 1, zl_, B)
        to_sibling(zl_, left, B)
        if far == 1:
            arrived(block_of(zl, opposite, H0), far_sem.at[0, 0], to_left)
            arrived(block_of(zl, opposite, H1), far_sem.at[1, 0], to_right)
            pass_on(zl, opposite, H, z_sem.at[6], to_pair)
            to_sibling(zl, opposite, H)
            arrived(block_of(other, x, H), z_sem.at[2], to_pair)
            to_sibling(other, x, H)
    for d in range(3):
        y_ = lax.rem(y + 3 - d, RING)
        arrived(w_out.at[y_, half], w_sem.at[d], to_y[2 - d])
    for d in range(4):
        y_ = lax.rem(y + d, RING)
        if d == 0:
            local[3].wait()
        send(w_out.at[y_, half], w_out.at[y_, half], w_sib_sem.at[d], to_sib)
    for zl_, far in ((zl, 1), (other, 2)):
        arrived(block_of(zl_, opposite, A), far_sem.at[0, far], to_left)
        to_sibling(zl_, opposite, A)
        arrived(block_of(zl_, opposite, B), far_sem.at[1, far], to_right)
        to_sibling(zl_, opposite, B)
    for n, x_ in ((4, left), (5, right), (6, opposite)):
        arrived(block_of(other, x_, H), z_sem.at[n], to_pair)
        to_sibling(other, x_, H)
    arrived(q_out.at[pl.ds(3, 2)], z_sem.at[3], to_pair)
    for d in range(4):
        y_ = lax.rem(y + d, RING)
        arrived(w_out.at[y_, other_half], w_sib_sem.at[d], to_sib)
    for n, (zl_, x_, part) in enumerate(sib_waits):
        arrived(kv_out.at[seq_of(zl_, x_, 1 - core), part], sib_sem.at[n], to_sib)
    for c in sends:
        c.wait_send()
    for c in local[:3]:
        c.wait()


def gather(q, k, v, w):
    bf16 = jnp.bfloat16
    return pl.pallas_call(
        gather_kernel,
        out_shape=[
            jax.ShapeDtypeStruct((SEQ, 6, ROWS, HEAD_DIM), bf16),
            jax.ShapeDtypeStruct((5, ROWS, HEAD_DIM), bf16),
            jax.ShapeDtypeStruct((RING, ROWS, 2 * ROWS), bf16),
        ],
        in_specs=[pl.BlockSpec(memory_space=pl.ANY)] * 4,
        out_specs=[pl.BlockSpec(memory_space=pl.ANY)] * 3,
        scratch_shapes=[
            pltpu.VMEM((12, ROWS, HEAD_DIM), bf16),
            pltpu.VMEM((5, ROWS, HEAD_DIM), bf16),
            pltpu.SemaphoreType.DMA((12,)),
            pltpu.SemaphoreType.DMA((5,)),
            pltpu.SemaphoreType.DMA((64,)),
            pltpu.SemaphoreType.DMA((7,)),
            pltpu.SemaphoreType.DMA((2, 5)),
            pltpu.SemaphoreType.DMA((2, 3)),
            pltpu.SemaphoreType.DMA((24,)),
            pltpu.SemaphoreType.DMA((3,)),
            pltpu.SemaphoreType.DMA((4,)),
        ],
        compiler_params=pltpu.CompilerParams(collective_id=0, has_side_effects=True),
        name="gather_heads",
    )(q, k, v, w)


GROUP = 10
LOG2E = 1.4426950408889634


def attend_kernel(
    mask_ref, q_ref, kv_hbm, o_ref, tiles_ref, counts_ref, kv_ref, s00, s01, s02, s10, s11, s12, acc0, acc1, acc2, sem
):
    scores = ((s00, s01, s02), (s10, s11, s12))
    accs = (acc0, acc1, acc2)
    factor = HEAD_DIM ** -0.5 * LOG2E
    loads = [pltpu.make_async_copy(kv_hbm.at[:, p], kv_ref.at[:, p], sem.at[p]) for p in (0, 2, 4, 1, 3, 5)]
    for c in loads:
        c.start()
    zl, x, core, _, _ = place()
    first = ((zl * RING + x) * 2 + core) * ROW_TILES
    first_pair = (((1 - zl) * RING + x) * 2 + core) * ROW_TILES

    def compact(i, _):
        row = jnp.where(i < ROW_TILES, first + i, first_pair + i - ROW_TILES)
        count = jnp.int32(0)
        for t in range(TILE_COUNT):
            tiles_ref[i, count] = jnp.int32(t)
            count = count + jnp.where(mask_ref[row, t] > 0, 1, 0)
        for t in range(GROUP):
            tiles_ref[i, count + t] = jnp.int32(0)
        counts_ref[i] = count
        return 0

    lax.fori_loop(0, 2 * ROW_TILES, compact, 0)
    for c in loads[:3]:
        c.wait()

    def place_of(row, n):
        t = tiles_ref[row, n]
        owner = lax.shift_right_logical(t * 205, 10)
        return owner, pl.ds(pl.multiple_of((t - owner * ROW_TILES) * TILE, TILE), TILE)

    def run(slots, base, between):
        heads = len(slots)

        def rows_of(i):
            return pl.ds(pl.multiple_of(i * TILE, TILE), TILE)

        def groups_of(i):
            return lax.div(counts_ref[base + i] + (GROUP - 1), GROUP)

        def load_queries(i):
            qs = [q_ref[slot, rows_of(i), :].T for slot in slots]
            zero = jnp.zeros((HEAD_DIM, TILE), jnp.bfloat16)
            both = jnp.concatenate(
                [jnp.concatenate([qs[0], zero], axis=1), jnp.concatenate([zero, qs[1]], axis=1)], axis=0
            )
            return [both] + qs[2:]

        def score(i, side, g, peak, qt):
            count = counts_ref[base + i]
            at = [place_of(base + i, g * GROUP + t) for t in range(GROUP)]
            keys = [jnp.concatenate([kv_ref[o, 2 * h, r, :] for o, r in at], axis=0) for h in range(heads)]
            pair = jnp.dot(jnp.concatenate(keys[:2], axis=1), qt[0], preferred_element_type=jnp.float32)
            s = [pair[:, :TILE], pair[:, TILE:]]
            if heads == 3:
                s.append(jnp.dot(keys[2], qt[1], preferred_element_type=jnp.float32))
            out = []
            for h in range(heads):
                top = peak[h]
                for t in range(GROUP):
                    part = jnp.where(g * GROUP + t < count, s[h][t * TILE : (t + 1) * TILE], MASKED)
                    scores[side][h][g * GROUP + t] = part
                    top = jnp.maximum(top, jnp.max(part.reshape(TILE // 8, 8, TILE), axis=0))
                out.append(top)
            return tuple(out)

        def blend(i, side, g, totals, peak):
            at = [place_of(base + i, g * GROUP + t) for t in range(GROUP)]
            out = []
            for h in range(heads):
                total = totals[h]
                weights = []
                for t in range(GROUP):
                    w = jnp.exp2((scores[side][h][g * GROUP + t] - peak[h]) * factor)
                    total = total + jnp.sum(w.reshape(TILE // 8, 8, TILE), axis=0)
                    weights.append(w.astype(jnp.bfloat16))
                values = jnp.concatenate([kv_ref[o, 2 * h + 1, r, :] for o, r in at], axis=1)
                accs[h][...] += jnp.dot(values, jnp.concatenate(weights, axis=0), preferred_element_type=jnp.float32)
                out.append(total)
            return tuple(out)

        lowest = tuple(jnp.full((8, TILE), MASKED, jnp.float32) for _ in slots)
        zeros = tuple(jnp.zeros((8, TILE), jnp.float32) for _ in slots)

        def row_max(peak):
            return tuple(jnp.max(p, axis=0, keepdims=True) for p in peak)

        def clear():
            for h in range(heads):
                accs[h][...] = jnp.zeros((HEAD_DIM, TILE), jnp.float32)

        def finish(i, totals):
            for h in range(heads):
                o = accs[h][...] * (1.0 / jnp.sum(totals[h], axis=0, keepdims=True))
                o_ref[slots[h], rows_of(i), :] = o.T.astype(o_ref.dtype)

        def step(i, side, peak):
            qt = load_queries(i + 1)
            peak = row_max(peak)
            clear()
            here, there = groups_of(i), groups_of(i + 1)
            both = jnp.minimum(here, there)

            def together(g, carry):
                return score(i + 1, 1 - side, g, carry[0], qt), blend(i, side, g, carry[1], peak)

            above, totals = lax.fori_loop(0, both, together, (lowest, zeros))
            above = lax.fori_loop(both, there, lambda g, c: score(i + 1, 1 - side, g, c, qt), above)
            totals = lax.fori_loop(both, here, lambda g, c: blend(i, side, g, c, peak), totals)
            finish(i, totals)
            return above

        qt = load_queries(0)
        peak = lax.fori_loop(0, groups_of(0), lambda g, c: score(0, 0, g, c, qt), lowest)
        between()
        peak = lax.fori_loop(0, 2, lambda n, c: step(2 * n + 1, 1, step(2 * n, 0, c)), peak)
        peak = row_max(peak)
        clear()
        finish(4, lax.fori_loop(0, groups_of(4), lambda g, c: blend(4, 0, g, c, peak), zeros))

    def values_here():
        for c in loads[3:]:
            c.wait()

    run((0, 1, 2), 0, values_here)
    run((3, 4), ROW_TILES, lambda: None)


def attend(tile_mask, q, kv):
    room = -(-TILE_COUNT // GROUP) * GROUP
    return pl.pallas_call(
        attend_kernel,
        out_shape=jax.ShapeDtypeStruct((5, ROWS, HEAD_DIM), jnp.bfloat16),
        in_specs=[
            pl.BlockSpec(memory_space=pltpu.SMEM),
            pl.BlockSpec(memory_space=pltpu.VMEM),
            pl.BlockSpec(memory_space=pl.ANY),
        ],
        out_specs=pl.BlockSpec(memory_space=pltpu.VMEM),
        scratch_shapes=[
            pltpu.SMEM((2 * ROW_TILES, TILE_COUNT + 16), jnp.int32),
            pltpu.SMEM((2 * ROW_TILES,), jnp.int32),
            pltpu.VMEM((SEQ, 6, ROWS, HEAD_DIM), jnp.bfloat16),
        ]
        + [pltpu.VMEM((room, TILE, TILE), jnp.float32)] * 6
        + [pltpu.VMEM((HEAD_DIM, TILE), jnp.float32)] * 3
        + [pltpu.SemaphoreType.DMA((6,))],
        compiler_params=pltpu.CompilerParams(vmem_limit_bytes=60 << 20),
        name="attend",
    )(tile_mask, q, kv)


def project_kernel(
    o_ref, w_hbm, bias_ref, gate_ref, res_hbm, out_ref,
    w, res_ref, att, mine, sent, got, w_sem, res_sem, put_sem, send_sem, z_sem, y_sem, far_sem, sum_sem,
):
    zl, x, core, y, zh = place()
    other = 1 - zl
    me = (zl * RING + x) * 2 + core
    head_me = y * 2 + zh
    to_pair = ((other * RING + x) * 2 + core, head_me)
    right, left, opposite = lax.rem(y + 1, RING), lax.rem(y + 3, RING), lax.rem(y + 2, RING)
    to_right, to_left = (me, right * 2 + zh), (me, left * 2 + zh)
    to_sum = (me, y * 2 + 1 - zh)

    barrier = pltpu.get_barrier_semaphore()
    neighbours = [to_pair, to_right, to_left, to_sum]
    for n in neighbours:
        pl.semaphore_signal(barrier, inc=1, device_id=n, device_id_type=MESH)
    fetch = pltpu.make_async_copy(w_hbm, w, w_sem)
    fetch.start()
    fetch_res = pltpu.make_async_copy(res_hbm, res_ref, res_sem)
    fetch_res.start()
    puts = []
    for c in range(ROW_TILES):
        rows = pl.ds(c * TILE, TILE)
        puts.append(
            pltpu.make_async_copy(o_ref.at[pl.ds(0, 2), rows], att.at[c, y, pl.ds(2 * zl, 2)], put_sem.at[2 * c])
        )
        puts.append(pltpu.make_async_copy(o_ref.at[2, rows], att.at[c, y, 4], put_sem.at[2 * c + 1]))
    for c in puts:
        c.start()
    pl.semaphore_wait(barrier, len(neighbours))

    sends = []

    def send(src, dst, recv, target):
        c = pltpu.make_async_remote_copy(
            src_ref=src, dst_ref=dst, send_sem=send_sem.at[len(sends)], recv_sem=recv, device_id=target, device_id_type=MESH
        )
        c.start()
        sends.append(c)

    def arrived(dst, recv, source):
        pltpu.make_async_remote_copy(
            src_ref=dst, dst_ref=dst, send_sem=send_sem.at[0], recv_sem=recv, device_id=source, device_id_type=MESH
        ).wait_recv()

    for c in range(ROW_TILES):
        send(
            o_ref.at[pl.ds(3, 2), pl.ds(c * TILE, TILE)], att.at[c, y, pl.ds(2 * zl, 2)], z_sem.at[c], to_pair
        )
    for c in range(ROW_TILES):
        puts[2 * c].wait()
        puts[2 * c + 1].wait()
        arrived(att.at[c, y, pl.ds(2 * other, 2)], z_sem.at[c], to_pair)
        send(att.at[c, y], att.at[c, y], y_sem.at[0, c], to_right)
        send(att.at[c, y], att.at[c, y], y_sem.at[1, c], to_left)

    def halves(c):
        cut = 3 if c % 2 == 0 else 2
        return pl.ds(0, cut), pl.ds(cut, 5 - cut)

    def contract(c):
        first, second = halves(c)
        arrived(att.at[c, opposite, first], far_sem.at[0, c], to_left)
        arrived(att.at[c, opposite, second], far_sem.at[1, c], to_right)
        if c == 0:
            fetch.wait()
        rows = jnp.concatenate([att[c, n, h] for n in range(RING) for h in range(5)], axis=1)
        theirs = w[:, pl.ds(pl.multiple_of((1 - zh) * ROWS, TILE), ROWS)]
        sent[c] = jnp.dot(rows, theirs, preferred_element_type=jnp.float32).astype(jnp.bfloat16)
        send(sent.at[c], got.at[c], sum_sem.at[c], to_sum)
        ours = w[:, pl.ds(pl.multiple_of(zh * ROWS, TILE), ROWS)]
        mine[c] = jnp.dot(rows, ours, preferred_element_type=jnp.float32)

    for c in range(ROW_TILES):
        first, second = halves(c)
        arrived(att.at[c, left], y_sem.at[0, c], to_left)
        send(att.at[c, left, first], att.at[c, left, first], far_sem.at[0, c], to_right)
        arrived(att.at[c, right], y_sem.at[1, c], to_right)
        send(att.at[c, right, second], att.at[c, right, second], far_sem.at[1, c], to_left)
        if c > 0:
            contract(c - 1)
    contract(ROW_TILES - 1)
    fetch_res.wait()
    for c in range(ROW_TILES):
        arrived(got.at[c], sum_sem.at[c], to_sum)
        rows = pl.ds(c * TILE, TILE)
        projected = mine[c] + got[c].astype(jnp.float32)
        out = res_ref[rows, :].astype(jnp.float32) + gate_ref[...] * (projected + bias_ref[...])
        out_ref[rows, :] = out.astype(out_ref.dtype)
    for c in sends:
        c.wait_send()


def project(o, panel, bias, gate, residual):
    bf16 = jnp.bfloat16
    return pl.pallas_call(
        project_kernel,
        out_shape=jax.ShapeDtypeStruct((ROWS, ROWS), bf16),
        in_specs=[
            pl.BlockSpec(memory_space=pltpu.VMEM),
            pl.BlockSpec(memory_space=pl.ANY),
            pl.BlockSpec(memory_space=pltpu.VMEM),
            pl.BlockSpec(memory_space=pltpu.VMEM),
            pl.BlockSpec(memory_space=pl.ANY),
        ],
        out_specs=pl.BlockSpec(memory_space=pltpu.VMEM),
        scratch_shapes=[
            pltpu.VMEM((RING * ROWS, 2 * ROWS), bf16),
            pltpu.VMEM((ROWS, ROWS), bf16),
            pltpu.VMEM((ROW_TILES, RING, 5, TILE, HEAD_DIM), bf16),
            pltpu.VMEM((ROW_TILES, TILE, ROWS), jnp.float32),
            pltpu.VMEM((ROW_TILES, TILE, ROWS), bf16),
            pltpu.VMEM((ROW_TILES, TILE, ROWS), bf16),
            pltpu.SemaphoreType.DMA,
            pltpu.SemaphoreType.DMA,
            pltpu.SemaphoreType.DMA((10,)),
            pltpu.SemaphoreType.DMA((32,)),
            pltpu.SemaphoreType.DMA((5,)),
            pltpu.SemaphoreType.DMA((2, 5)),
            pltpu.SemaphoreType.DMA((2, 5)),
            pltpu.SemaphoreType.DMA((5,)),
        ],
        compiler_params=pltpu.CompilerParams(collective_id=1, has_side_effects=True, vmem_limit_bytes=62 << 20),
        name="project",
    )(o, panel, bias, gate, residual)


LIMIT = 40
KEYS_OF = pl.ds(0, 1)
VALUES_OF = pl.ds(1, 1)


def whole_kernel(
    owners_ref, starts_ref, bars_ref, q_ref, k_ref, v_ref, w_ref, bias_ref, gate_ref, res_hbm, out_ref,
    stage, raw_values, kva, kvb, kvh, q_own, q_pair, att, back, panel, mine, theirs, sent, got, res_ref,
    s00, s01, s10, s11, acc0, acc1,
    stage_sem, local_sem, send_sem, z_sem, x_sem, far_sem, sib_sem, w_sem, w_sib_sem, ret_sem, y_sem, y_far_sem, sum_sem,
):
    zl, x, core, y, zh = place()
    other = 1 - zl
    right, left, opposite = lax.rem(x + 1, RING), lax.rem(x + 3, RING), lax.rem(x + 2, RING)
    y_right, y_left, y_opposite = lax.rem(y + 1, RING), lax.rem(y + 3, RING), lax.rem(y + 2, RING)

    def seq_of(zl_, x_, core_):
        return (zl_ * RING + x_) * 2 + core_

    head_me = y * 2 + zh
    me = seq_of(zl, x, core)
    to_pair = (seq_of(other, x, core), head_me)
    to_right = (seq_of(zl, right, core), head_me)
    to_left = (seq_of(zl, left, core), head_me)
    to_sib = (seq_of(zl, x, 1 - core), head_me)
    to_y = [(me, lax.rem(y + d, RING) * 2 + zh) for d in (1, 2, 3)]
    to_sum = (me, y * 2 + 1 - zh)

    barrier = pltpu.get_barrier_semaphore()
    neighbours = [to_pair, to_right, to_left, to_sib, to_sum] + to_y
    for n in neighbours:
        pl.semaphore_signal(barrier, inc=1, device_id=n, device_id_type=MESH)

    def head_columns(h):
        return pl.ds(pl.multiple_of(h * HEAD_DIM, HEAD_DIM), HEAD_DIM)

    own_a, pair_a = zl * 2, other * 2
    staged = [
        (k_ref, pair_a, stage.at[6]),
        (v_ref, pair_a, raw_values.at[3]),
        (k_ref, own_a, stage.at[0]),
        (v_ref, own_a, raw_values.at[0]),
        (k_ref, own_a + 1, stage.at[2]),
        (v_ref, own_a + 1, raw_values.at[1]),
        (k_ref, pair_a + 1, stage.at[8]),
        (v_ref, pair_a + 1, raw_values.at[4]),
        (k_ref, 4, stage.at[4]),
        (v_ref, 4, raw_values.at[2]),
        (q_ref, pair_a, stage.at[10]),
        (q_ref, pair_a + 1, stage.at[11]),
    ]
    stage_copies = [
        pltpu.make_async_copy(src.at[:, :, head_columns(h)], dst, stage_sem.at[n])
        for n, (src, h, dst) in enumerate(staged)
    ]
    for c in stage_copies:
        c.start()
    half = pl.ds(pl.multiple_of(core * (ROWS // 2), ROWS // 2), ROWS // 2)
    other_half = pl.ds(pl.multiple_of((1 - core) * (ROWS // 2), ROWS // 2), ROWS // 2)

    def columns_of(y_):
        return pl.ds(pl.multiple_of(y_ * (2 * ROWS), 2 * ROWS), 2 * ROWS)

    local = [
        pltpu.make_async_copy(q_ref.at[:, :, head_columns(own_a)], q_own.at[0], local_sem.at[0]),
        pltpu.make_async_copy(q_ref.at[:, :, head_columns(own_a + 1)], q_own.at[1], local_sem.at[1]),
        pltpu.make_async_copy(q_ref.at[:, :, head_columns(4)], q_own.at[2], local_sem.at[2]),
        pltpu.make_async_copy(w_ref.at[half, columns_of(y)], panel.at[y, half], local_sem.at[3]),
        pltpu.make_async_copy(res_hbm, res_ref, local_sem.at[4]),
    ]
    for c in local:
        c.start()

    def turn(piece):
        def one(r, _):
            stage[2 * piece + 1, r] = raw_values[piece, r].T
            return 0

        lax.fori_loop(0, ROW_TILES, one, 0)

    for c in stage_copies[:4]:
        c.wait()
    turn(0)
    turn(3)
    own = [
        pltpu.make_async_copy(stage.at[pl.ds(2 * n, 2)], kv.at[me], local_sem.at[5 + n])
        for n, kv in enumerate((kva, kvb, kvh))
    ]
    own[0].start()
    pl.semaphore_wait(barrier, len(neighbours))

    sends = []

    def send(src, dst, recv, target):
        c = pltpu.make_async_remote_copy(
            src_ref=src, dst_ref=dst, send_sem=send_sem.at[len(sends)], recv_sem=recv, device_id=target, device_id_type=MESH
        )
        c.start()
        sends.append(c)

    def arrived(dst, recv, source):
        pltpu.make_async_remote_copy(
            src_ref=dst, dst_ref=dst, send_sem=send_sem.at[0], recv_sem=recv, device_id=source, device_id_type=MESH
        ).wait_recv()

    both_parts = pl.ds(0, 2)
    k_part, v_part = KEYS_OF, VALUES_OF
    sib_waits = {"a": [], "b": [], "h": []}
    sib_count = [0]

    def block(kv, zl_, x_, part=both_parts):
        return kv.at[seq_of(zl_, x_, core), part]

    def to_sibling(name, kv, zl_, x_, part=both_parts):
        n = sib_count[0]
        sib_count[0] += 1
        send(block(kv, zl_, x_, part), block(kv, zl_, x_, part), sib_sem.at[n], to_sib)
        sib_waits[name].append((n, kv, zl_, x_, part))

    def from_sibling(name):
        for n, kv, zl_, x_, part in sib_waits[name]:
            arrived(kv.at[seq_of(zl_, x_, 1 - core), part], sib_sem.at[n], to_sib)

    def ring_send(item, kv, zl_, x_, part=both_parts):
        send(block(kv, zl_, x_, part), block(kv, zl_, x_, part), x_sem.at[0, item], to_right)
        send(block(kv, zl_, x_, part), block(kv, zl_, x_, part), x_sem.at[1, item], to_left)

    def ring_pass(item, name, kv, zl_):
        arrived(block(kv, zl_, left), x_sem.at[0, item], to_left)
        send(block(kv, zl_, left, k_part), block(kv, zl_, left, k_part), far_sem.at[0, item], to_right)
        arrived(block(kv, zl_, right), x_sem.at[1, item], to_right)
        send(block(kv, zl_, right, v_part), block(kv, zl_, right, v_part), far_sem.at[1, item], to_left)
        to_sibling(name, kv, zl_, left)
        to_sibling(name, kv, zl_, right)

    def ring_far(item, name, kv, zl_):
        arrived(block(kv, zl_, opposite, k_part), far_sem.at[0, item], to_left)
        arrived(block(kv, zl_, opposite, v_part), far_sem.at[1, item], to_right)
        to_sibling(name, kv, zl_, opposite)

    A0, A1, B0, B1, H0, V1 = range(6)
    send(stage.at[pl.ds(6, 2)], kva.at[me], z_sem.at[0], to_pair)
    send(stage.at[pl.ds(0, 2)], kva.at[me], x_sem.at[0, A0], to_right)
    send(stage.at[pl.ds(0, 2)], kva.at[me], x_sem.at[1, A0], to_left)
    send(stage.at[pl.ds(0, 2)], kva.at[me], sib_sem.at[0], to_sib)
    sib_count[0] = 1
    sib_waits["a"].append((0, kva, zl, x, both_parts))
    for d in range(3):
        send(w_ref.at[half, columns_of(lax.rem(y + d + 1, RING))], panel.at[y, half], w_sem.at[d], to_y[d])
    for c in stage_copies[4:]:
        c.wait()
    turn(1)
    turn(4)
    turn(2)
    for c in own[1:]:
        c.start()
    for c in own:
        c.wait()
    arrived(block(kva, other, x), z_sem.at[0], to_pair)
    ring_send(A1, kva, other, x)
    send(stage.at[pl.ds(8, 2)], kvb.at[me], z_sem.at[1], to_pair)
    send(stage.at[pl.ds(10, 2)], q_pair, z_sem.at[2], to_pair)
    to_sibling("a", kva, other, x)
    ring_pass(A0, "a", kva, zl)
    ring_pass(A1, "a", kva, other)
    ring_send(B0, kvb, zl, x)
    to_sibling("b", kvb, zl, x)
    arrived(block(kvb, other, x), z_sem.at[1], to_pair)
    ring_send(B1, kvb, other, x)
    to_sibling("b", kvb, other, x)
    send(stage.at[pl.ds(4, 2)], kvh.at[me], z_sem.at[3], to_pair)
    ring_far(A0, "a", kva, zl)
    ring_far(A1, "a", kva, other)
    for c in local[:3]:
        c.wait()
    arrived(q_pair, z_sem.at[2], to_pair)
    from_sibling("a")

    scores = ((s00, s01), (s10, s11))
    accs = (acc0, acc1)
    factor = HEAD_DIM ** -0.5 * LOG2E
    lowest = jnp.full((8, TILE), MASKED, jnp.float32)
    nothing = jnp.zeros((8, TILE), jnp.float32)

    def place_of(row, n):
        return owners_ref[n, row], starts_ref[n, row]

    def score(kv, rows, side, g, peaks, queries, group):
        out = []
        for u, row in enumerate(rows):
            at = [place_of(row, g * group + t) for t in range(group)]
            keys = jnp.concatenate([kv[o, 0, r] for o, r in at], axis=0)
            s = jnp.dot(keys, queries[u], preferred_element_type=jnp.float32)
            top = peaks[u]
            for t in range(group):
                part = s[t * TILE : (t + 1) * TILE] + bars_ref[g * group + t, row]
                scores[side][u][g * group + t] = part
                top = jnp.maximum(top, jnp.max(part.reshape(TILE // 8, 8, TILE), axis=0))
            out.append(top)
        return tuple(out)

    def blend(kv, rows, side, g, totals, peaks, group):
        out = []
        for u, row in enumerate(rows):
            total = totals[u]
            weights = []
            for t in range(group):
                w = jnp.exp2((scores[side][u][g * group + t] - peaks[u]) * factor)
                total = total + jnp.sum(w.reshape(TILE // 8, 8, TILE), axis=0)
                weights.append(w.astype(jnp.bfloat16))
            at = [place_of(row, g * group + t) for t in range(group)]
            values = jnp.concatenate([kv[o, 1, r] for o, r in at], axis=1)
            accs[u][...] += jnp.dot(values, jnp.concatenate(weights, axis=0), preferred_element_type=jnp.float32)
            out.append(total)
        return tuple(out)

    def attention(kv, plan, tasks, group=GROUP):
        peaks = None
        for i in range(-1, len(plan)):
            here = plan[i] if i >= 0 else []
            there = plan[i + 1] if i + 1 < len(plan) else []
            side = i % 2
            rows, rows_next = [u[0] for u in here], [u[0] for u in there]
            queries = [q_of[j, r].T for _, (q_of, j, r), _ in there]
            tops = [jnp.max(p, axis=0, keepdims=True) for p in peaks] if here else []
            for u in range(len(here)):
                accs[u][...] = jnp.zeros((HEAD_DIM, TILE), jnp.float32)

            def body(g, carry):
                new_peaks = score(kv, rows_next, 1 - side, g, carry[0], queries, group)
                return new_peaks, blend(kv, rows, side, g, carry[1], tops, group)

            peaks, totals = lax.fori_loop(0, LIMIT // group, body, ((lowest,) * len(there), (nothing,) * len(here)))
            for u, (_, _, (dst, r)) in enumerate(here):
                o = accs[u][...] * (1.0 / jnp.sum(totals[u], axis=0, keepdims=True))
                dst[r, :] = o.T.astype(jnp.bfloat16)
            if i in tasks:
                tasks[i]()

    def tile_rows(i):
        return pl.ds(i * TILE, TILE)

    def plan_of(j):
        return [
            [
                (i, (q_own, j, i), (att.at[y, own_a + j], tile_rows(i))),
                (ROW_TILES + i, (q_pair, j, i), (back.at[j], tile_rows(i))),
            ]
            for i in range(ROW_TILES)
        ]

    positions = [own_a, own_a + 1, pair_a, pair_a + 1, 4]

    row_groups = {0: [(0, 640)], 1: [(0, 384), (384, 256)], 2: [(0, 640)], 3: [(0, 384), (384, 256)]}
    row_groups[4] = [(TILE * i, TILE) for i in range(ROW_TILES)]
    first_sem = {0: 0, 1: 1, 2: 3, 3: 4, 4: 6}

    def y_block(n, y_, start, count):
        return att.at[y_, positions[n], pl.ds(start, count)]

    def y_send(n, g=0):
        part = y_block(n, y, *row_groups[n][g])
        send(part, part, y_sem.at[0, first_sem[n] + g], to_y[0])
        send(part, part, y_sem.at[1, first_sem[n] + g], to_y[2])

    def y_pass(n, g=0):
        start, count = row_groups[n][g]
        arrived(y_block(n, y_left, start, count), y_sem.at[0, first_sem[n] + g], to_y[2])
        part = y_block(n, y_left, start, count // 2)
        send(part, part, y_far_sem.at[0, first_sem[n] + g], to_y[0])
        arrived(y_block(n, y_right, start, count), y_sem.at[1, first_sem[n] + g], to_y[0])
        part = y_block(n, y_right, start + count // 2, count // 2)
        send(part, part, y_far_sem.at[1, first_sem[n] + g], to_y[2])

    def y_far(n, g=0):
        start, count = row_groups[n][g]
        arrived(y_block(n, y_opposite, start, count // 2), y_far_sem.at[0, first_sem[n] + g], to_y[2])
        arrived(y_block(n, y_opposite, start + count // 2, count // 2), y_far_sem.at[1, first_sem[n] + g], to_y[0])

    def give_back(j, g=0):
        rows = pl.ds(*row_groups[2 + j][g])
        send(back.at[j, rows], att.at[y, own_a + j, rows], ret_sem.at[j + g], to_pair)

    def given_back(j, g=0):
        rows = pl.ds(*row_groups[2 + j][g])
        arrived(att.at[y, pair_a + j, rows], ret_sem.at[j + g], to_pair)
        y_send(2 + j, g)

    ours_columns = pl.ds(pl.multiple_of(zh * ROWS, TILE), ROWS)
    theirs_columns = pl.ds(pl.multiple_of((1 - zh) * ROWS, TILE), ROWS)

    def product(units, rows, columns):
        lhs = jnp.concatenate([att[n, positions[u], rows, :] for u in units for n in range(RING)], axis=1)
        rhs = jnp.concatenate([panel[n, head_columns(positions[u]), columns] for u in units for n in range(RING)], axis=0)
        return jnp.dot(lhs, rhs, preferred_element_type=jnp.float32)

    def contract(units, first, parts):
        def one(c, _):
            rows = pl.ds(pl.multiple_of(c * TILE, TILE), TILE)
            for total, columns in parts:
                p = product(units, rows, columns)
                total[rows, :] = p if first else total[rows, :] + p
            return 0

        lax.fori_loop(0, ROW_TILES, one, 0)

    def panel_here():
        for d in range(3):
            arrived(panel.at[lax.rem(y + 3 - d, RING), half], w_sem.at[d], to_y[2 - d])
        local[3].wait()
        for d in range(RING):
            y_ = lax.rem(y + d, RING)
            send(panel.at[y_, half], panel.at[y_, half], w_sib_sem.at[d], to_sib)

    def after_a1():
        ring_pass(B0, "b", kvb, zl)

    def after_a3():
        ring_pass(B1, "b", kvb, other)
        ring_send(H0, kvh, zl, x)
        to_sibling("h", kvh, zl, x)

    attention(kva, plan_of(0), {1: after_a1, 3: after_a3})
    give_back(0)
    y_send(0)
    arrived(block(kvh, other, x), z_sem.at[3], to_pair)
    ring_send(V1, kvh, other, x, v_part)
    to_sibling("h", kvh, other, x)
    ring_far(B0, "b", kvb, zl)
    ring_far(B1, "b", kvb, other)
    panel_here()
    from_sibling("b")

    v_first, v_second = pl.ds(0, 3), pl.ds(3, 2)

    def v_block(x_, rows=None):
        at = kvh.at[seq_of(other, x_, core), 1]
        return at if rows is None else at.at[rows]

    def after_b1():
        given_back(0)
        ring_pass(H0, "h", kvh, zl)
        for n, x_ in ((4, left), (5, right)):
            send(block(kvh, zl, x_, k_part), block(kvh, zl, x_, k_part), z_sem.at[n], to_pair)
        y_pass(0)

    def after_b3():
        arrived(block(kvh, other, left, v_part), x_sem.at[0, V1], to_left)
        send(v_block(left, v_first), v_block(left, v_first), far_sem.at[0, V1], to_right)
        arrived(block(kvh, other, right, v_part), x_sem.at[1, V1], to_right)
        send(v_block(right, v_second), v_block(right, v_second), far_sem.at[1, V1], to_left)
        to_sibling("h", kvh, other, left, v_part)
        to_sibling("h", kvh, other, right, v_part)
        y_pass(2)

    def after_b2():
        give_back(1, 0)
        y_send(1, 0)

    attention(kvb, plan_of(1), {1: after_b1, 2: after_b2, 3: after_b3})
    give_back(1, 1)
    y_send(1, 1)
    ring_far(H0, "h", kvh, zl)
    send(block(kvh, zl, opposite, k_part), block(kvh, zl, opposite, k_part), z_sem.at[6], to_pair)
    arrived(v_block(opposite, v_first), far_sem.at[0, V1], to_left)
    arrived(v_block(opposite, v_second), far_sem.at[1, V1], to_right)
    to_sibling("h", kvh, other, opposite, v_part)
    for n, x_ in ((4, left), (5, right)):
        arrived(block(kvh, other, x_, k_part), z_sem.at[n], to_pair)
        to_sibling("h", kvh, other, x_, k_part)
    given_back(1, 0)
    y_pass(1, 0)
    y_far(0)
    y_far(2)
    for d in range(RING):
        arrived(panel.at[lax.rem(y + d, RING), other_half], w_sib_sem.at[d], to_sib)
    contract((0, 2), True, ((theirs, theirs_columns), (mine, ours_columns)))
    given_back(1, 1)
    arrived(block(kvh, other, opposite, k_part), z_sem.at[6], to_pair)
    to_sibling("h", kvh, other, opposite, k_part)
    y_pass(1, 1)
    y_pass(3, 0)
    from_sibling("h")

    units = [
        (i, (q_own, 2, i), (att.at[y, 4], tile_rows(i))) for i in range(ROW_TILES)
    ]

    def sum_out(c):
        y_far(4, c)
        rows = tile_rows(c)
        sent[rows, :] = (theirs[rows, :] + product((1, 3, 4), rows, theirs_columns)).astype(sent.dtype)
        send(sent.at[rows], got.at[rows], sum_sem.at[c], to_sum)

    def after_h(i):
        y_send(4, i)
        if i == 0:
            y_pass(3, 1)
        else:
            y_pass(4, i - 1)
        if i == 2:
            for n in (1, 3):
                for g in range(2):
                    y_far(n, g)
        if i >= 2:
            sum_out(i - 2)

    attention(kvh, [[u] for u in units], {i: functools.partial(after_h, i) for i in range(ROW_TILES)}, 2 * GROUP)
    y_pass(4, 4)
    sum_out(3)
    sum_out(4)
    local[4].wait()
    contract((1, 3, 4), False, ((mine, ours_columns),))
    for c in range(ROW_TILES):
        rows = tile_rows(c)
        arrived(got.at[rows], sum_sem.at[c], to_sum)
        projected = mine[rows, :] + got[rows, :].astype(jnp.float32)
        out = res_ref[rows, :].astype(jnp.float32) + gate_ref[...][None, :] * (projected + bias_ref[...][None, :])
        out_ref[rows, :] = out.astype(out_ref.dtype)
    for c in sends:
        c.wait_send()


def whole(owners, starts, bars, q, k, v, w, bias, gate, residual):
    bf16, f32 = jnp.bfloat16, jnp.float32

    def by_tile(array):
        return array.reshape(ROW_TILES, TILE, ROWS)

    smem, vmem, anywhere = (
        pl.BlockSpec(memory_space=pltpu.SMEM),
        pl.BlockSpec(memory_space=pltpu.VMEM),
        pl.BlockSpec(memory_space=pl.ANY),
    )
    dma = pltpu.SemaphoreType.DMA
    return pl.pallas_call(
        whole_kernel,
        out_shape=jax.ShapeDtypeStruct((ROWS, ROWS), bf16),
        in_specs=[smem, smem, smem, anywhere, anywhere, anywhere, anywhere, vmem, vmem, anywhere],
        out_specs=vmem,
        scratch_shapes=[
            pltpu.VMEM((12, ROW_TILES, TILE, HEAD_DIM), bf16),
            pltpu.VMEM((5, ROW_TILES, TILE, HEAD_DIM), bf16),
            pltpu.VMEM((SEQ, 2, ROW_TILES, TILE, HEAD_DIM), bf16),
            pltpu.VMEM((SEQ, 2, ROW_TILES, TILE, HEAD_DIM), bf16),
            pltpu.VMEM((SEQ, 2, ROW_TILES, TILE, HEAD_DIM), bf16),
            pltpu.VMEM((3, ROW_TILES, TILE, HEAD_DIM), bf16),
            pltpu.VMEM((2, ROW_TILES, TILE, HEAD_DIM), bf16),
            pltpu.VMEM((RING, 5, ROWS, HEAD_DIM), bf16),
            pltpu.VMEM((2, ROWS, HEAD_DIM), bf16),
            pltpu.VMEM((RING, ROWS, 2 * ROWS), bf16),
            pltpu.VMEM((ROWS, ROWS), f32),
            pltpu.VMEM((ROWS, ROWS), f32),
            pltpu.VMEM((ROWS, ROWS), bf16),
            pltpu.VMEM((ROWS, ROWS), bf16),
            pltpu.VMEM((ROWS, ROWS), bf16),
        ]
        + [pltpu.VMEM((LIMIT, TILE, TILE), f32)] * 4
        + [pltpu.VMEM((HEAD_DIM, TILE), f32)] * 2
        + [
            dma((12,)), dma((8,)), dma((128,)), dma((7,)), dma((2, 6)), dma((2, 6)), dma((28,)), dma((3,)), dma((4,)),
            dma((3,)), dma((2, 11)), dma((2, 11)), dma((5,)),
        ],
        compiler_params=pltpu.CompilerParams(collective_id=2, has_side_effects=True, vmem_limit_bytes=62 << 20),
        name="whole",
    )(owners, starts, bars, by_tile(q), by_tile(k), by_tile(v), w, bias, gate, residual)


def list_kernel(mask_ref, owners_ref, starts_ref, bars_ref, longest_ref):
    zl, x, core, _, _ = place()
    rows = []
    for plane in (zl, 1 - zl):
        first = ((plane * RING + x) * 2 + core) * ROW_TILES
        rows += [mask_ref[pl.ds(first + i, 1), :] for i in range(ROW_TILES)]
    allowed = jnp.where(jnp.concatenate(rows, axis=0) > 0, 1.0, 0.0)
    square = (TILE_COUNT, TILE_COUNT)
    earlier = lax.broadcasted_iota(jnp.int32, square, 0) < lax.broadcasted_iota(jnp.int32, square, 1)
    before = jnp.dot(allowed, jnp.where(earlier, 1.0, 0.0), preferred_element_type=jnp.float32).astype(jnp.int32)
    entry = lax.broadcasted_iota(jnp.int32, (LIMIT, TILE_COUNT), 0)
    tile = lax.broadcasted_iota(jnp.int32, (LIMIT, TILE_COUNT), 1)
    lane = lax.broadcasted_iota(jnp.int32, (LIMIT, 128), 1)
    entry_column = lax.broadcasted_iota(jnp.int32, (LIMIT, 128), 0)
    owner = jnp.zeros((LIMIT, TILE_COUNT), jnp.int32)
    for n in range(1, SEQ):
        owner = owner + jnp.where(tile >= n * ROW_TILES, 1, 0)
    start = tile - owner * ROW_TILES
    owners = jnp.zeros((LIMIT, 128), jnp.int32)
    starts = jnp.zeros((LIMIT, 128), jnp.int32)
    bars = jnp.full((LIMIT, 128), MASKED, jnp.float32)
    for i in range(2 * ROW_TILES):
        hit = (before[i : i + 1] == entry) & (allowed[i : i + 1] > 0.5)
        count = jnp.sum(allowed[i : i + 1], axis=1, keepdims=True).astype(jnp.int32)
        owners = jnp.where(lane == i, jnp.sum(jnp.where(hit, owner, 0), axis=1, keepdims=True), owners)
        starts = jnp.where(lane == i, jnp.sum(jnp.where(hit, start, 0), axis=1, keepdims=True), starts)
        bars = jnp.where((lane == i) & (entry_column < count), 0.0, bars)
    owners_ref[...] = owners
    starts_ref[...] = starts
    bars_ref[...] = bars
    longest_ref[0] = jnp.max(jnp.sum(jnp.where(mask_ref[...] > 0, 1, 0), axis=1, keepdims=True))


def tile_lists(tile_mask):
    vmem, smem = pl.BlockSpec(memory_space=pltpu.VMEM), pl.BlockSpec(memory_space=pltpu.SMEM)
    return pl.pallas_call(
        list_kernel,
        out_shape=[
            jax.ShapeDtypeStruct((LIMIT, 128), jnp.int32),
            jax.ShapeDtypeStruct((LIMIT, 128), jnp.int32),
            jax.ShapeDtypeStruct((LIMIT, 128), jnp.float32),
            jax.ShapeDtypeStruct((1,), jnp.int32),
        ],
        in_specs=[vmem],
        out_specs=[vmem, vmem, vmem, smem],
        name="tile_lists",
    )(tile_mask)


def local(queries, key_states, value_states, tile_mask, out_weight, out_bias, residual, gate_scale):
    bias, gate = out_bias, gate_scale
    owners, starts, bars, longest = tile_lists(tile_mask)

    def by_lists(_):
        return whole(owners, starts, bars, queries, key_states, value_states, out_weight, bias, gate, residual)

    def in_parts(_):
        kv, q, panel = gather(queries, key_states, value_states, out_weight)
        o = attend(tile_mask, q, kv)
        return project(o, panel.reshape(RING * ROWS, 2 * ROWS), bias[None, :], gate[None, :], residual)

    return lax.cond(longest[0] <= LIMIT, by_lists, in_parts, 0)


def solution(mesh):
    return jax.shard_map(
        local,
        mesh=mesh,
        in_specs=(
            P("seq", "head"),
            P("seq", "head"),
            P("seq", "head"),
            P(),
            P("head", None),
            P("head"),
            P("seq", "head"),
            P("head"),
        ),
        out_specs=P("seq", "head"),
        check_vma=False,
    )
```

```python
import functools

import jax
import jax.numpy as jnp
from jax import lax
from jax.experimental import pallas as pl
from jax.experimental.pallas import tpu as pltpu
from jax.sharding import PartitionSpec as P

HEAD_DIM = 128
TILE = 128
ROWS = 640
ROW_TILES = ROWS // TILE
SEQ = 16
RING = 4
TILE_COUNT = 80
MESH = pl.DeviceIdType.MESH
MASKED = -1e30


def place():
    s = lax.axis_index("seq")
    h = lax.axis_index("head")
    return lax.div(s, 8), lax.rem(lax.div(s, 2), 4), lax.rem(s, 2), lax.div(h, 2), lax.rem(h, 2)


def gather_kernel(
    q_ref, k_ref, v_ref, w_ref, kv_out, q_out, w_out,
    stage, raw_values, stage_sem, local_sem, send_sem, z_sem, x_sem, far_sem, sib_sem, w_sem, w_sib_sem,
):
    zl, x, core, y, zh = place()
    other = 1 - zl
    right, left = lax.rem(x + 1, RING), lax.rem(x + 3, RING)
    opposite = lax.rem(x + 2, RING)

    def seq_of(zl_, x_, core_):
        return (zl_ * RING + x_) * 2 + core_

    head_me = y * 2 + zh
    me = seq_of(zl, x, core)
    to_pair = (seq_of(other, x, core), head_me)
    to_right = (seq_of(zl, right, core), head_me)
    to_left = (seq_of(zl, left, core), head_me)
    to_sib = (seq_of(zl, x, 1 - core), head_me)
    to_y = [(me, lax.rem(y + d, RING) * 2 + zh) for d in (1, 2, 3)]

    barrier = pltpu.get_barrier_semaphore()
    neighbours = [to_pair, to_right, to_left, to_sib] + to_y
    for n in neighbours:
        pl.semaphore_signal(barrier, inc=1, device_id=n, device_id_type=MESH)

    def head_columns(h):
        return pl.ds(pl.multiple_of(h * HEAD_DIM, HEAD_DIM), HEAD_DIM)

    own_a, pair_a = zl * 2, other * 2
    staged = [
        (k_ref, own_a, stage.at[0]),
        (k_ref, own_a + 1, stage.at[2]),
        (k_ref, 4, stage.at[4]),
        (k_ref, pair_a, stage.at[6]),
        (k_ref, pair_a + 1, stage.at[8]),
        (q_ref, pair_a, stage.at[10]),
        (q_ref, pair_a + 1, stage.at[11]),
        (v_ref, own_a, raw_values.at[0]),
        (v_ref, own_a + 1, raw_values.at[1]),
        (v_ref, 4, raw_values.at[2]),
        (v_ref, pair_a, raw_values.at[3]),
        (v_ref, pair_a + 1, raw_values.at[4]),
    ]
    stage_copies = [
        pltpu.make_async_copy(src.at[:, head_columns(h)], dst, stage_sem.at[n])
        for n, (src, h, dst) in enumerate(staged)
    ]
    for c in stage_copies:
        c.start()
    half = pl.ds(pl.multiple_of(core * (ROWS // 2), ROWS // 2), ROWS // 2)
    other_half = pl.ds(pl.multiple_of((1 - core) * (ROWS // 2), ROWS // 2), ROWS // 2)

    def panel(y_):
        return pl.ds(pl.multiple_of(y_ * (2 * ROWS), 2 * ROWS), 2 * ROWS)

    local = [
        pltpu.make_async_copy(q_ref.at[:, head_columns(zl * 2)], q_out.at[0], local_sem.at[0]),
        pltpu.make_async_copy(q_ref.at[:, head_columns(zl * 2 + 1)], q_out.at[1], local_sem.at[1]),
        pltpu.make_async_copy(q_ref.at[:, head_columns(4)], q_out.at[2], local_sem.at[2]),
        pltpu.make_async_copy(w_ref.at[half, panel(y)], w_out.at[y, half], local_sem.at[3]),
    ]
    for c in local:
        c.start()
    for c in stage_copies:
        c.wait()

    def turn(n, _):
        piece = lax.div(n, ROW_TILES)
        rows = pl.ds(pl.multiple_of((n - piece * ROW_TILES) * TILE, TILE), TILE)
        stage[2 * piece + 1, rows, :] = raw_values[piece, rows, :].T
        return 0

    lax.fori_loop(0, 5 * ROW_TILES, turn, 0)
    own = pltpu.make_async_copy(stage.at[pl.ds(0, 6)], kv_out.at[me], local_sem.at[4])
    own.start()
    pl.semaphore_wait(barrier, len(neighbours))

    sends = []

    def send(src, dst, recv, target):
        c = pltpu.make_async_remote_copy(
            src_ref=src, dst_ref=dst, send_sem=send_sem.at[len(sends)], recv_sem=recv, device_id=target, device_id_type=MESH
        )
        c.start()
        sends.append(c)

    def arrived(dst, recv, source):
        pltpu.make_async_remote_copy(
            src_ref=dst, dst_ref=dst, send_sem=send_sem.at[0], recv_sem=recv, device_id=source, device_id_type=MESH
        ).wait_recv()

    A, B, H = pl.ds(0, 2), pl.ds(2, 2), pl.ds(4, 2)
    H0, H1 = pl.ds(4, 1), pl.ds(5, 1)
    sib_waits = []

    def to_sibling(origin_zl, origin_x, part):
        n = len(sib_waits)
        block = kv_out.at[seq_of(origin_zl, origin_x, core), part]
        send(block, block, sib_sem.at[n], to_sib)
        sib_waits.append((origin_zl, origin_x, part))

    def pass_on(origin_zl, origin_x, part, recv, target):
        block = kv_out.at[seq_of(origin_zl, origin_x, core), part]
        send(block, block, recv, target)

    def block_of(origin_zl, origin_x, part):
        return kv_out.at[seq_of(origin_zl, origin_x, core), part]

    send(stage.at[pl.ds(6, 2)], kv_out.at[me, A], z_sem.at[0], to_pair)
    send(stage.at[pl.ds(8, 2)], kv_out.at[me, B], z_sem.at[1], to_pair)
    for item, part, at in ((0, H, 4), (1, A, 0), (2, B, 2)):
        send(stage.at[pl.ds(at, 2)], kv_out.at[me, part], x_sem.at[0, item], to_right)
        send(stage.at[pl.ds(at, 2)], kv_out.at[me, part], x_sem.at[1, item], to_left)
    for d in range(3):
        send(w_ref.at[half, panel(lax.rem(y + d + 1, RING))], w_out.at[y, half], w_sem.at[d], to_y[d])
    own.wait()
    to_sibling(zl, x, pl.ds(0, 6))

    for item, part, n in ((3, A, 0), (4, B, 1)):
        arrived(block_of(other, x, part), z_sem.at[n], to_pair)
        pass_on(other, x, part, x_sem.at[0, item], to_right)
        pass_on(other, x, part, x_sem.at[1, item], to_left)
        if n == 0:
            send(stage.at[pl.ds(4, 2)], kv_out.at[me, H], z_sem.at[2], to_pair)
        else:
            send(stage.at[pl.ds(10, 2)], q_out.at[pl.ds(3, 2)], z_sem.at[3], to_pair)
        to_sibling(other, x, part)

    def from_left(item, zl_, part):
        arrived(block_of(zl_, left, part), x_sem.at[0, item], to_left)

    def from_right(item, zl_, part):
        arrived(block_of(zl_, right, part), x_sem.at[1, item], to_right)

    from_left(0, zl, H)
    pass_on(zl, left, H0, far_sem.at[0, 0], to_right)
    pass_on(zl, left, H, z_sem.at[4], to_pair)
    to_sibling(zl, left, H)
    from_right(0, zl, H)
    pass_on(zl, right, H1, far_sem.at[1, 0], to_left)
    pass_on(zl, right, H, z_sem.at[5], to_pair)
    to_sibling(zl, right, H)

    for item, zl_, far in ((1, zl, 1), (3, other, 2)):
        from_left(item, zl_, A)
        pass_on(zl_, left, A, far_sem.at[0, far], to_right)
        to_sibling(zl_, left, A)
        from_right(item, zl_, A)
        to_sibling(zl_, right, A)
        from_right(item + 1, zl_, B)
        pass_on(zl_, right, B, far_sem.at[1, far], to_left)
        to_sibling(zl_, right, B)
        from_left(item + 1, zl_, B)
        to_sibling(zl_, left, B)
        if far == 1:
            arrived(block_of(zl, opposite, H0), far_sem.at[0, 0], to_left)
            arrived(block_of(zl, opposite, H1), far_sem.at[1, 0], to_right)
            pass_on(zl, opposite, H, z_sem.at[6], to_pair)
            to_sibling(zl, opposite, H)
            arrived(block_of(other, x, H), z_sem.at[2], to_pair)
            to_sibling(other, x, H)
    for d in range(3):
        y_ = lax.rem(y + 3 - d, RING)
        arrived(w_out.at[y_, half], w_sem.at[d], to_y[2 - d])
    for d in range(4):
        y_ = lax.rem(y + d, RING)
        if d == 0:
            local[3].wait()
        send(w_out.at[y_, half], w_out.at[y_, half], w_sib_sem.at[d], to_sib)
    for zl_, far in ((zl, 1), (other, 2)):
        arrived(block_of(zl_, opposite, A), far_sem.at[0, far], to_left)
        to_sibling(zl_, opposite, A)
        arrived(block_of(zl_, opposite, B), far_sem.at[1, far], to_right)
        to_sibling(zl_, opposite, B)
    for n, x_ in ((4, left), (5, right), (6, opposite)):
        arrived(block_of(other, x_, H), z_sem.at[n], to_pair)
        to_sibling(other, x_, H)
    arrived(q_out.at[pl.ds(3, 2)], z_sem.at[3], to_pair)
    for d in range(4):
        y_ = lax.rem(y + d, RING)
        arrived(w_out.at[y_, other_half], w_sib_sem.at[d], to_sib)
    for n, (zl_, x_, part) in enumerate(sib_waits):
        arrived(kv_out.at[seq_of(zl_, x_, 1 - core), part], sib_sem.at[n], to_sib)
    for c in sends:
        c.wait_send()
    for c in local[:3]:
        c.wait()


def gather(q, k, v, w):
    bf16 = jnp.bfloat16
    return pl.pallas_call(
        gather_kernel,
        out_shape=[
            jax.ShapeDtypeStruct((SEQ, 6, ROWS, HEAD_DIM), bf16),
            jax.ShapeDtypeStruct((5, ROWS, HEAD_DIM), bf16),
            jax.ShapeDtypeStruct((RING, ROWS, 2 * ROWS), bf16),
        ],
        in_specs=[pl.BlockSpec(memory_space=pl.ANY)] * 4,
        out_specs=[pl.BlockSpec(memory_space=pl.ANY)] * 3,
        scratch_shapes=[
            pltpu.VMEM((12, ROWS, HEAD_DIM), bf16),
            pltpu.VMEM((5, ROWS, HEAD_DIM), bf16),
            pltpu.SemaphoreType.DMA((12,)),
            pltpu.SemaphoreType.DMA((5,)),
            pltpu.SemaphoreType.DMA((64,)),
            pltpu.SemaphoreType.DMA((7,)),
            pltpu.SemaphoreType.DMA((2, 5)),
            pltpu.SemaphoreType.DMA((2, 3)),
            pltpu.SemaphoreType.DMA((24,)),
            pltpu.SemaphoreType.DMA((3,)),
            pltpu.SemaphoreType.DMA((4,)),
        ],
        compiler_params=pltpu.CompilerParams(collective_id=0, has_side_effects=True),
        name="gather_heads",
    )(q, k, v, w)


GROUP = 10
LOG2E = 1.4426950408889634


def attend_kernel(
    mask_ref, q_ref, kv_hbm, o_ref, tiles_ref, counts_ref, kv_ref, s00, s01, s02, s10, s11, s12, acc0, acc1, acc2, sem
):
    scores = ((s00, s01, s02), (s10, s11, s12))
    accs = (acc0, acc1, acc2)
    factor = HEAD_DIM ** -0.5 * LOG2E
    loads = [pltpu.make_async_copy(kv_hbm.at[:, p], kv_ref.at[:, p], sem.at[p]) for p in (0, 2, 4, 1, 3, 5)]
    for c in loads:
        c.start()
    zl, x, core, _, _ = place()
    first = ((zl * RING + x) * 2 + core) * ROW_TILES
    first_pair = (((1 - zl) * RING + x) * 2 + core) * ROW_TILES

    def compact(i, _):
        row = jnp.where(i < ROW_TILES, first + i, first_pair + i - ROW_TILES)
        count = jnp.int32(0)
        for t in range(TILE_COUNT):
            tiles_ref[i, count] = jnp.int32(t)
            count = count + jnp.where(mask_ref[row, t] > 0, 1, 0)
        for t in range(GROUP):
            tiles_ref[i, count + t] = jnp.int32(0)
        counts_ref[i] = count
        return 0

    lax.fori_loop(0, 2 * ROW_TILES, compact, 0)
    for c in loads[:3]:
        c.wait()

    def place_of(row, n):
        t = tiles_ref[row, n]
        owner = lax.shift_right_logical(t * 205, 10)
        return owner, pl.ds(pl.multiple_of((t - owner * ROW_TILES) * TILE, TILE), TILE)

    def run(slots, base, between):
        heads = len(slots)

        def rows_of(i):
            return pl.ds(pl.multiple_of(i * TILE, TILE), TILE)

        def groups_of(i):
            return lax.div(counts_ref[base + i] + (GROUP - 1), GROUP)

        def load_queries(i):
            qs = [q_ref[slot, rows_of(i), :].T for slot in slots]
            zero = jnp.zeros((HEAD_DIM, TILE), jnp.bfloat16)
            both = jnp.concatenate(
                [jnp.concatenate([qs[0], zero], axis=1), jnp.concatenate([zero, qs[1]], axis=1)], axis=0
            )
            return [both] + qs[2:]

        def score(i, side, g, peak, qt):
            count = counts_ref[base + i]
            at = [place_of(base + i, g * GROUP + t) for t in range(GROUP)]
            keys = [jnp.concatenate([kv_ref[o, 2 * h, r, :] for o, r in at], axis=0) for h in range(heads)]
            pair = jnp.dot(jnp.concatenate(keys[:2], axis=1), qt[0], preferred_element_type=jnp.float32)
            s = [pair[:, :TILE], pair[:, TILE:]]
            if heads == 3:
                s.append(jnp.dot(keys[2], qt[1], preferred_element_type=jnp.float32))
            out = []
            for h in range(heads):
                top = peak[h]
                for t in range(GROUP):
                    part = jnp.where(g * GROUP + t < count, s[h][t * TILE : (t + 1) * TILE], MASKED)
                    scores[side][h][g * GROUP + t] = part
                    top = jnp.maximum(top, jnp.max(part.reshape(TILE // 8, 8, TILE), axis=0))
                out.append(top)
            return tuple(out)

        def blend(i, side, g, totals, peak):
            at = [place_of(base + i, g * GROUP + t) for t in range(GROUP)]
            out = []
            for h in range(heads):
                total = totals[h]
                weights = []
                for t in range(GROUP):
                    w = jnp.exp2((scores[side][h][g * GROUP + t] - peak[h]) * factor)
                    total = total + jnp.sum(w.reshape(TILE // 8, 8, TILE), axis=0)
                    weights.append(w.astype(jnp.bfloat16))
                values = jnp.concatenate([kv_ref[o, 2 * h + 1, r, :] for o, r in at], axis=1)
                accs[h][...] += jnp.dot(values, jnp.concatenate(weights, axis=0), preferred_element_type=jnp.float32)
                out.append(total)
            return tuple(out)

        lowest = tuple(jnp.full((8, TILE), MASKED, jnp.float32) for _ in slots)
        zeros = tuple(jnp.zeros((8, TILE), jnp.float32) for _ in slots)

        def row_max(peak):
            return tuple(jnp.max(p, axis=0, keepdims=True) for p in peak)

        def clear():
            for h in range(heads):
                accs[h][...] = jnp.zeros((HEAD_DIM, TILE), jnp.float32)

        def finish(i, totals):
            for h in range(heads):
                o = accs[h][...] * (1.0 / jnp.sum(totals[h], axis=0, keepdims=True))
                o_ref[slots[h], rows_of(i), :] = o.T.astype(o_ref.dtype)

        def step(i, side, peak):
            qt = load_queries(i + 1)
            peak = row_max(peak)
            clear()
            here, there = groups_of(i), groups_of(i + 1)
            both = jnp.minimum(here, there)

            def together(g, carry):
                return score(i + 1, 1 - side, g, carry[0], qt), blend(i, side, g, carry[1], peak)

            above, totals = lax.fori_loop(0, both, together, (lowest, zeros))
            above = lax.fori_loop(both, there, lambda g, c: score(i + 1, 1 - side, g, c, qt), above)
            totals = lax.fori_loop(both, here, lambda g, c: blend(i, side, g, c, peak), totals)
            finish(i, totals)
            return above

        qt = load_queries(0)
        peak = lax.fori_loop(0, groups_of(0), lambda g, c: score(0, 0, g, c, qt), lowest)
        between()
        peak = lax.fori_loop(0, 2, lambda n, c: step(2 * n + 1, 1, step(2 * n, 0, c)), peak)
        peak = row_max(peak)
        clear()
        finish(4, lax.fori_loop(0, groups_of(4), lambda g, c: blend(4, 0, g, c, peak), zeros))

    def values_here():
        for c in loads[3:]:
            c.wait()

    run((0, 1, 2), 0, values_here)
    run((3, 4), ROW_TILES, lambda: None)


def attend(tile_mask, q, kv):
    room = -(-TILE_COUNT // GROUP) * GROUP
    return pl.pallas_call(
        attend_kernel,
        out_shape=jax.ShapeDtypeStruct((5, ROWS, HEAD_DIM), jnp.bfloat16),
        in_specs=[
            pl.BlockSpec(memory_space=pltpu.SMEM),
            pl.BlockSpec(memory_space=pltpu.VMEM),
            pl.BlockSpec(memory_space=pl.ANY),
        ],
        out_specs=pl.BlockSpec(memory_space=pltpu.VMEM),
        scratch_shapes=[
            pltpu.SMEM((2 * ROW_TILES, TILE_COUNT + 16), jnp.int32),
            pltpu.SMEM((2 * ROW_TILES,), jnp.int32),
            pltpu.VMEM((SEQ, 6, ROWS, HEAD_DIM), jnp.bfloat16),
        ]
        + [pltpu.VMEM((room, TILE, TILE), jnp.float32)] * 6
        + [pltpu.VMEM((HEAD_DIM, TILE), jnp.float32)] * 3
        + [pltpu.SemaphoreType.DMA((6,))],
        compiler_params=pltpu.CompilerParams(vmem_limit_bytes=60 << 20),
        name="attend",
    )(tile_mask, q, kv)


def project_kernel(
    o_ref, w_hbm, bias_ref, gate_ref, res_hbm, out_ref,
    w, res_ref, att, mine, sent, got, w_sem, res_sem, put_sem, send_sem, z_sem, y_sem, far_sem, sum_sem,
):
    zl, x, core, y, zh = place()
    other = 1 - zl
    me = (zl * RING + x) * 2 + core
    head_me = y * 2 + zh
    to_pair = ((other * RING + x) * 2 + core, head_me)
    right, left, opposite = lax.rem(y + 1, RING), lax.rem(y + 3, RING), lax.rem(y + 2, RING)
    to_right, to_left = (me, right * 2 + zh), (me, left * 2 + zh)
    to_sum = (me, y * 2 + 1 - zh)

    barrier = pltpu.get_barrier_semaphore()
    neighbours = [to_pair, to_right, to_left, to_sum]
    for n in neighbours:
        pl.semaphore_signal(barrier, inc=1, device_id=n, device_id_type=MESH)
    fetch = pltpu.make_async_copy(w_hbm, w, w_sem)
    fetch.start()
    fetch_res = pltpu.make_async_copy(res_hbm, res_ref, res_sem)
    fetch_res.start()
    puts = []
    for c in range(ROW_TILES):
        rows = pl.ds(c * TILE, TILE)
        puts.append(
            pltpu.make_async_copy(o_ref.at[pl.ds(0, 2), rows], att.at[c, y, pl.ds(2 * zl, 2)], put_sem.at[2 * c])
        )
        puts.append(pltpu.make_async_copy(o_ref.at[2, rows], att.at[c, y, 4], put_sem.at[2 * c + 1]))
    for c in puts:
        c.start()
    pl.semaphore_wait(barrier, len(neighbours))

    sends = []

    def send(src, dst, recv, target):
        c = pltpu.make_async_remote_copy(
            src_ref=src, dst_ref=dst, send_sem=send_sem.at[len(sends)], recv_sem=recv, device_id=target, device_id_type=MESH
        )
        c.start()
        sends.append(c)

    def arrived(dst, recv, source):
        pltpu.make_async_remote_copy(
            src_ref=dst, dst_ref=dst, send_sem=send_sem.at[0], recv_sem=recv, device_id=source, device_id_type=MESH
        ).wait_recv()

    for c in range(ROW_TILES):
        send(
            o_ref.at[pl.ds(3, 2), pl.ds(c * TILE, TILE)], att.at[c, y, pl.ds(2 * zl, 2)], z_sem.at[c], to_pair
        )
    for c in range(ROW_TILES):
        puts[2 * c].wait()
        puts[2 * c + 1].wait()
        arrived(att.at[c, y, pl.ds(2 * other, 2)], z_sem.at[c], to_pair)
        send(att.at[c, y], att.at[c, y], y_sem.at[0, c], to_right)
        send(att.at[c, y], att.at[c, y], y_sem.at[1, c], to_left)

    def halves(c):
        cut = 3 if c % 2 == 0 else 2
        return pl.ds(0, cut), pl.ds(cut, 5 - cut)

    def contract(c):
        first, second = halves(c)
        arrived(att.at[c, opposite, first], far_sem.at[0, c], to_left)
        arrived(att.at[c, opposite, second], far_sem.at[1, c], to_right)
        if c == 0:
            fetch.wait()
        rows = jnp.concatenate([att[c, n, h] for n in range(RING) for h in range(5)], axis=1)
        theirs = w[:, pl.ds(pl.multiple_of((1 - zh) * ROWS, TILE), ROWS)]
        sent[c] = jnp.dot(rows, theirs, preferred_element_type=jnp.float32).astype(jnp.bfloat16)
        send(sent.at[c], got.at[c], sum_sem.at[c], to_sum)
        ours = w[:, pl.ds(pl.multiple_of(zh * ROWS, TILE), ROWS)]
        mine[c] = jnp.dot(rows, ours, preferred_element_type=jnp.float32)

    for c in range(ROW_TILES):
        first, second = halves(c)
        arrived(att.at[c, left], y_sem.at[0, c], to_left)
        send(att.at[c, left, first], att.at[c, left, first], far_sem.at[0, c], to_right)
        arrived(att.at[c, right], y_sem.at[1, c], to_right)
        send(att.at[c, right, second], att.at[c, right, second], far_sem.at[1, c], to_left)
        if c > 0:
            contract(c - 1)
    contract(ROW_TILES - 1)
    fetch_res.wait()
    for c in range(ROW_TILES):
        arrived(got.at[c], sum_sem.at[c], to_sum)
        rows = pl.ds(c * TILE, TILE)
        projected = mine[c] + got[c].astype(jnp.float32)
        out = res_ref[rows, :].astype(jnp.float32) + gate_ref[...] * (projected + bias_ref[...])
        out_ref[rows, :] = out.astype(out_ref.dtype)
    for c in sends:
        c.wait_send()


def project(o, panel, bias, gate, residual):
    bf16 = jnp.bfloat16
    return pl.pallas_call(
        project_kernel,
        out_shape=jax.ShapeDtypeStruct((ROWS, ROWS), bf16),
        in_specs=[
            pl.BlockSpec(memory_space=pltpu.VMEM),
            pl.BlockSpec(memory_space=pl.ANY),
            pl.BlockSpec(memory_space=pltpu.VMEM),
            pl.BlockSpec(memory_space=pltpu.VMEM),
            pl.BlockSpec(memory_space=pl.ANY),
        ],
        out_specs=pl.BlockSpec(memory_space=pltpu.VMEM),
        scratch_shapes=[
            pltpu.VMEM((RING * ROWS, 2 * ROWS), bf16),
            pltpu.VMEM((ROWS, ROWS), bf16),
            pltpu.VMEM((ROW_TILES, RING, 5, TILE, HEAD_DIM), bf16),
            pltpu.VMEM((ROW_TILES, TILE, ROWS), jnp.float32),
            pltpu.VMEM((ROW_TILES, TILE, ROWS), bf16),
            pltpu.VMEM((ROW_TILES, TILE, ROWS), bf16),
            pltpu.SemaphoreType.DMA,
            pltpu.SemaphoreType.DMA,
            pltpu.SemaphoreType.DMA((10,)),
            pltpu.SemaphoreType.DMA((32,)),
            pltpu.SemaphoreType.DMA((5,)),
            pltpu.SemaphoreType.DMA((2, 5)),
            pltpu.SemaphoreType.DMA((2, 5)),
            pltpu.SemaphoreType.DMA((5,)),
        ],
        compiler_params=pltpu.CompilerParams(collective_id=1, has_side_effects=True, vmem_limit_bytes=62 << 20),
        name="project",
    )(o, panel, bias, gate, residual)


LIMIT = 40
KEYS_OF = pl.ds(0, 1)
VALUES_OF = pl.ds(1, 1)


def whole_kernel(
    owners_ref, starts_ref, bars_ref, q_ref, k_ref, v_ref, w_ref, bias_ref, gate_ref, res_hbm, out_ref,
    stage, raw_values, kva, kvb, kvh, q_own, q_pair, att, back, panel, mine, theirs, sent, got, res_ref,
    s00, s01, s10, s11, acc0, acc1,
    stage_sem, local_sem, send_sem, z_sem, x_sem, far_sem, sib_sem, w_sem, w_sib_sem, ret_sem, y_sem, y_far_sem, sum_sem,
):
    zl, x, core, y, zh = place()
    other = 1 - zl
    right, left, opposite = lax.rem(x + 1, RING), lax.rem(x + 3, RING), lax.rem(x + 2, RING)
    y_right, y_left, y_opposite = lax.rem(y + 1, RING), lax.rem(y + 3, RING), lax.rem(y + 2, RING)

    def seq_of(zl_, x_, core_):
        return (zl_ * RING + x_) * 2 + core_

    head_me = y * 2 + zh
    me = seq_of(zl, x, core)
    to_pair = (seq_of(other, x, core), head_me)
    to_right = (seq_of(zl, right, core), head_me)
    to_left = (seq_of(zl, left, core), head_me)
    to_sib = (seq_of(zl, x, 1 - core), head_me)
    to_y = [(me, lax.rem(y + d, RING) * 2 + zh) for d in (1, 2, 3)]
    to_sum = (me, y * 2 + 1 - zh)

    barrier = pltpu.get_barrier_semaphore()
    neighbours = [to_pair, to_right, to_left, to_sib, to_sum] + to_y
    for n in neighbours:
        pl.semaphore_signal(barrier, inc=1, device_id=n, device_id_type=MESH)

    def head_columns(h):
        return pl.ds(pl.multiple_of(h * HEAD_DIM, HEAD_DIM), HEAD_DIM)

    own_a, pair_a = zl * 2, other * 2
    staged = [
        (k_ref, pair_a, stage.at[6]),
        (v_ref, pair_a, raw_values.at[3]),
        (k_ref, own_a, stage.at[0]),
        (v_ref, own_a, raw_values.at[0]),
        (k_ref, own_a + 1, stage.at[2]),
        (v_ref, own_a + 1, raw_values.at[1]),
        (k_ref, pair_a + 1, stage.at[8]),
        (v_ref, pair_a + 1, raw_values.at[4]),
        (k_ref, 4, stage.at[4]),
        (v_ref, 4, raw_values.at[2]),
        (q_ref, pair_a, stage.at[10]),
        (q_ref, pair_a + 1, stage.at[11]),
    ]
    stage_copies = [
        pltpu.make_async_copy(src.at[:, :, head_columns(h)], dst, stage_sem.at[n])
        for n, (src, h, dst) in enumerate(staged)
    ]
    for c in stage_copies:
        c.start()
    half = pl.ds(pl.multiple_of(core * (ROWS // 2), ROWS // 2), ROWS // 2)
    other_half = pl.ds(pl.multiple_of((1 - core) * (ROWS // 2), ROWS // 2), ROWS // 2)

    def columns_of(y_):
        return pl.ds(pl.multiple_of(y_ * (2 * ROWS), 2 * ROWS), 2 * ROWS)

    local = [
        pltpu.make_async_copy(q_ref.at[:, :, head_columns(own_a)], q_own.at[0], local_sem.at[0]),
        pltpu.make_async_copy(q_ref.at[:, :, head_columns(own_a + 1)], q_own.at[1], local_sem.at[1]),
        pltpu.make_async_copy(q_ref.at[:, :, head_columns(4)], q_own.at[2], local_sem.at[2]),
        pltpu.make_async_copy(w_ref.at[half, columns_of(y)], panel.at[y, half], local_sem.at[3]),
        pltpu.make_async_copy(res_hbm, res_ref, local_sem.at[4]),
    ]
    for c in local:
        c.start()

    def turn(piece):
        def one(r, _):
            stage[2 * piece + 1, r] = raw_values[piece, r].T
            return 0

        lax.fori_loop(0, ROW_TILES, one, 0)

    for c in stage_copies[:4]:
        c.wait()
    turn(0)
    turn(3)
    own = [
        pltpu.make_async_copy(stage.at[pl.ds(2 * n, 2)], kv.at[me], local_sem.at[5 + n])
        for n, kv in enumerate((kva, kvb, kvh))
    ]
    own[0].start()
    pl.semaphore_wait(barrier, len(neighbours))

    sends = []

    def send(src, dst, recv, target):
        c = pltpu.make_async_remote_copy(
            src_ref=src, dst_ref=dst, send_sem=send_sem.at[len(sends)], recv_sem=recv, device_id=target, device_id_type=MESH
        )
        c.start()
        sends.append(c)

    def arrived(dst, recv, source):
        pltpu.make_async_remote_copy(
            src_ref=dst, dst_ref=dst, send_sem=send_sem.at[0], recv_sem=recv, device_id=source, device_id_type=MESH
        ).wait_recv()

    both_parts = pl.ds(0, 2)
    k_part, v_part = KEYS_OF, VALUES_OF
    sib_waits = {"a": [], "b": [], "h": []}
    sib_count = [0]

    def block(kv, zl_, x_, part=both_parts):
        return kv.at[seq_of(zl_, x_, core), part]

    def to_sibling(name, kv, zl_, x_, part=both_parts):
        n = sib_count[0]
        sib_count[0] += 1
        send(block(kv, zl_, x_, part), block(kv, zl_, x_, part), sib_sem.at[n], to_sib)
        sib_waits[name].append((n, kv, zl_, x_, part))

    def from_sibling(name):
        for n, kv, zl_, x_, part in sib_waits[name]:
            arrived(kv.at[seq_of(zl_, x_, 1 - core), part], sib_sem.at[n], to_sib)

    def ring_send(item, kv, zl_, x_, part=both_parts):
        send(block(kv, zl_, x_, part), block(kv, zl_, x_, part), x_sem.at[0, item], to_right)
        send(block(kv, zl_, x_, part), block(kv, zl_, x_, part), x_sem.at[1, item], to_left)

    def ring_pass(item, name, kv, zl_):
        arrived(block(kv, zl_, left), x_sem.at[0, item], to_left)
        send(block(kv, zl_, left, k_part), block(kv, zl_, left, k_part), far_sem.at[0, item], to_right)
        arrived(block(kv, zl_, right), x_sem.at[1, item], to_right)
        send(block(kv, zl_, right, v_part), block(kv, zl_, right, v_part), far_sem.at[1, item], to_left)
        to_sibling(name, kv, zl_, left)
        to_sibling(name, kv, zl_, right)

    def ring_far(item, name, kv, zl_):
        arrived(block(kv, zl_, opposite, k_part), far_sem.at[0, item], to_left)
        arrived(block(kv, zl_, opposite, v_part), far_sem.at[1, item], to_right)
        to_sibling(name, kv, zl_, opposite)

    A0, A1, B0, B1, H0, V1 = range(6)
    send(stage.at[pl.ds(6, 2)], kva.at[me], z_sem.at[0], to_pair)
    send(stage.at[pl.ds(0, 2)], kva.at[me], x_sem.at[0, A0], to_right)
    send(stage.at[pl.ds(0, 2)], kva.at[me], x_sem.at[1, A0], to_left)
    send(stage.at[pl.ds(0, 2)], kva.at[me], sib_sem.at[0], to_sib)
    sib_count[0] = 1
    sib_waits["a"].append((0, kva, zl, x, both_parts))
    for d in range(3):
        send(w_ref.at[half, columns_of(lax.rem(y + d + 1, RING))], panel.at[y, half], w_sem.at[d], to_y[d])
    for c in stage_copies[4:]:
        c.wait()
    turn(1)
    turn(4)
    turn(2)
    for c in own[1:]:
        c.start()
    for c in own:
        c.wait()
    arrived(block(kva, other, x), z_sem.at[0], to_pair)
    ring_send(A1, kva, other, x)
    send(stage.at[pl.ds(8, 2)], kvb.at[me], z_sem.at[1], to_pair)
    send(stage.at[pl.ds(10, 2)], q_pair, z_sem.at[2], to_pair)
    to_sibling("a", kva, other, x)
    ring_pass(A0, "a", kva, zl)
    ring_pass(A1, "a", kva, other)
    ring_send(B0, kvb, zl, x)
    to_sibling("b", kvb, zl, x)
    arrived(block(kvb, other, x), z_sem.at[1], to_pair)
    ring_send(B1, kvb, other, x)
    to_sibling("b", kvb, other, x)
    send(stage.at[pl.ds(4, 2)], kvh.at[me], z_sem.at[3], to_pair)
    ring_far(A0, "a", kva, zl)
    ring_far(A1, "a", kva, other)
    for c in local[:3]:
        c.wait()
    arrived(q_pair, z_sem.at[2], to_pair)
    from_sibling("a")

    scores = ((s00, s01), (s10, s11))
    accs = (acc0, acc1)
    factor = HEAD_DIM ** -0.5 * LOG2E
    lowest = jnp.full((8, TILE), MASKED, jnp.float32)
    nothing = jnp.zeros((8, TILE), jnp.float32)

    def place_of(row, n):
        return owners_ref[n, row], starts_ref[n, row]

    def score(kv, rows, side, g, peaks, queries, group):
        out = []
        for u, row in enumerate(rows):
            at = [place_of(row, g * group + t) for t in range(group)]
            keys = jnp.concatenate([kv[o, 0, r] for o, r in at], axis=0)
            s = jnp.dot(keys, queries[u], preferred_element_type=jnp.float32)
            top = peaks[u]
            for t in range(group):
                part = s[t * TILE : (t + 1) * TILE] + bars_ref[g * group + t, row]
                scores[side][u][g * group + t] = part
                top = jnp.maximum(top, jnp.max(part.reshape(TILE // 8, 8, TILE), axis=0))
            out.append(top)
        return tuple(out)

    def blend(kv, rows, side, g, totals, peaks, group):
        out = []
        for u, row in enumerate(rows):
            total = totals[u]
            weights = []
            for t in range(group):
                w = jnp.exp2((scores[side][u][g * group + t] - peaks[u]) * factor)
                total = total + jnp.sum(w.reshape(TILE // 8, 8, TILE), axis=0)
                weights.append(w.astype(jnp.bfloat16))
            at = [place_of(row, g * group + t) for t in range(group)]
            values = jnp.concatenate([kv[o, 1, r] for o, r in at], axis=1)
            accs[u][...] += jnp.dot(values, jnp.concatenate(weights, axis=0), preferred_element_type=jnp.float32)
            out.append(total)
        return tuple(out)

    def attention(kv, plan, tasks, group=GROUP):
        peaks = None
        for i in range(-1, len(plan)):
            here = plan[i] if i >= 0 else []
            there = plan[i + 1] if i + 1 < len(plan) else []
            side = i % 2
            rows, rows_next = [u[0] for u in here], [u[0] for u in there]
            queries = [q_of[j, r].T for _, (q_of, j, r), _ in there]
            tops = [jnp.max(p, axis=0, keepdims=True) for p in peaks] if here else []
            for u in range(len(here)):
                accs[u][...] = jnp.zeros((HEAD_DIM, TILE), jnp.float32)

            def body(g, carry):
                new_peaks = score(kv, rows_next, 1 - side, g, carry[0], queries, group)
                return new_peaks, blend(kv, rows, side, g, carry[1], tops, group)

            peaks, totals = lax.fori_loop(0, LIMIT // group, body, ((lowest,) * len(there), (nothing,) * len(here)))
            for u, (_, _, (dst, r)) in enumerate(here):
                o = accs[u][...] * (1.0 / jnp.sum(totals[u], axis=0, keepdims=True))
                dst[r, :] = o.T.astype(jnp.bfloat16)
            if i in tasks:
                tasks[i]()

    def tile_rows(i):
        return pl.ds(i * TILE, TILE)

    def plan_of(j):
        return [
            [
                (i, (q_own, j, i), (att.at[y, own_a + j], tile_rows(i))),
                (ROW_TILES + i, (q_pair, j, i), (back.at[j], tile_rows(i))),
            ]
            for i in range(ROW_TILES)
        ]

    positions = [own_a, own_a + 1, pair_a, pair_a + 1, 4]

    row_groups = {0: [(0, 640)], 1: [(0, 256), (256, 256), (512, 128)], 2: [(0, 640)], 3: [(0, 256), (256, 256), (512, 128)]}
    row_groups[4] = [(TILE * i, TILE) for i in range(ROW_TILES)]
    first_sem = {0: 0, 1: 1, 2: 4, 3: 5, 4: 8}

    def y_block(n, y_, start, count):
        return att.at[y_, positions[n], pl.ds(start, count)]

    def y_send(n, g=0):
        part = y_block(n, y, *row_groups[n][g])
        send(part, part, y_sem.at[0, first_sem[n] + g], to_y[0])
        send(part, part, y_sem.at[1, first_sem[n] + g], to_y[2])

    def y_pass(n, g=0):
        start, count = row_groups[n][g]
        arrived(y_block(n, y_left, start, count), y_sem.at[0, first_sem[n] + g], to_y[2])
        part = y_block(n, y_left, start, count // 2)
        send(part, part, y_far_sem.at[0, first_sem[n] + g], to_y[0])
        arrived(y_block(n, y_right, start, count), y_sem.at[1, first_sem[n] + g], to_y[0])
        part = y_block(n, y_right, start + count // 2, count // 2)
        send(part, part, y_far_sem.at[1, first_sem[n] + g], to_y[2])

    def y_far(n, g=0):
        start, count = row_groups[n][g]
        arrived(y_block(n, y_opposite, start, count // 2), y_far_sem.at[0, first_sem[n] + g], to_y[2])
        arrived(y_block(n, y_opposite, start + count // 2, count // 2), y_far_sem.at[1, first_sem[n] + g], to_y[0])

    def give_back(j, g=0):
        rows = pl.ds(*row_groups[2 + j][g])
        send(back.at[j, rows], att.at[y, own_a + j, rows], ret_sem.at[j + g], to_pair)

    def given_back(j, g=0):
        rows = pl.ds(*row_groups[2 + j][g])
        arrived(att.at[y, pair_a + j, rows], ret_sem.at[j + g], to_pair)
        y_send(2 + j, g)

    ours_columns = pl.ds(pl.multiple_of(zh * ROWS, TILE), ROWS)
    theirs_columns = pl.ds(pl.multiple_of((1 - zh) * ROWS, TILE), ROWS)

    def product(units, rows, columns):
        lhs = jnp.concatenate([att[n, positions[u], rows, :] for u in units for n in range(RING)], axis=1)
        rhs = jnp.concatenate([panel[n, head_columns(positions[u]), columns] for u in units for n in range(RING)], axis=0)
        return jnp.dot(lhs, rhs, preferred_element_type=jnp.float32)

    def contract(units, first, parts):
        def one(c, _):
            rows = pl.ds(pl.multiple_of(c * TILE, TILE), TILE)
            for total, columns in parts:
                p = product(units, rows, columns)
                total[rows, :] = p if first else total[rows, :] + p
            return 0

        lax.fori_loop(0, ROW_TILES, one, 0)

    def panel_here():
        for d in range(3):
            arrived(panel.at[lax.rem(y + 3 - d, RING), half], w_sem.at[d], to_y[2 - d])
        local[3].wait()
        for d in range(RING):
            y_ = lax.rem(y + d, RING)
            send(panel.at[y_, half], panel.at[y_, half], w_sib_sem.at[d], to_sib)

    def after_a1():
        ring_pass(B0, "b", kvb, zl)

    def after_a3():
        ring_pass(B1, "b", kvb, other)
        ring_send(H0, kvh, zl, x)
        to_sibling("h", kvh, zl, x)

    attention(kva, plan_of(0), {1: after_a1, 3: after_a3})
    give_back(0)
    y_send(0)
    arrived(block(kvh, other, x), z_sem.at[3], to_pair)
    ring_send(V1, kvh, other, x, v_part)
    to_sibling("h", kvh, other, x)
    ring_far(B0, "b", kvb, zl)
    ring_far(B1, "b", kvb, other)
    panel_here()
    from_sibling("b")

    v_first, v_second = pl.ds(0, 3), pl.ds(3, 2)

    def v_block(x_, rows=None):
        at = kvh.at[seq_of(other, x_, core), 1]
        return at if rows is None else at.at[rows]

    def after_b1():
        given_back(0)
        ring_pass(H0, "h", kvh, zl)
        for n, x_ in ((4, left), (5, right)):
            send(block(kvh, zl, x_, k_part), block(kvh, zl, x_, k_part), z_sem.at[n], to_pair)
        y_pass(0)

    def after_b3():
        arrived(block(kvh, other, left, v_part), x_sem.at[0, V1], to_left)
        send(v_block(left, v_first), v_block(left, v_first), far_sem.at[0, V1], to_right)
        arrived(block(kvh, other, right, v_part), x_sem.at[1, V1], to_right)
        send(v_block(right, v_second), v_block(right, v_second), far_sem.at[1, V1], to_left)
        to_sibling("h", kvh, other, left, v_part)
        to_sibling("h", kvh, other, right, v_part)
        y_pass(2)

    def hand_out_b(g):
        give_back(1, g)
        y_send(1, g)

    def after_b1_too():
        hand_out_b(0)
        after_b1()

    def after_b3_too():
        hand_out_b(1)
        after_b3()
        given_back(1, 0)
        y_pass(1, 0)

    attention(kvb, plan_of(1), {1: after_b1_too, 3: after_b3_too}, 2 * GROUP)
    hand_out_b(2)
    ring_far(H0, "h", kvh, zl)
    send(block(kvh, zl, opposite, k_part), block(kvh, zl, opposite, k_part), z_sem.at[6], to_pair)
    arrived(v_block(opposite, v_first), far_sem.at[0, V1], to_left)
    arrived(v_block(opposite, v_second), far_sem.at[1, V1], to_right)
    to_sibling("h", kvh, other, opposite, v_part)
    for n, x_ in ((4, left), (5, right)):
        arrived(block(kvh, other, x_, k_part), z_sem.at[n], to_pair)
        to_sibling("h", kvh, other, x_, k_part)
    given_back(1, 1)
    y_pass(1, 1)
    y_far(0)
    y_far(2)
    for d in range(RING):
        arrived(panel.at[lax.rem(y + d, RING), other_half], w_sib_sem.at[d], to_sib)
    contract((0, 2), True, ((theirs, theirs_columns), (mine, ours_columns)))
    given_back(1, 2)
    arrived(block(kvh, other, opposite, k_part), z_sem.at[6], to_pair)
    to_sibling("h", kvh, other, opposite, k_part)
    y_pass(1, 2)
    y_pass(3, 0)
    from_sibling("h")
    y_pass(3, 1)

    units = [
        (i, (q_own, 2, i), (att.at[y, 4], tile_rows(i))) for i in range(ROW_TILES)
    ]

    def sum_out(c):
        y_far(4, c)
        rows = tile_rows(c)
        sent[rows, :] = (theirs[rows, :] + product((1, 3, 4), rows, theirs_columns)).astype(sent.dtype)
        send(sent.at[rows], got.at[rows], sum_sem.at[c], to_sum)

    def after_h(i):
        y_send(4, i)
        if i == 0:
            y_pass(3, 2)
        else:
            y_pass(4, i - 1)
        if i == 2:
            for n in (1, 3):
                for g in range(3):
                    y_far(n, g)
        if i >= 2:
            sum_out(i - 2)

    attention(kvh, [[u] for u in units], {i: functools.partial(after_h, i) for i in range(ROW_TILES)}, 2 * GROUP)
    y_pass(4, 4)
    sum_out(3)
    sum_out(4)
    local[4].wait()
    contract((1, 3, 4), False, ((mine, ours_columns),))
    for c in range(ROW_TILES):
        rows = tile_rows(c)
        arrived(got.at[rows], sum_sem.at[c], to_sum)
        projected = mine[rows, :] + got[rows, :].astype(jnp.float32)
        out = res_ref[rows, :].astype(jnp.float32) + gate_ref[...][None, :] * (projected + bias_ref[...][None, :])
        out_ref[rows, :] = out.astype(out_ref.dtype)
    for c in sends:
        c.wait_send()


def whole(owners, starts, bars, q, k, v, w, bias, gate, residual):
    bf16, f32 = jnp.bfloat16, jnp.float32

    def by_tile(array):
        return array.reshape(ROW_TILES, TILE, ROWS)

    smem, vmem, anywhere = (
        pl.BlockSpec(memory_space=pltpu.SMEM),
        pl.BlockSpec(memory_space=pltpu.VMEM),
        pl.BlockSpec(memory_space=pl.ANY),
    )
    dma = pltpu.SemaphoreType.DMA
    return pl.pallas_call(
        whole_kernel,
        out_shape=jax.ShapeDtypeStruct((ROWS, ROWS), bf16),
        in_specs=[smem, smem, smem, anywhere, anywhere, anywhere, anywhere, vmem, vmem, anywhere],
        out_specs=vmem,
        scratch_shapes=[
            pltpu.VMEM((12, ROW_TILES, TILE, HEAD_DIM), bf16),
            pltpu.VMEM((5, ROW_TILES, TILE, HEAD_DIM), bf16),
            pltpu.VMEM((SEQ, 2, ROW_TILES, TILE, HEAD_DIM), bf16),
            pltpu.VMEM((SEQ, 2, ROW_TILES, TILE, HEAD_DIM), bf16),
            pltpu.VMEM((SEQ, 2, ROW_TILES, TILE, HEAD_DIM), bf16),
            pltpu.VMEM((3, ROW_TILES, TILE, HEAD_DIM), bf16),
            pltpu.VMEM((2, ROW_TILES, TILE, HEAD_DIM), bf16),
            pltpu.VMEM((RING, 5, ROWS, HEAD_DIM), bf16),
            pltpu.VMEM((2, ROWS, HEAD_DIM), bf16),
            pltpu.VMEM((RING, ROWS, 2 * ROWS), bf16),
            pltpu.VMEM((ROWS, ROWS), f32),
            pltpu.VMEM((ROWS, ROWS), f32),
            pltpu.VMEM((ROWS, ROWS), bf16),
            pltpu.VMEM((ROWS, ROWS), bf16),
            pltpu.VMEM((ROWS, ROWS), bf16),
        ]
        + [pltpu.VMEM((LIMIT, TILE, TILE), f32)] * 4
        + [pltpu.VMEM((HEAD_DIM, TILE), f32)] * 2
        + [
            dma((12,)), dma((8,)), dma((160,)), dma((7,)), dma((2, 6)), dma((2, 6)), dma((28,)), dma((3,)), dma((4,)),
            dma((4,)), dma((2, 13)), dma((2, 13)), dma((5,)),
        ],
        compiler_params=pltpu.CompilerParams(collective_id=2, has_side_effects=True, vmem_limit_bytes=62 << 20),
        name="whole",
    )(owners, starts, bars, by_tile(q), by_tile(k), by_tile(v), w, bias, gate, residual)


def list_kernel(mask_ref, owners_ref, starts_ref, bars_ref, longest_ref):
    zl, x, core, _, _ = place()
    rows = []
    for plane in (zl, 1 - zl):
        first = ((plane * RING + x) * 2 + core) * ROW_TILES
        rows += [mask_ref[pl.ds(first + i, 1), :] for i in range(ROW_TILES)]
    allowed = jnp.where(jnp.concatenate(rows, axis=0) > 0, 1.0, 0.0)
    square = (TILE_COUNT, TILE_COUNT)
    earlier = lax.broadcasted_iota(jnp.int32, square, 0) < lax.broadcasted_iota(jnp.int32, square, 1)
    before = jnp.dot(allowed, jnp.where(earlier, 1.0, 0.0), preferred_element_type=jnp.float32).astype(jnp.int32)
    entry = lax.broadcasted_iota(jnp.int32, (LIMIT, TILE_COUNT), 0)
    tile = lax.broadcasted_iota(jnp.int32, (LIMIT, TILE_COUNT), 1)
    lane = lax.broadcasted_iota(jnp.int32, (LIMIT, 128), 1)
    entry_column = lax.broadcasted_iota(jnp.int32, (LIMIT, 128), 0)
    owner = jnp.zeros((LIMIT, TILE_COUNT), jnp.int32)
    for n in range(1, SEQ):
        owner = owner + jnp.where(tile >= n * ROW_TILES, 1, 0)
    start = tile - owner * ROW_TILES
    owners = jnp.zeros((LIMIT, 128), jnp.int32)
    starts = jnp.zeros((LIMIT, 128), jnp.int32)
    bars = jnp.full((LIMIT, 128), MASKED, jnp.float32)
    for i in range(2 * ROW_TILES):
        hit = (before[i : i + 1] == entry) & (allowed[i : i + 1] > 0.5)
        count = jnp.sum(allowed[i : i + 1], axis=1, keepdims=True).astype(jnp.int32)
        owners = jnp.where(lane == i, jnp.sum(jnp.where(hit, owner, 0), axis=1, keepdims=True), owners)
        starts = jnp.where(lane == i, jnp.sum(jnp.where(hit, start, 0), axis=1, keepdims=True), starts)
        bars = jnp.where((lane == i) & (entry_column < count), 0.0, bars)
    owners_ref[...] = owners
    starts_ref[...] = starts
    bars_ref[...] = bars
    longest_ref[0] = jnp.max(jnp.sum(jnp.where(mask_ref[...] > 0, 1, 0), axis=1, keepdims=True))


def tile_lists(tile_mask):
    vmem, smem = pl.BlockSpec(memory_space=pltpu.VMEM), pl.BlockSpec(memory_space=pltpu.SMEM)
    return pl.pallas_call(
        list_kernel,
        out_shape=[
            jax.ShapeDtypeStruct((LIMIT, 128), jnp.int32),
            jax.ShapeDtypeStruct((LIMIT, 128), jnp.int32),
            jax.ShapeDtypeStruct((LIMIT, 128), jnp.float32),
            jax.ShapeDtypeStruct((1,), jnp.int32),
        ],
        in_specs=[vmem],
        out_specs=[vmem, vmem, vmem, smem],
        name="tile_lists",
    )(tile_mask)


def local(queries, key_states, value_states, tile_mask, out_weight, out_bias, residual, gate_scale):
    bias, gate = out_bias, gate_scale
    owners, starts, bars, longest = tile_lists(tile_mask)

    def by_lists(_):
        return whole(owners, starts, bars, queries, key_states, value_states, out_weight, bias, gate, residual)

    def in_parts(_):
        kv, q, panel = gather(queries, key_states, value_states, out_weight)
        o = attend(tile_mask, q, kv)
        return project(o, panel.reshape(RING * ROWS, 2 * ROWS), bias[None, :], gate[None, :], residual)

    return lax.cond(longest[0] <= LIMIT, by_lists, in_parts, 0)


def solution(mesh):
    return jax.shard_map(
        local,
        mesh=mesh,
        in_specs=(
            P("seq", "head"),
            P("seq", "head"),
            P("seq", "head"),
            P(),
            P("head", None),
            P("head"),
            P("seq", "head"),
            P("head"),
        ),
        out_specs=P("seq", "head"),
        check_vma=False,
    )
```
